32 devices in a mesh: pr: 8 (over z, y), tp: 4 (over x, core).
Axes of the slice: x: 2, y: 2, z: 4, core: 2. Of those that a mesh axis runs over, the one named last changes fastest.
Arguments:
- tokens: bfloat16 [2048, 896], P('pr'), may hold values from -18 to 18
- prompt_lengths: int32 [8, 2], P('pr'), may hold values from 1 to 160, 256 in all within a row
- query_weight: bfloat16 [896, 1024], P(None, 'tp'), may hold values from -0.1875 to 0.1875
- key_weight: bfloat16 [896, 256], P(None, 'tp'), may hold values from -0.1875 to 0.1875
- value_weight: bfloat16 [896, 256], P(None, 'tp'), may hold values from -1.5 to 1.5
- attention_gain: float32 [1024], P('tp'), may hold values from 0.1 to 1.9
- inner_weight: bfloat16 [896, 2, 2048], P(None, None, 'tp'), may hold values from -0.1875 to 0.1875
- conv_weight: float32 [4, 2048], P(None, 'tp'), may hold values from -3 to 3
- scan_weight: bfloat16 [2048, 96], P('tp'), may hold values from -0.125 to 0.125
- step_weight: bfloat16 [64, 2048], P(None, 'tp'), may hold values from -0.75 to 0.75
- step_bias: float32 [2048], P('tp'), may hold values from -4 to -1
- mamba_rate: float32 [16, 2048], P(None, 'tp'), may hold values from 0.05 to 1
- mamba_skip: float32 [2048], P('tp'), may hold values from 0.3 to 2.7
- mamba_gain: float32 [2048], P('tp'), may hold values from 0.1 to 1.9
- request_prompt: int32 [448], P('pr'), may hold values from 0 to 1, as said below
- request_owner: int32 [448], P('pr'), may hold values from 0 to 7, as said below
- request_slot: int32 [448], P('pr'), may hold values from 0 to 55, as said below
Outputs:
- attention_out: bfloat16 [2048, 1024], P('pr', 'tp')
- mamba_out: bfloat16 [2048, 2048], P('pr', 'tp')
- cache_keyval: bfloat16 [448, 2, 32, 256], P('pr', None, None, 'tp')
- cache_state: bfloat16 [448, 16, 2048], P('pr', None, 'tp')
- cache_conv: bfloat16 [448, 3, 2048], P('pr', None, 'tp')
The draws below stay inside these ranges and needn't reach their ends.
Inputs may be any that keep to these rules, and one draw needn't show every extreme that they name: `request_prompt`: in each group one prompt has 29 requests and the other 27. `request_owner`: every owner receives exactly 56 requests; the requests of one group that name an owner name it exactly 7 times. `request_slot`: the requests of one owner have distinct slots.
All inputs are finite; a program needn't handle non-finite values.
Results may differ from the reference program's by a relative error of at most 0.012.
The reference program's roundings to bfloat16 on the way count: a program that leaves them out, or rounds other values in their place, can miss the bound.
Values may be sent and summed in bfloat16 or wider, within the bound.
No kernel may reach another device: no remote copies, remote signals or barrier semaphores. Data moves between devices by JAX's collectives and lax.ppermute only.
A program may use at most 64 MiB of HBM per device.

```python
import math
import jax
import jax.numpy as jnp
import numpy as np
from jax import lax

D = 896
HEADS = 16
KV_HEADS = 4
HEAD_DIM = 64
INNER = 2048
STATE = 16
DT_RANK = 64
CONV = 4
WINDOW = 32
TOK_DEV = 256
PROMPTS_DEV = 2
REQ_DEV = 56
LONGEST = 160
CAP = 7
GROUPS = 8
TOKENS = 2048
PROMPTS = 16
REQUESTS = 448


def draw_tokens(key, part):
    first_key, second_key = jax.random.split(key)
    base_draw = jnp.clip(jax.random.normal(first_key, (TOKENS, D), jnp.float32), -6.0, 6.0)
    row_scale = jnp.exp(jax.random.uniform(second_key, (TOKENS, 1), jnp.float32, -0.7, 0.7))
    return (base_draw * row_scale).astype(jnp.bfloat16)


def draw_value_weight(key, part):
    base_draw = jnp.clip(jax.random.normal(key, (D, KV_HEADS * HEAD_DIM), jnp.float32), -6.0, 6.0)
    head_index = (jnp.arange(KV_HEADS * HEAD_DIM) // HEAD_DIM).astype(jnp.float32)
    head_scale = 0.6 * 3.0 ** (head_index / max(KV_HEADS - 1, 1))
    return (base_draw * head_scale[None, :] / math.sqrt(D)).astype(jnp.bfloat16)


def draw_mamba_skip(key, part):
    base_draw = jax.random.uniform(key, (INNER,), jnp.float32, 0.5, 1.5)
    channel = jnp.arange(INNER).astype(jnp.float32)
    return base_draw * 0.6 * 3.0 ** (channel / (INNER - 1))


def draw_request_prompt(key, part):
    groups = REQUESTS // REQ_DEV
    half_count = REQ_DEV // 2
    group_keys = jax.random.split(jax.random.fold_in(key, 21), groups)

    def one_source(sub_key):
        second_key, third_key = jax.random.split(sub_key, 2)
        counts = jnp.stack([half_count + 1, half_count - 1])
        counts = counts[jax.random.permutation(second_key, 2)]
        bounds = jnp.cumsum(counts)
        position = jnp.arange(REQ_DEV, dtype=jnp.int32)
        labels = jnp.sum((position[:, None] >= bounds[None, :]).astype(jnp.int32), axis=1)
        return labels[jax.random.permutation(third_key, REQ_DEV)]
    return jax.vmap(one_source)(group_keys).reshape(-1).astype(jnp.int32)


def request_layout(key):
    groups = REQUESTS // REQ_DEV
    peer_total = REQ_DEV // CAP
    offsets = jax.random.permutation(jax.random.fold_in(key, 11), groups)[:peer_total]

    def permute_one(sub_key):
        return jax.random.permutation(sub_key, REQ_DEV)
    request_order = jax.vmap(permute_one)(jax.random.split(jax.random.fold_in(key, 12), groups))
    source = jnp.arange(groups, dtype=jnp.int32)[:, None]
    peer_slot = request_order // CAP
    within = request_order % CAP
    owner_of = (source + offsets[peer_slot]) % groups
    shuffle = jax.vmap(permute_one)(jax.random.split(jax.random.fold_in(key, 13), groups))
    slot_of = shuffle[owner_of, peer_slot * CAP + within]
    return (owner_of.reshape(-1).astype(jnp.int32), slot_of.reshape(-1).astype(jnp.int32))


def draw_request_owner(key, part):
    return request_layout(key)[0]


def draw_request_slot(key, part):
    return request_layout(key)[1]


def block_levels(own_key, shape, cuts, low, top_value):
    gain = 1.0
    for dim, shards_of in cuts:
        heights = jax.random.uniform(jax.random.fold_in(jax.random.fold_in(own_key, 6), dim), (shards_of,), jnp.float32, low / len(cuts), top_value / len(cuts))
        gain = gain * jnp.repeat(jnp.exp(heights), shape[dim] // shards_of).reshape((-1,) + (1,) * (len(shape) - 1 - dim))
    return gain


def profile(amount, total, reach, lean):
    loads = [(1 << 20) // math.isqrt(standing ** lean) + 1 for standing in range(2, amount + 1)]
    rest, given = total - reach - (amount - 1), [1] * (amount - 1)
    while rest > 0:
        candidates = [i for i in range(amount - 1) if given[i] < reach]
        whole, budget = sum([loads[i] for i in candidates]), rest
        for i in candidates:
            extra = min(reach - given[i], max(1, budget * loads[i] // whole), rest)
            given[i] = given[i] + extra
            rest = rest - extra
    return np.array([reach] + given)


def uneven(rng, count, total, most, skew):
    if count == 2:
        one = jax.random.randint(rng, (), max(1, total - most), min(most, total - 1) + 1)
        return jnp.stack([one, total - one])
    tallies = jnp.asarray(profile(count, total, most, skew), jnp.int32)
    pairs = (count - 1) // 2
    source_of, taker = tallies[1:1 + 2 * pairs:2], tallies[2:2 + 2 * pairs:2]
    slack = jnp.minimum(source_of - 1, most - taker)
    moved = jax.random.randint(jax.random.fold_in(rng, 1), (pairs,), 0, 1 << 20) % (slack + 1)
    tallies = tallies.at[1:1 + 2 * pairs:2].set(source_of - moved).at[2:2 + 2 * pairs:2].set(taker + moved)
    return tallies[jax.random.permutation(jax.random.fold_in(rng, 2), count)]


def scatter_about(rng, extent, width, limit, pieces=(), held_as=jnp.bfloat16):
    factor_of = block_levels(rng, extent, pieces, -0.22, 0.18) if pieces else 1.0
    drawn = jax.random.normal(rng, extent, jnp.float32) * width * factor_of
    return jnp.minimum(jnp.maximum(drawn, -limit), limit).astype(held_as)


def setup_inputs(seed: int = 0) -> dict:
    seeds = jax.random.split(jax.random.key(seed), 18)
    return {
        "tokens": draw_tokens(jax.random.fold_in(seeds[17], 71), 0),
        "prompt_lengths": jax.vmap(lambda own: uneven(own, PROMPTS_DEV, TOK_DEV, LONGEST, 2))(jax.random.split(seeds[1], GROUPS)).reshape((GROUPS, PROMPTS_DEV)).astype(jnp.int32),
        "query_weight": scatter_about(seeds[2], (D, HEADS * HEAD_DIM), D ** -0.5, 0.1875, ((1, 4),)),
        "key_weight": scatter_about(seeds[3], (D, KV_HEADS * HEAD_DIM), D ** -0.5, 0.1875, ((1, 4),)),
        "value_weight": draw_value_weight(jax.random.fold_in(seeds[17], 71), 0),
        "attention_gain": jnp.clip(1.0 + 0.18 * jax.random.normal(seeds[5], (HEADS * HEAD_DIM,), jnp.float32), 0.1, 1.9),
        "inner_weight": scatter_about(seeds[6], (D, 2, INNER), D ** -0.5, 0.1875, ((2, 4),)),
        "conv_weight": scatter_about(seeds[7], (CONV, INNER), 0.5, 3.0, ((1, 4),), jnp.float32),
        "scan_weight": scatter_about(seeds[8], (INNER, DT_RANK + 2 * STATE), INNER ** -0.5, 0.125, ((0, 4),)),
        "step_weight": scatter_about(seeds[9], (DT_RANK, INNER), DT_RANK ** -0.5, 0.75, ((1, 4),)),
        "step_bias": jnp.clip(-4.0 + 3.0 * jax.random.uniform(seeds[10], (INNER,), jnp.float32) ** block_levels(seeds[10], (INNER,), ((0, 4),), -0.2, 0.2), -4.0, -1.0),
        "mamba_rate": jnp.clip(jnp.exp(math.log(1.0) - 2.9957323 * jax.random.uniform(seeds[11], (STATE, INNER), jnp.float32) ** block_levels(seeds[11], (STATE, INNER), ((1, 4),), -0.2, 0.2)), 0.05, 1.0),
        "mamba_skip": draw_mamba_skip(jax.random.fold_in(seeds[17], 71), 0),
        "mamba_gain": jnp.clip(1.0 + 0.18 * jax.random.normal(seeds[13], (INNER,), jnp.float32), 0.1, 1.9),
        "request_prompt": draw_request_prompt(jax.random.fold_in(seeds[17], 71), 0),
        "request_owner": draw_request_owner(jax.random.fold_in(seeds[17], 71), 0),
        "request_slot": draw_request_slot(jax.random.fold_in(seeds[17], 71), 0),
    }


EPSILON = 1e-06

def prompt_layout(lengths, total_rows):
    prompt_ends = jnp.cumsum(lengths).astype(jnp.int32)
    starts = (prompt_ends - lengths).astype(jnp.int32)
    position = jnp.arange(total_rows, dtype=jnp.int32)
    member = (position[:, None] >= starts[None, :]) & (position[:, None] < prompt_ends[None, :])
    segment = lax.optimization_barrier(jnp.sum((position[:, None] >= prompt_ends[None, :]).astype(jnp.int32), axis=1))
    first_pos = lax.optimization_barrier(jnp.sum(jnp.where(member, starts[None, :], 0), axis=1)).astype(jnp.int32)
    return (starts, prompt_ends, segment, position - first_pos)

def tail_rows(values, starts, prompt_ends, tail_depth):
    offsets = jnp.arange(tail_depth, dtype=jnp.int32)
    wanted = prompt_ends[:, None] - tail_depth + offsets[None, :]
    inside_prompt = wanted >= starts[:, None]
    picked = jnp.take(values, jnp.clip(wanted, 0, values.shape[0] - 1).astype(jnp.int32), axis=0)
    return jnp.where(inside_prompt[:, :, None], picked, jnp.zeros((), values.dtype))

def one_group(tokens, lengths, params):
    query_weight, key_weight, value_weight, attention_gain, inner_weight, conv_weight, scan_weight, step_weight, step_bias, mamba_rate, mamba_skip, mamba_gain = params
    total_rows = tokens.shape[0]
    starts, prompt_ends, segment, offset = prompt_layout(lengths, total_rows)
    queries = jnp.dot(tokens, query_weight, preferred_element_type=jnp.float32).astype(jnp.bfloat16)
    keys_bf = jnp.dot(tokens, key_weight, preferred_element_type=jnp.float32).astype(jnp.bfloat16)
    values_bf = jnp.dot(tokens, value_weight, preferred_element_type=jnp.float32).astype(jnp.bfloat16)
    group_size = HEADS // KV_HEADS
    query_heads = queries.reshape(total_rows, HEADS, HEAD_DIM).astype(jnp.float32)
    key_heads = jnp.repeat(keys_bf.reshape(total_rows, KV_HEADS, HEAD_DIM).astype(jnp.float32), group_size, axis=1)
    value_heads = jnp.repeat(values_bf.reshape(total_rows, KV_HEADS, HEAD_DIM).astype(jnp.float32), group_size, axis=1)
    scores = jnp.einsum('thd,uhd->htu', query_heads, key_heads) * HEAD_DIM ** (-0.5)
    position = jnp.arange(total_rows, dtype=jnp.int32)
    distance = position[:, None] - position[None, :]
    allowed = (segment[:, None] == segment[None, :]) & (distance >= 0) & (distance < WINDOW)
    masked = jnp.where(allowed[None], scores, -1e+30)
    row_max = lax.optimization_barrier(jnp.max(masked, axis=2, keepdims=True))
    expons = jnp.where(allowed[None], jnp.exp(masked - row_max), 0.0)
    weights = (expons / lax.optimization_barrier(jnp.sum(expons, axis=2, keepdims=True))).astype(jnp.bfloat16)
    attended = jnp.einsum('htu,uhd->thd', weights.astype(jnp.float32), value_heads).reshape(total_rows, HEADS * HEAD_DIM)
    norm_attn = jnp.sqrt(lax.optimization_barrier(jnp.mean(attended * attended, axis=1, keepdims=True)) + EPSILON)
    attention_out = (attended / norm_attn * attention_gain).astype(jnp.bfloat16)
    inner_proj = jnp.dot(tokens, inner_weight.reshape(D, 2 * INNER), preferred_element_type=jnp.float32)
    inner_proj = inner_proj.astype(jnp.bfloat16).reshape(total_rows, 2, INNER)
    raw_inner = inner_proj[:, 0]
    gate_inner = inner_proj[:, 1]
    conv_sum = jnp.zeros((total_rows, INNER), jnp.float32)
    for tap_index in range(CONV):
        lag_rows = CONV - 1 - tap_index
        shifted = jnp.pad(raw_inner, ((lag_rows, 0), (0, 0)))[:total_rows].astype(jnp.float32)
        shifted = jnp.where((offset >= lag_rows)[:, None], shifted, 0.0)
        conv_sum = conv_sum + shifted * conv_weight[tap_index]
    mixed_inner = jax.nn.silu(conv_sum).astype(jnp.bfloat16)
    projected = jnp.dot(mixed_inner, scan_weight, preferred_element_type=jnp.float32)
    low_rank = projected[:, :DT_RANK].astype(jnp.bfloat16)
    input_map = projected[:, DT_RANK:DT_RANK + STATE]
    output_map = projected[:, DT_RANK + STATE:]
    step_size = jax.nn.softplus(jnp.dot(low_rank, step_weight, preferred_element_type=jnp.float32) + step_bias)
    mixed_float = mixed_inner.astype(jnp.float32)
    keep_state = jnp.where(offset == 0, 0.0, 1.0).astype(step_size.dtype)

    def advance(carried, block_item):
        step_row, input_row, mixed_row, keep_row = block_item
        decay_rate = jnp.exp(-step_row[None, :] * mamba_rate)
        carried = carried * decay_rate * keep_row + input_row[:, None] * (step_row * mixed_row)[None, :]
        return (carried, carried)
    start_state = jnp.zeros((STATE, INNER), jnp.float32)
    _, states = lax.scan(advance, start_state, (step_size, input_map, mixed_float, keep_state))
    scanned = jnp.einsum('tn,tnc->tc', output_map, states)
    gated_out = (scanned + mamba_skip * mixed_float) * jax.nn.silu(gate_inner.astype(jnp.float32))
    norm_mamba = jnp.sqrt(lax.optimization_barrier(jnp.mean(gated_out * gated_out, axis=1, keepdims=True)) + EPSILON)
    mamba_out = (gated_out / norm_mamba * mamba_gain).astype(jnp.bfloat16)
    keyval = jnp.stack([tail_rows(keys_bf, starts, prompt_ends, WINDOW), tail_rows(values_bf, starts, prompt_ends, WINDOW)], axis=1)
    final_state = states[prompt_ends - 1].astype(jnp.bfloat16)
    conv_tail = tail_rows(raw_inner, starts, prompt_ends, CONV - 1)
    return (attention_out, mamba_out, keyval, final_state, conv_tail)

def reference(tokens, prompt_lengths, query_weight, key_weight, value_weight, attention_gain, inner_weight, conv_weight, scan_weight, step_weight, step_bias, mamba_rate, mamba_skip, mamba_gain, request_prompt, request_owner, request_slot):
    params = (query_weight, key_weight, value_weight, attention_gain, inner_weight, conv_weight, scan_weight, step_weight, step_bias, mamba_rate, mamba_skip, mamba_gain)

    def run_group(block_item):
        return one_group(block_item[0], block_item[1], params)
    attention_out, mamba_out, keyval, final_state, conv_tail = lax.map(run_group, (tokens.reshape(GROUPS, TOK_DEV, D), prompt_lengths))
    source = jnp.arange(REQUESTS, dtype=jnp.int32) // REQ_DEV
    prompt_index = (source * PROMPTS_DEV + request_prompt).astype(jnp.int32)
    target_row = (request_owner * REQ_DEV + request_slot).astype(jnp.int32)

    def deliver(cache_table):
        flat_table = cache_table.reshape((PROMPTS,) + cache_table.shape[2:])
        empty_rows = jnp.zeros((REQUESTS,) + flat_table.shape[1:], flat_table.dtype)
        return empty_rows.at[target_row].set(flat_table[prompt_index])
    return (attention_out.reshape(TOKENS, HEADS * HEAD_DIM), mamba_out.reshape(TOKENS, INNER), deliver(keyval), deliver(final_state), deliver(conv_tail))
```

```python
import functools
import math

import jax
import jax.numpy as jnp
from jax import lax
from jax.experimental import pallas as pl
from jax.experimental.pallas import tpu as pltpu
from jax.sharding import PartitionSpec as P

HEADS = 16
KV_HEADS = 4
HEAD_DIM = 64
INNER = 2048
STATE = 16
DT_RANK = 64
CONV = 4
WINDOW = 32
EPSILON = 1e-06
LANES = 128
BLOCK = 16
RESET = 1e30

F32 = jnp.float32
BF16 = jnp.bfloat16
VMEM = pl.BlockSpec(memory_space=pltpu.VMEM)
SMEM = pl.BlockSpec(memory_space=pltpu.SMEM)
ANY = pl.BlockSpec(memory_space=pl.ANY)


def params(mib):
    return pltpu.CompilerParams(vmem_limit_bytes=mib << 20)


def dot_nt(a, b):
    return lax.dot_general(a, b, (((1,), (1,)), ((), ())), preferred_element_type=F32)


def bounds(len_ref, prompts):
    starts, ends = [], []
    at = 0
    for p in range(prompts):
        starts.append(at)
        at = at + len_ref[0, p]
        ends.append(at)
    return starts, ends


def first_row_of(position, starts, prompts):
    first = jnp.zeros_like(position)
    for p in range(1, prompts):
        first = jnp.where(position >= starts[p], starts[p], first)
    return first


def interleave(tokens, which):
    out = []
    for at in range(0, tokens.shape[1], LANES):
        wide = min(LANES, tokens.shape[1] - at)
        row = lax.broadcasted_iota(jnp.int32, (wide, 2 * wide), 0)
        column = lax.broadcasted_iota(jnp.int32, (wide, 2 * wide), 1)
        pick = jnp.where(column == 2 * row + which, 1.0, 0.0).astype(BF16)
        out.append(
            jnp.dot(tokens[:, at : at + wide], pick, preferred_element_type=F32).astype(BF16)
        )
    return jnp.concatenate(out, axis=1)


def last_rows(shape, depth, starts, ends):
    row = lax.broadcasted_iota(jnp.int32, shape, 0)
    position = lax.broadcasted_iota(jnp.int32, shape, 1)
    hit = jnp.zeros(shape, F32)
    for p in range(len(starts)):
        here = (row >= p * depth) & (row < (p + 1) * depth) & (position >= starts[p])
        hit = jnp.where(here & (position - row == ends[p] - (p + 1) * depth), 1.0, hit)
    return hit.astype(BF16)


def sigmoid(x):
    return 0.5 * jnp.tanh(0.5 * x) + 0.5


def mix_kernel(
    prompts,
    len_ref,
    tokens_hbm,
    inner_hbm,
    conv_ref,
    scan_ref,
    partial_ref,
    mixed_ref,
    tail_ref,
    tokens_ref,
    inner_ref,
    raw_ref,
    sems,
):
    tokens_copy = pltpu.make_async_copy(tokens_hbm, tokens_ref, sems.at[0])
    inner_copy = pltpu.make_async_copy(inner_hbm, inner_ref, sems.at[1])
    tokens_copy.start()
    inner_copy.start()
    rows, width = tokens_ref.shape
    channels = inner_ref.shape[2]
    starts, ends = bounds(len_ref, prompts)
    tokens_copy.wait()
    spread = interleave(tokens_ref[...], 0)
    inner_copy.wait()
    weight = inner_ref[...].reshape(2 * width, channels)
    raw = jnp.dot(spread, weight, preferred_element_type=F32).astype(BF16).astype(F32)
    raw_ref[pl.ds(0, 8), :] = jnp.zeros((8, channels), F32)
    raw_ref[pl.ds(8, rows), :] = raw
    position = lax.broadcasted_iota(jnp.int32, (rows, 1), 0)
    offset = position - first_row_of(position, starts, prompts)
    total = raw * conv_ref[CONV - 1 : CONV, :]
    for lag in range(1, CONV):
        shifted = raw_ref[pl.ds(8 - lag, rows), :]
        shifted = jnp.where(offset >= lag, shifted, 0.0)
        total = total + shifted * conv_ref[CONV - 1 - lag : CONV - lag, :]
    mixed = (total * sigmoid(total)).astype(BF16)
    mixed_ref[...] = mixed
    partial_ref[...] = dot_nt(scan_ref[...], mixed)
    pick = last_rows((8, rows), CONV - 1, starts, ends)
    tail_ref[...] = jnp.dot(pick, raw.astype(BF16), preferred_element_type=F32)


def attend_kernel(
    prompts,
    len_ref,
    tokens_ref,
    query_ref,
    key_ref,
    value_ref,
    inner_hbm,
    tail_ref,
    prompt_ref,
    owner_ref,
    slot_ref,
    attended_ref,
    square_ref,
    gate_ref,
    packed_ref,
    inner_ref,
    request_ref,
    sem,
):
    inner_copy = pltpu.make_async_copy(inner_hbm, inner_ref, sem)
    inner_copy.start()
    rows, width = tokens_ref.shape
    channels = inner_ref.shape[2]
    features = query_ref.shape[1]
    group = features // HEAD_DIM
    starts, ends = bounds(len_ref, prompts)
    tokens = tokens_ref[...]
    queries = jnp.dot(tokens, query_ref[...], preferred_element_type=F32).astype(BF16)
    keys = dot_nt(tokens, jnp.concatenate([key_ref[...]] * group, axis=0)).astype(BF16)
    values = dot_nt(tokens, jnp.concatenate([value_ref[...]] * group, axis=0)).astype(BF16)
    at_row = lax.broadcasted_iota(jnp.int32, (rows, rows), 0)
    at_column = lax.broadcasted_iota(jnp.int32, (rows, rows), 1)
    row_first = first_row_of(at_row, starts, prompts)
    allowed = (at_column <= at_row) & (at_row - at_column < WINDOW) & (at_column >= row_first)
    head_of = lax.broadcasted_iota(jnp.int32, (rows, features), 1) // HEAD_DIM
    zero = jnp.zeros((), BF16)
    attended = jnp.zeros((rows, features), F32)
    for head in range(group):
        mine = head_of == head
        scores = dot_nt(queries, jnp.where(mine, keys, zero)) * HEAD_DIM ** (-0.5)
        scores = jnp.where(allowed, scores, -1e30)
        top = jnp.max(scores, axis=1, keepdims=True)
        expons = jnp.exp(scores - top)
        weights = expons * (1.0 / jnp.sum(expons, axis=1, keepdims=True))
        attended = attended + jnp.dot(
            weights.astype(BF16), jnp.where(mine, values, zero), preferred_element_type=F32
        )
    attended_ref[...] = attended
    ones = jnp.ones((8, features), BF16)
    square_ref[...] = dot_nt(ones, (attended * attended).astype(BF16))
    lane = lax.broadcasted_iota(jnp.int32, (rows, LANES), 1)
    both = jnp.where(lane < HEAD_DIM, keys[:, :LANES], values[:, :LANES])
    pick = last_rows((prompts * WINDOW, rows), WINDOW, starts, ends)
    packed_ref[: prompts * WINDOW, :] = jnp.dot(pick, both, preferred_element_type=F32).astype(
        BF16
    )
    request_ref[...] = jnp.zeros(request_ref.shape, F32)
    requests = owner_ref.shape[1]
    request_ref[0:1, 0:requests] = owner_ref[...].astype(F32)
    request_ref[1:2, 0:requests] = slot_ref[...].astype(F32)
    request_ref[2:3, 0:requests] = prompt_ref[...].astype(F32)
    base = prompts * WINDOW
    for tile in range(channels // LANES):
        tail = tail_ref[:, tile * LANES : (tile + 1) * LANES]
        extra = request_ref[...] if tile == 0 else jnp.zeros((8, LANES), F32)
        packed_ref[base + 16 * tile : base + 16 * (tile + 1), :] = jnp.concatenate(
            [tail, extra], axis=0
        ).astype(BF16)
    inner_copy.wait()
    spread = interleave(tokens, 1)
    gate_ref[...] = jnp.dot(
        spread, inner_ref[...].reshape(2 * width, channels), preferred_element_type=F32
    ).astype(BF16)


def scan_kernel(
    prompts,
    len_ref,
    own_ref,
    other_ref,
    mixed_ref,
    gate_ref,
    step_weight_ref,
    step_bias_ref,
    rate_ref,
    skip_ref,
    early_ref,
    square_ref,
    gated_ref,
    sums_ref,
    payload_ref,
    decay_ref,
    input_ref,
    partial_ref,
    in_map_ref,
    out_map_ref,
    begin_ref,
    final_ref,
):
    rows, channels = mixed_ref.shape
    blocks = rows // BLOCK
    starts, ends = bounds(len_ref, prompts)
    projected = own_ref[...] + other_ref[...]
    low = projected[:DT_RANK, :].T.astype(BF16)
    pre = jnp.dot(low, step_weight_ref[...], preferred_element_type=F32) + step_bias_ref[...]
    step = jnp.maximum(pre, 0.0) + jnp.log1p(jnp.exp(-jnp.abs(pre)))
    position = lax.broadcasted_iota(jnp.int32, (rows, 1), 0)
    is_first = position == 0
    for p in range(1, prompts):
        is_first = is_first | (position == starts[p])
    decay_ref[...] = jnp.where(is_first, RESET, step)
    input_ref[...] = step * mixed_ref[...].astype(F32)
    for block in range(blocks):
        columns = slice(block * BLOCK, (block + 1) * BLOCK)
        in_map_ref[block, :, 0:BLOCK] = projected[DT_RANK : DT_RANK + STATE, columns]
        out_map_ref[block, :, 0:BLOCK] = projected[DT_RANK + STATE :, columns]
    rate = rate_ref[...] * (-math.log2(math.e))

    def advance(state, block, index):
        at = pl.multiple_of(block * BLOCK, BLOCK) + index
        decay = jnp.exp2(decay_ref[pl.ds(at, 1), :] * rate)
        entering = in_map_ref[block, :, index : index + 1] * input_ref[pl.ds(at, 1), :]
        return state * decay + entering

    def step_block(block, state):
        begin_ref[block] = state
        for index in range(BLOCK):
            state = advance(state, block, index)
            leaving = out_map_ref[block, :, index : index + 1] * state
            at = pl.multiple_of(block * BLOCK * 8, BLOCK * 8) + 8 * index
            half = leaving[:8, :] + leaving[8:, :]
            for tile in range(channels // LANES):
                partial_ref[tile, pl.ds(at, 8), :] = half[:, tile * LANES : (tile + 1) * LANES]
        return state

    state = lax.fori_loop(0, blocks, step_block, jnp.zeros((STATE, channels), F32))
    for p in range(prompts):
        if p < prompts - 1:
            last = ends[p] - 1
            block = last // BLOCK
            final_ref[...] = begin_ref[block]

            def again(index, _, block=block):
                at = block * BLOCK + index
                decay = jnp.exp2(decay_ref[pl.ds(at, 1), :] * rate)
                lane = lax.broadcasted_iota(jnp.int32, (STATE, LANES), 1)
                column = jnp.sum(
                    jnp.where(lane == index, in_map_ref[block], 0.0), axis=1, keepdims=True
                )
                entering = column * input_ref[pl.ds(at, 1), :]
                final_ref[...] = final_ref[...] * decay + entering
                return 0

            lax.fori_loop(0, last - block * BLOCK + 1, again, 0)
            final = final_ref[...].astype(BF16)
        else:
            final = state.astype(BF16)
        for tile in range(channels // LANES):
            at = (p * (channels // LANES) + tile) * STATE
            payload_ref[at : at + STATE, :] = final[:, tile * LANES : (tile + 1) * LANES]
    base = prompts * channels // LANES * STATE
    payload_ref[base:, :] = early_ref[...]
    scanned = []
    for tile in range(channels // LANES):
        total = partial_ref[tile, pl.ds(0, rows, stride=8), :]
        for index in range(1, 8):
            total = total + partial_ref[tile, pl.ds(index, rows, stride=8), :]
        scanned.append(total)
    scanned = jnp.concatenate(scanned, axis=1)
    gate = gate_ref[...].astype(F32)
    gated = (scanned + skip_ref[...] * mixed_ref[...].astype(F32)) * (gate * sigmoid(gate))
    gated_ref[...] = gated
    ones = jnp.ones((8, channels), BF16)
    sums_ref[0:1, :] = square_ref[0:1, :]
    sums_ref[1:2, :] = dot_nt(ones, (gated * gated).astype(BF16))[0:1, :]


def finish_kernel(
    prompts,
    pieces,
    order,
    me_ref,
    attended_ref,
    gated_ref,
    own_ref,
    other_ref,
    attention_gain_ref,
    mamba_gain_ref,
    *refs,
):
    piece_refs = refs[:pieces]
    (
        attention_ref,
        mamba_ref,
        keyval_ref,
        state_ref,
        conv_ref,
        window_ref,
        tail_ref,
        pick_vmem,
        pick_smem,
        sem,
    ) = refs[pieces:]
    me = me_ref[0]
    slots = keyval_ref.shape[0]
    channels = state_ref.shape[2]
    tiles = channels // LANES
    state_rows = prompts * tiles * STATE
    early = state_rows + prompts * WINDOW
    where = []
    for piece in range(pieces):
        for block in range(piece_refs[piece].shape[0]):
            where.append((piece, block))
    sources = len(where)

    key_rows, value_rows = [], []
    for index, (piece, block) in enumerate(where):
        request = piece_refs[piece][block, early : early + 16, :].astype(F32)
        mine = request[8:9, :] == me.astype(F32)
        key_rows.append(jnp.where(mine, request[9:10, :], -1.0))
        value_rows.append(request[10:11, :] + float(index * prompts))
    keys = jnp.concatenate(key_rows, axis=0).T
    values = jnp.concatenate(value_rows, axis=0).T
    lane = lax.broadcasted_iota(jnp.int32, (LANES, LANES), 1).astype(F32)
    total = jnp.zeros((LANES, LANES), F32)
    requests = LANES
    lane_ok = lax.broadcasted_iota(jnp.int32, (LANES, LANES), 0) < slots
    for index in range(sources):
        hit = (keys[:, index : index + 1] == lane) & lane_ok
        total = total + jnp.where(hit, values[:, index : index + 1], 0.0)
    pick = jnp.sum(total, axis=0, keepdims=True).astype(jnp.int32)
    pick_vmem[...] = pick
    pick_copy = pltpu.make_async_copy(pick_vmem, pick_smem, sem)
    pick_copy.start()

    for index, (piece, block) in enumerate(where):
        rows = piece_refs[piece]
        for p in range(prompts):
            at = state_rows + p * WINDOW
            pair = rows[block, at : at + WINDOW, :]
            window_ref[index * prompts + p, 0] = pair[:, :HEAD_DIM]
            window_ref[index * prompts + p, 1] = pair[:, HEAD_DIM:]
        for tile in range(tiles):
            tail_ref[index * 16 : (index + 1) * 16, tile * LANES : (tile + 1) * LANES] = rows[
                block, early + 16 * tile : early + 16 * (tile + 1), :
            ]

    sums = (own_ref[...] + other_ref[...])
    sums = jnp.concatenate([sums, jnp.zeros((6, sums.shape[1]), F32)], axis=0).T
    attention_scale = lax.rsqrt(sums[:, 0:1] / (HEADS * HEAD_DIM) + EPSILON)
    attention_ref[...] = (attended_ref[...] * attention_scale * attention_gain_ref[...]).astype(
        BF16
    )
    mamba_scale = lax.rsqrt(sums[:, 1:2] / INNER + EPSILON)
    mamba_ref[...] = (gated_ref[...] * mamba_scale * mamba_gain_ref[...]).astype(BF16)

    row = lax.broadcasted_iota(jnp.int32, (sources * 16, LANES), 0)
    depth = CONV - 1
    first = (pick // prompts) * 16 + (pick % prompts) * depth
    for tap in range(depth):
        hot = jnp.where(row == first + tap, 1.0, 0.0).T.astype(BF16)
        conv_ref[tap] = jnp.dot(hot[:slots, :], tail_ref[...], preferred_element_type=F32).astype(
            BF16
        )

    pick_copy.wait()

    def deliver(slot, _):
        wanted = pick_smem[0, slot]
        keyval_ref[slot] = window_ref[wanted]
        index = wanted // prompts
        p = wanted - index * prompts
        at = 0
        for piece in range(pieces):
            count = piece_refs[piece].shape[0]

            @pl.when((index >= at) & (index < at + count))
            def _(piece=piece, at=at):
                for tile in range(tiles):
                    start = pl.multiple_of((p * tiles + tile) * STATE, STATE)
                    state_ref[slot, :, tile * LANES : (tile + 1) * LANES] = piece_refs[piece][
                        index - at, pl.ds(start, STATE), :
                    ]

            at += count
        return 0

    lax.fori_loop(0, slots, deliver, 0)


def on_device(
    pr_size,
    tp_size,
    tokens,
    prompt_lengths,
    query_weight,
    key_weight,
    value_weight,
    attention_gain,
    inner_weight,
    conv_weight,
    scan_weight,
    step_weight,
    step_bias,
    mamba_rate,
    mamba_skip,
    mamba_gain,
    request_prompt,
    request_owner,
    request_slot,
):
    rows, width = tokens.shape
    prompts = prompt_lengths.shape[1]
    channels = inner_weight.shape[2]
    features = query_weight.shape[1]
    slots = request_owner.shape[0]
    tiles = channels // LANES

    def shape(dims, dtype=F32):
        return jax.ShapeDtypeStruct(dims, dtype)

    partial, mixed, tail = pl.pallas_call(
        functools.partial(mix_kernel, prompts),
        out_shape=(
            shape((DT_RANK + 2 * STATE, rows)),
            shape((rows, channels), BF16),
            shape((8, channels)),
        ),
        in_specs=[SMEM, ANY, ANY, VMEM, VMEM],
        out_specs=(VMEM, VMEM, VMEM),
        scratch_shapes=[
            pltpu.VMEM((rows, width), BF16),
            pltpu.VMEM((width, 2, channels), BF16),
            pltpu.VMEM((rows + 8, channels), F32),
            pltpu.SemaphoreType.DMA((2,)),
        ],
        compiler_params=params(32),
        name="mix",
    )(prompt_lengths, tokens, inner_weight, conv_weight, scan_weight.T)

    def swap(x, axis, size, bit):
        return lax.ppermute(x, axis, [(i, i ^ bit) for i in range(size)])

    near = swap(partial, "tp", tp_size, 1)
    early_rows = prompts * WINDOW + 16 * tiles
    attended, square, gate, early = pl.pallas_call(
        functools.partial(attend_kernel, prompts),
        out_shape=(
            shape((rows, features)),
            shape((8, rows)),
            shape((rows, channels), BF16),
            shape((early_rows, LANES), BF16),
        ),
        in_specs=[SMEM, VMEM, VMEM, VMEM, VMEM, ANY, VMEM, VMEM, VMEM, VMEM],
        out_specs=(VMEM, VMEM, VMEM, VMEM),
        scratch_shapes=[
            pltpu.VMEM((width, 2, channels), BF16),
            pltpu.VMEM((8, LANES), F32),
            pltpu.SemaphoreType.DMA,
        ],
        compiler_params=params(32),
        cost_estimate=pl.CostEstimate(
            flops=2 * rows * width * (features + channels), bytes_accessed=4 << 20, transcendentals=0
        ),
        name="attend",
    )(
        prompt_lengths,
        tokens,
        query_weight,
        key_weight.T,
        value_weight.T,
        inner_weight,
        tail,
        request_prompt[None],
        request_owner[None],
        request_slot[None],
    )
    pair = partial + near
    bit = 2
    while bit < tp_size // 2:
        pair = pair + swap(pair, "tp", tp_size, bit)
        bit *= 2
    far = swap(pair, "tp", tp_size, bit)

    payload_rows = prompts * tiles * STATE + early_rows
    gated, sums, payload = pl.pallas_call(
        functools.partial(scan_kernel, prompts),
        out_shape=(
            shape((rows, channels)),
            shape((2, rows)),
            shape((payload_rows, LANES), BF16),
        ),
        in_specs=[SMEM] + [VMEM] * 10,
        out_specs=(VMEM, VMEM, VMEM),
        scratch_shapes=[
            pltpu.VMEM((rows, channels), F32),
            pltpu.VMEM((rows, channels), F32),
            pltpu.VMEM((tiles, rows * 8, LANES), F32),
            pltpu.VMEM((rows // BLOCK, STATE, LANES), F32),
            pltpu.VMEM((rows // BLOCK, STATE, LANES), F32),
            pltpu.VMEM((rows // BLOCK, STATE, channels), F32),
            pltpu.VMEM((STATE, channels), F32),
        ],
        compiler_params=params(32),
        name="scan",
    )(
        prompt_lengths,
        pair,
        far,
        mixed,
        gate,
        step_weight,
        step_bias[None],
        mamba_rate,
        mamba_skip[None],
        early,
        square,
    )

    me = lax.axis_index("pr").astype(jnp.int32)
    pieces = [payload[None]]
    order = []
    bit = pr_size // 2
    while bit:
        held = pieces[0] if len(pieces) == 1 else jnp.concatenate(pieces, axis=0)
        pieces.append(swap(held, "pr", pr_size, bit))
        order.append(bit)
        bit //= 2
    bit = 1
    while bit < tp_size // 2:
        sums = sums + swap(sums, "tp", tp_size, bit)
        bit *= 2
    sums_far = swap(sums, "tp", tp_size, bit)

    attention_out, mamba_out, keyval, state, conv = pl.pallas_call(
        functools.partial(finish_kernel, prompts, len(pieces), tuple(order)),
        out_shape=(
            shape((rows, features), BF16),
            shape((rows, channels), BF16),
            shape((slots, 2, WINDOW, HEAD_DIM), BF16),
            shape((slots, STATE, channels), BF16),
            shape((CONV - 1, slots, channels), BF16),
        ),
        in_specs=[SMEM] + [VMEM] * (6 + len(pieces)),
        out_specs=(VMEM,) * 5,
        scratch_shapes=[
            pltpu.VMEM((pr_size * prompts, 2, WINDOW, HEAD_DIM), BF16),
            pltpu.VMEM((pr_size * 16, channels), BF16),
            pltpu.VMEM((1, LANES), jnp.int32),
            pltpu.SMEM((1, LANES), jnp.int32),
            pltpu.SemaphoreType.DMA,
        ],
        compiler_params=params(32),
        name="finish",
    )(
        me[None],
        attended,
        gated,
        sums,
        sums_far,
        attention_gain[None],
        mamba_gain[None],
        *pieces,
    )
    return (attention_out, mamba_out, keyval, state, conv.transpose(1, 0, 2))


def solution(mesh):
    return jax.shard_map(
        functools.partial(on_device, mesh.shape["pr"], mesh.shape["tp"]),
        mesh=mesh,
        in_specs=(
            P("pr", None),
            P("pr", None),
            P(None, "tp"),
            P(None, "tp"),
            P(None, "tp"),
            P("tp"),
            P(None, None, "tp"),
            P(None, "tp"),
            P("tp", None),
            P(None, "tp"),
            P("tp"),
            P(None, "tp"),
            P("tp"),
            P("tp"),
            P("pr"),
            P("pr"),
            P("pr"),
        ),
        out_specs=(
            P("pr", "tp"),
            P("pr", "tp"),
            P("pr", None, None, "tp"),
            P("pr", None, "tp"),
            P("pr", None, "tp"),
        ),
        check_vma=False,
    )
```

```python
import functools
import math

import jax
import jax.numpy as jnp
from jax import lax
from jax.experimental import pallas as pl
from jax.experimental.pallas import tpu as pltpu
from jax.sharding import PartitionSpec as P

HEADS = 16
KV_HEADS = 4
HEAD_DIM = 64
INNER = 2048
STATE = 16
DT_RANK = 64
CONV = 4
WINDOW = 32
EPSILON = 1e-06
LANES = 128
BLOCK = 16
RESET = 1e30

F32 = jnp.float32
BF16 = jnp.bfloat16
VMEM = pl.BlockSpec(memory_space=pltpu.VMEM)
SMEM = pl.BlockSpec(memory_space=pltpu.SMEM)
ANY = pl.BlockSpec(memory_space=pl.ANY)


def params(mib):
    return pltpu.CompilerParams(vmem_limit_bytes=mib << 20)


def dot_nt(a, b):
    return lax.dot_general(a, b, (((1,), (1,)), ((), ())), preferred_element_type=F32)


def bounds(len_ref, prompts):
    starts, ends = [], []
    at = 0
    for p in range(prompts):
        starts.append(at)
        at = at + len_ref[0, p]
        ends.append(at)
    return starts, ends


def first_row_of(position, starts, prompts):
    first = jnp.zeros_like(position)
    for p in range(1, prompts):
        first = jnp.where(position >= starts[p], starts[p], first)
    return first


def interleave(tokens, which):
    out = []
    for at in range(0, tokens.shape[1], LANES):
        wide = min(LANES, tokens.shape[1] - at)
        row = lax.broadcasted_iota(jnp.int32, (wide, 2 * wide), 0)
        column = lax.broadcasted_iota(jnp.int32, (wide, 2 * wide), 1)
        pick = jnp.where(column == 2 * row + which, 1.0, 0.0).astype(BF16)
        out.append(
            jnp.dot(tokens[:, at : at + wide], pick, preferred_element_type=F32).astype(BF16)
        )
    return jnp.concatenate(out, axis=1)


def last_rows(shape, depth, starts, ends):
    row = lax.broadcasted_iota(jnp.int32, shape, 0)
    position = lax.broadcasted_iota(jnp.int32, shape, 1)
    hit = jnp.zeros(shape, F32)
    for p in range(len(starts)):
        here = (row >= p * depth) & (row < (p + 1) * depth) & (position >= starts[p])
        hit = jnp.where(here & (position - row == ends[p] - (p + 1) * depth), 1.0, hit)
    return hit.astype(BF16)


def sigmoid(x):
    return 0.5 * jnp.tanh(0.5 * x) + 0.5


def mix_kernel(
    prompts,
    len_hbm,
    tokens_hbm,
    inner_hbm,
    conv_hbm,
    scan_hbm,
    partial_ref,
    mixed_ref,
    tail_ref,
    len_ref,
    tokens_ref,
    inner_ref,
    conv_ref,
    scan_ref,
    raw_ref,
    sems,
):
    tokens_copy = pltpu.make_async_copy(tokens_hbm, tokens_ref, sems.at[0])
    inner_copy = pltpu.make_async_copy(inner_hbm, inner_ref, sems.at[1])
    small_copies = [
        pltpu.make_async_copy(len_hbm, len_ref, sems.at[2]),
        pltpu.make_async_copy(conv_hbm, conv_ref, sems.at[3]),
        pltpu.make_async_copy(scan_hbm, scan_ref, sems.at[4]),
    ]
    tokens_copy.start()
    inner_copy.start()
    for copy in small_copies:
        copy.start()
    rows, width = tokens_ref.shape
    channels = inner_ref.shape[2]
    tokens_copy.wait()
    spread = interleave(tokens_ref[...], 0)
    inner_copy.wait()
    weight = inner_ref[...].reshape(2 * width, channels)
    raw = jnp.dot(spread, weight, preferred_element_type=F32).astype(BF16).astype(F32)
    raw_ref[pl.ds(0, 8), :] = jnp.zeros((8, channels), F32)
    raw_ref[pl.ds(8, rows), :] = raw
    for copy in small_copies:
        copy.wait()
    starts, ends = bounds(len_ref, prompts)
    position = lax.broadcasted_iota(jnp.int32, (rows, 1), 0)
    offset = position - first_row_of(position, starts, prompts)
    total = raw * conv_ref[CONV - 1 : CONV, :]
    for lag in range(1, CONV):
        shifted = raw_ref[pl.ds(8 - lag, rows), :]
        shifted = jnp.where(offset >= lag, shifted, 0.0)
        total = total + shifted * conv_ref[CONV - 1 - lag : CONV - lag, :]
    mixed = (total * sigmoid(total)).astype(BF16)
    mixed_ref[...] = mixed
    partial_ref[...] = dot_nt(scan_ref[...], mixed)
    pick = last_rows((8, rows), CONV - 1, starts, ends)
    tail_ref[...] = jnp.dot(pick, raw.astype(BF16), preferred_element_type=F32)


def attend_kernel(
    prompts,
    len_ref,
    tokens_ref,
    query_ref,
    key_ref,
    value_ref,
    inner_hbm,
    tail_ref,
    prompt_ref,
    owner_ref,
    slot_ref,
    attended_ref,
    square_ref,
    gate_ref,
    packed_ref,
    inner_ref,
    request_ref,
    sem,
):
    inner_copy = pltpu.make_async_copy(inner_hbm, inner_ref, sem)
    inner_copy.start()
    rows, width = tokens_ref.shape
    channels = inner_ref.shape[2]
    features = query_ref.shape[1]
    group = features // HEAD_DIM
    starts, ends = bounds(len_ref, prompts)
    tokens = tokens_ref[...]
    queries = jnp.dot(tokens, query_ref[...], preferred_element_type=F32).astype(BF16)
    keys = dot_nt(tokens, jnp.concatenate([key_ref[...]] * group, axis=0)).astype(BF16)
    values = dot_nt(tokens, jnp.concatenate([value_ref[...]] * group, axis=0)).astype(BF16)
    at_row = lax.broadcasted_iota(jnp.int32, (rows, rows), 0)
    at_column = lax.broadcasted_iota(jnp.int32, (rows, rows), 1)
    row_first = first_row_of(at_row, starts, prompts)
    allowed = (at_column <= at_row) & (at_row - at_column < WINDOW) & (at_column >= row_first)
    head_of = lax.broadcasted_iota(jnp.int32, (rows, features), 1) // HEAD_DIM
    zero = jnp.zeros((), BF16)
    attended = jnp.zeros((rows, features), F32)
    for head in range(group):
        mine = head_of == head
        scores = dot_nt(queries, jnp.where(mine, keys, zero)) * HEAD_DIM ** (-0.5)
        scores = jnp.where(allowed, scores, -1e30)
        top = jnp.max(scores, axis=1, keepdims=True)
        expons = jnp.exp(scores - top)
        weights = expons * (1.0 / jnp.sum(expons, axis=1, keepdims=True))
        attended = attended + jnp.dot(
            weights.astype(BF16), jnp.where(mine, values, zero), preferred_element_type=F32
        )
    attended_ref[...] = attended
    ones = jnp.ones((8, features), BF16)
    square_ref[...] = dot_nt(ones, (attended * attended).astype(BF16))
    lane = lax.broadcasted_iota(jnp.int32, (rows, LANES), 1)
    both = jnp.where(lane < HEAD_DIM, keys[:, :LANES], values[:, :LANES])
    pick = last_rows((prompts * WINDOW, rows), WINDOW, starts, ends)
    packed_ref[: prompts * WINDOW, :] = jnp.dot(pick, both, preferred_element_type=F32).astype(
        BF16
    )
    requests = owner_ref.shape[1]
    request_ref[...] = jnp.full(request_ref.shape, -1, jnp.int32)
    request_ref[0:1, 0:requests] = owner_ref[...]
    request_ref[1:2, 0:requests] = slot_ref[...]
    request_ref[2:3, 0:requests] = prompt_ref[...]
    owners = packed_ref.shape[0] - prompts * WINDOW - 8 * (channels // LANES)
    owner = lax.broadcasted_iota(jnp.int32, (owners, LANES), 0) == request_ref[0:1, :]
    slot = lax.broadcasted_iota(jnp.int32, (LANES, LANES), 0) == request_ref[1:2, :]
    number = request_ref[2:3, :] + 1
    filled = dot_nt(
        jnp.where(owner, 1.0, 0.0).astype(BF16),
        jnp.where(slot, number, 0).astype(F32).astype(BF16),
    )
    base = prompts * WINDOW
    for tile in range(0, channels // LANES, 2):
        packed_ref[base + 8 * tile : base + 8 * (tile + 2), :] = jnp.concatenate(
            [
                tail_ref[:, tile * LANES : (tile + 1) * LANES],
                tail_ref[:, (tile + 1) * LANES : (tile + 2) * LANES],
            ],
            axis=0,
        ).astype(BF16)
    packed_ref[base + 8 * (channels // LANES) :, :] = filled.astype(BF16)
    inner_copy.wait()
    spread = interleave(tokens, 1)
    gate_ref[...] = jnp.dot(
        spread, inner_ref[...].reshape(2 * width, channels), preferred_element_type=F32
    ).astype(BF16)


def scan_kernel(
    prompts,
    len_ref,
    own_ref,
    other_ref,
    mixed_ref,
    gate_ref,
    step_weight_ref,
    step_bias_ref,
    rate_ref,
    skip_ref,
    early_ref,
    square_ref,
    gated_ref,
    sums_ref,
    payload_ref,
    decay_ref,
    input_ref,
    partial_ref,
    in_map_ref,
    out_map_ref,
    begin_ref,
    final_ref,
):
    rows, channels = mixed_ref.shape
    blocks = rows // BLOCK
    starts, ends = bounds(len_ref, prompts)
    projected = own_ref[...] + other_ref[...]
    low = projected[:DT_RANK, :].T.astype(BF16)
    pre = jnp.dot(low, step_weight_ref[...], preferred_element_type=F32) + step_bias_ref[...]
    step = jnp.maximum(pre, 0.0) + jnp.log1p(jnp.exp(-jnp.abs(pre)))
    position = lax.broadcasted_iota(jnp.int32, (rows, 1), 0)
    is_first = position == 0
    for p in range(1, prompts):
        is_first = is_first | (position == starts[p])
    decay_ref[...] = jnp.where(is_first, RESET, step)
    input_ref[...] = step * mixed_ref[...].astype(F32)
    for block in range(blocks):
        columns = slice(block * BLOCK, (block + 1) * BLOCK)
        in_map_ref[block, :, 0:BLOCK] = projected[DT_RANK : DT_RANK + STATE, columns]
        out_map_ref[block, :, 0:BLOCK] = projected[DT_RANK + STATE :, columns]
    rate = rate_ref[...] * (-math.log2(math.e))

    def advance(state, block, index):
        at = pl.multiple_of(block * BLOCK, BLOCK) + index
        decay = jnp.exp2(decay_ref[pl.ds(at, 1), :] * rate)
        entering = in_map_ref[block, :, index : index + 1] * input_ref[pl.ds(at, 1), :]
        return state * decay + entering

    def step_block(block, state):
        begin_ref[block] = state
        for index in range(BLOCK):
            state = advance(state, block, index)
            leaving = out_map_ref[block, :, index : index + 1] * state
            at = pl.multiple_of(block * BLOCK * 8, BLOCK * 8) + 8 * index
            half = leaving[:8, :] + leaving[8:, :]
            for tile in range(channels // LANES):
                partial_ref[tile, pl.ds(at, 8), :] = half[:, tile * LANES : (tile + 1) * LANES]
        return state

    state = lax.fori_loop(0, blocks, step_block, jnp.zeros((STATE, channels), F32))
    for p in range(prompts):
        if p < prompts - 1:
            last = ends[p] - 1
            block = last // BLOCK
            final_ref[...] = begin_ref[block]

            def again(index, _, block=block):
                at = block * BLOCK + index
                decay = jnp.exp2(decay_ref[pl.ds(at, 1), :] * rate)
                lane = lax.broadcasted_iota(jnp.int32, (STATE, LANES), 1)
                column = jnp.sum(
                    jnp.where(lane == index, in_map_ref[block], 0.0), axis=1, keepdims=True
                )
                entering = column * input_ref[pl.ds(at, 1), :]
                final_ref[...] = final_ref[...] * decay + entering
                return 0

            lax.fori_loop(0, last - block * BLOCK + 1, again, 0)
            final = final_ref[...].astype(BF16)
        else:
            final = state.astype(BF16)
        for tile in range(channels // LANES):
            at = (p * (channels // LANES) + tile) * STATE
            payload_ref[at : at + STATE, :] = final[:, tile * LANES : (tile + 1) * LANES]
    base = prompts * channels // LANES * STATE
    payload_ref[base:, :] = early_ref[...]
    scanned = []
    for tile in range(channels // LANES):
        total = partial_ref[tile, pl.ds(0, rows, stride=8), :]
        for index in range(1, 8):
            total = total + partial_ref[tile, pl.ds(index, rows, stride=8), :]
        scanned.append(total)
    scanned = jnp.concatenate(scanned, axis=1)
    gate = gate_ref[...].astype(F32)
    gated = (scanned + skip_ref[...] * mixed_ref[...].astype(F32)) * (gate * sigmoid(gate))
    gated_ref[...] = gated
    ones = jnp.ones((8, channels), BF16)
    sums_ref[0:1, :] = square_ref[0:1, :]
    sums_ref[1:2, :] = dot_nt(ones, (gated * gated).astype(BF16))[0:1, :]


def join_kernel(held_ref, new_ref, own_ref, other_ref, joined_ref, sums_ref):
    count = held_ref.shape[0]
    joined_ref[:count] = held_ref[...]
    joined_ref[count:] = new_ref[...]
    sums_ref[...] = own_ref[...] + other_ref[...]


def norm_kernel(
    attended_ref,
    gated_ref,
    sums_ref,
    attention_gain_ref,
    mamba_gain_ref,
    attention_ref,
    mamba_ref,
):
    sums = sums_ref[...]
    sums = jnp.concatenate([sums, jnp.zeros((6, sums.shape[1]), F32)], axis=0).T
    attention_scale = lax.rsqrt(sums[:, 0:1] / (HEADS * HEAD_DIM) + EPSILON)
    attention_ref[...] = (attended_ref[...] * attention_scale * attention_gain_ref[...]).astype(
        BF16
    )
    mamba_scale = lax.rsqrt(sums[:, 1:2] / INNER + EPSILON)
    mamba_ref[...] = (gated_ref[...] * mamba_scale * mamba_gain_ref[...]).astype(BF16)


def one_hot(hit):
    return jnp.where(hit, 1.0, 0.0).astype(BF16)


def deliver_kernel(
    prompts,
    me_ref,
    held_ref,
    new_ref,
    keyval_hbm,
    state_hbm,
    conv_hbm,
    keyval_ref,
    state_ref,
    conv_ref,
    sems,
):
    me = me_ref[0]
    slots, _, channels = state_ref.shape
    tiles = channels // LANES
    half = held_ref.shape[0]
    sources = 2 * half
    window_at = prompts * tiles * STATE
    tail_at = window_at + prompts * WINDOW
    table_at = tail_at + 8 * tiles
    owners = held_ref.shape[1] - table_at

    def rows_of(source, at, size):
        ref, index = (held_ref, source) if source < half else (new_ref, source - half)
        return ref[index, at : at + size, :]

    owner = lax.broadcasted_iota(jnp.int32, (owners, LANES), 0)
    pick = jnp.zeros((1, LANES), F32)
    for source in range(sources):
        filled = rows_of(source, table_at, owners).astype(F32)
        filled = jnp.sum(jnp.where(owner == me, filled, 0.0), axis=0, keepdims=True)
        pick = pick + jnp.where(filled > 0.5, filled + float(source * prompts - 1), 0.0)
    pick = pick.astype(jnp.int32)

    chunk = min(sources, 8)
    picked_rows = slots * STATE
    row = lax.broadcasted_iota(jnp.int32, (picked_rows, LANES), 0)
    lane = lax.broadcasted_iota(jnp.int32, (picked_rows, LANES), 1)
    spread = one_hot(row // STATE == lane)
    span = chunk * prompts * STATE
    row = lax.broadcasted_iota(jnp.int32, (picked_rows, span), 0)
    lane = lax.broadcasted_iota(jnp.int32, (picked_rows, span), 1)
    same = row % STATE == lane % STATE
    states, windows, tails = None, None, None
    wide = -(-slots // 16) * 16
    row = lax.broadcasted_iota(jnp.int32, (wide, LANES), 0)
    lane = lax.broadcasted_iota(jnp.int32, (wide, LANES), 1)
    unit = one_hot(row == lane)
    depth = CONV - 1
    for first in range(0, sources, chunk):
        wanted = lax.broadcasted_iota(jnp.int32, (span, LANES), 0) // STATE + first * prompts
        take = dot_nt(spread, one_hot(wanted == pick))
        take = jnp.where(same, take, 0.0).astype(BF16)
        table = []
        for source in range(first, first + chunk):
            for p in range(prompts):
                at = p * tiles * STATE
                table.append(
                    jnp.concatenate(
                        [
                            rows_of(source, at + tile * STATE, STATE)
                            for tile in range(tiles)
                        ],
                        axis=1,
                    )
                )
        part = jnp.dot(take, jnp.concatenate(table, axis=0), preferred_element_type=F32)
        states = part if states is None else states + part
        table = []
        for source in range(first, first + chunk):
            for p in range(prompts):
                at = window_at + p * WINDOW
                table.append(
                    jnp.concatenate(
                        [
                            rows_of(source, at, WINDOW // 2),
                            rows_of(source, at + WINDOW // 2, WINDOW // 2),
                        ],
                        axis=1,
                    )
                )
        part = jnp.dot(take, jnp.concatenate(table, axis=0), preferred_element_type=F32)
        windows = part if windows is None else windows + part
        table = []
        for source in range(first, first + chunk):
            table.append(
                jnp.concatenate(
                    [rows_of(source, tail_at + 8 * tile, 16) for tile in range(0, tiles, 2)],
                    axis=1,
                )
            )
        span_rows = chunk * 16
        row = lax.broadcasted_iota(jnp.int32, (span_rows, LANES), 0)
        local = pick - first * prompts
        base = (local // prompts) * 16 + (local % prompts) * depth
        hits = [one_hot(row == base + 8 * odd + tap) for odd in (0, 1) for tap in range(depth)]
        hits = dot_nt(unit, jnp.concatenate(hits, axis=0)).astype(BF16)
        hits = jnp.concatenate(
            [hits[:, i * span_rows : (i + 1) * span_rows] for i in range(2 * depth)], axis=0
        )
        part = jnp.dot(hits, jnp.concatenate(table, axis=0), preferred_element_type=F32)
        tails = part if tails is None else tails + part

    state_ref[...] = states.astype(BF16).reshape(slots, STATE, channels)
    state_copy = pltpu.make_async_copy(state_ref, state_hbm, sems.at[0])
    state_copy.start()
    windows = windows.astype(BF16).reshape(slots, WINDOW // 2, 2 * LANES)
    for upper in range(2):
        for kind in range(2):
            at = upper * LANES + kind * HEAD_DIM
            keyval_ref[:, kind, upper * WINDOW // 2 : (upper + 1) * WINDOW // 2, :] = windows[
                :, :, at : at + HEAD_DIM
            ]
    keyval_copy = pltpu.make_async_copy(keyval_ref, keyval_hbm, sems.at[1])
    keyval_copy.start()
    for odd in range(2):
        for tap in range(depth):
            at = (odd * depth + tap) * wide
            for pair in range(tiles // 2):
                tile = 2 * pair + odd
                conv_ref[tap, :, tile * LANES : (tile + 1) * LANES] = tails[
                    at : at + slots, pair * LANES : (pair + 1) * LANES
                ].astype(BF16)
    conv_copy = pltpu.make_async_copy(conv_ref, conv_hbm, sems.at[2])
    conv_copy.start()
    state_copy.wait()
    keyval_copy.wait()
    conv_copy.wait()


def on_device(
    pr_size,
    tp_size,
    tokens,
    prompt_lengths,
    query_weight,
    key_weight,
    value_weight,
    attention_gain,
    inner_weight,
    conv_weight,
    scan_weight,
    step_weight,
    step_bias,
    mamba_rate,
    mamba_skip,
    mamba_gain,
    request_prompt,
    request_owner,
    request_slot,
):
    rows, width = tokens.shape
    prompts = prompt_lengths.shape[1]
    channels = inner_weight.shape[2]
    features = query_weight.shape[1]
    slots = request_owner.shape[0]
    tiles = channels // LANES

    def shape(dims, dtype=F32):
        return jax.ShapeDtypeStruct(dims, dtype)

    partial, mixed, tail = pl.pallas_call(
        functools.partial(mix_kernel, prompts),
        out_shape=(
            shape((DT_RANK + 2 * STATE, rows)),
            shape((rows, channels), BF16),
            shape((8, channels)),
        ),
        in_specs=[ANY] * 5,
        out_specs=(VMEM, VMEM, VMEM),
        scratch_shapes=[
            pltpu.SMEM((1, prompts), jnp.int32),
            pltpu.VMEM((rows, width), BF16),
            pltpu.VMEM((width, 2, channels), BF16),
            pltpu.VMEM(conv_weight.shape, F32),
            pltpu.VMEM(scan_weight.shape[::-1], BF16),
            pltpu.VMEM((rows + 8, channels), F32),
            pltpu.SemaphoreType.DMA((5,)),
        ],
        compiler_params=params(56),
        name="mix",
    )(prompt_lengths, tokens, inner_weight, conv_weight, scan_weight.T)

    def swap(x, axis, size, bit):
        return lax.ppermute(x, axis, [(i, i ^ bit) for i in range(size)])

    near = swap(partial, "tp", tp_size, 1)
    owners = -(-pr_size // 16) * 16
    early_rows = prompts * WINDOW + 8 * tiles + owners
    attended, square, gate, early = pl.pallas_call(
        functools.partial(attend_kernel, prompts),
        out_shape=(
            shape((rows, features)),
            shape((8, rows)),
            shape((rows, channels), BF16),
            shape((early_rows, LANES), BF16),
        ),
        in_specs=[SMEM, VMEM, VMEM, VMEM, VMEM, ANY, VMEM, VMEM, VMEM, VMEM],
        out_specs=(VMEM, VMEM, VMEM, VMEM),
        scratch_shapes=[
            pltpu.VMEM((width, 2, channels), BF16),
            pltpu.VMEM((8, LANES), jnp.int32),
            pltpu.SemaphoreType.DMA,
        ],
        compiler_params=params(32),
        cost_estimate=pl.CostEstimate(
            flops=2 * rows * width * (features + channels), bytes_accessed=4 << 20, transcendentals=0
        ),
        name="attend",
    )(
        prompt_lengths,
        tokens,
        query_weight,
        key_weight.T,
        value_weight.T,
        inner_weight,
        tail,
        request_prompt[None],
        request_owner[None],
        request_slot[None],
    )
    pair = partial + near
    bit = 2
    while bit < tp_size // 2:
        pair = pair + swap(pair, "tp", tp_size, bit)
        bit *= 2
    far = swap(pair, "tp", tp_size, bit)

    payload_rows = prompts * tiles * STATE + early_rows
    gated, sums, payload = pl.pallas_call(
        functools.partial(scan_kernel, prompts),
        out_shape=(
            shape((rows, channels)),
            shape((2, rows)),
            shape((payload_rows, LANES), BF16),
        ),
        in_specs=[SMEM] + [VMEM] * 10,
        out_specs=(VMEM, VMEM, VMEM),
        scratch_shapes=[
            pltpu.VMEM((rows, channels), F32),
            pltpu.VMEM((rows, channels), F32),
            pltpu.VMEM((tiles, rows * 8, LANES), F32),
            pltpu.VMEM((rows // BLOCK, STATE, LANES), F32),
            pltpu.VMEM((rows // BLOCK, STATE, LANES), F32),
            pltpu.VMEM((rows // BLOCK, STATE, channels), F32),
            pltpu.VMEM((STATE, channels), F32),
        ],
        compiler_params=params(32),
        name="scan",
    )(
        prompt_lengths,
        pair,
        far,
        mixed,
        gate,
        step_weight,
        step_bias[None],
        mamba_rate,
        mamba_skip[None],
        early,
        square,
    )

    me = lax.axis_index("pr").astype(jnp.int32)
    held = payload[None]
    pr_bits = [1 << i for i in reversed(range((pr_size - 1).bit_length()))]
    tp_bits = [1 << i for i in range((tp_size - 1).bit_length())]
    for index in range(max(len(pr_bits) - 1, len(tp_bits))):
        new = swap(held, "pr", pr_size, pr_bits[index]) if index < len(pr_bits) - 1 else None
        other = swap(sums, "tp", tp_size, tp_bits[index]) if index < len(tp_bits) else None
        if new is None:
            sums = sums + other
        elif other is None:
            held = jnp.concatenate([held, new], axis=0)
        else:
            held, sums = pl.pallas_call(
                join_kernel,
                out_shape=(
                    shape((2 * held.shape[0],) + held.shape[1:], BF16),
                    shape(sums.shape),
                ),
                in_specs=[VMEM] * 4,
                out_specs=(VMEM, VMEM),
                name="join",
            )(held, new, sums, other)
    new = swap(held, "pr", pr_size, pr_bits[-1])
    attention_out, mamba_out = pl.pallas_call(
        norm_kernel,
        out_shape=(shape((rows, features), BF16), shape((rows, channels), BF16)),
        in_specs=[VMEM] * 5,
        out_specs=(VMEM, VMEM),
        cost_estimate=pl.CostEstimate(flops=1 << 24, bytes_accessed=2 << 20, transcendentals=0),
        name="norm",
    )(attended, gated, sums, attention_gain[None], mamba_gain[None])
    keyval, state, conv = pl.pallas_call(
        functools.partial(deliver_kernel, prompts),
        out_shape=(
            shape((slots, 2, WINDOW, HEAD_DIM), BF16),
            shape((slots, STATE, channels), BF16),
            shape((CONV - 1, slots, channels), BF16),
        ),
        in_specs=[SMEM, VMEM, VMEM],
        out_specs=(ANY, ANY, ANY),
        scratch_shapes=[
            pltpu.VMEM((slots, 2, WINDOW, HEAD_DIM), BF16),
            pltpu.VMEM((slots, STATE, channels), BF16),
            pltpu.VMEM((CONV - 1, slots, channels), BF16),
            pltpu.SemaphoreType.DMA((3,)),
        ],
        compiler_params=params(32),
        name="deliver",
    )(me[None], held, new)
    return (attention_out, mamba_out, keyval, state, conv.transpose(1, 0, 2))


def solution(mesh):
    return jax.shard_map(
        functools.partial(on_device, mesh.shape["pr"], mesh.shape["tp"]),
        mesh=mesh,
        in_specs=(
            P("pr", None),
            P("pr", None),
            P(None, "tp"),
            P(None, "tp"),
            P(None, "tp"),
            P("tp"),
            P(None, None, "tp"),
            P(None, "tp"),
            P("tp", None),
            P(None, "tp"),
            P("tp"),
            P(None, "tp"),
            P("tp"),
            P("tp"),
            P("pr"),
            P("pr"),
            P("pr"),
        ),
        out_specs=(
            P("pr", "tp"),
            P("pr", "tp"),
            P("pr", None, None, "tp"),
            P("pr", None, "tp"),
            P("pr", None, "tp"),
        ),
        check_vma=False,
    )
```

```python
import functools
import math

import jax
import jax.numpy as jnp
from jax import lax
from jax.experimental import pallas as pl
from jax.experimental.pallas import tpu as pltpu
from jax.sharding import PartitionSpec as P

HEADS = 16
KV_HEADS = 4
HEAD_DIM = 64
INNER = 2048
STATE = 16
DT_RANK = 64
CONV = 4
WINDOW = 32
EPSILON = 1e-06
LANES = 128
BLOCK = 16
RESET = 1e30

F32 = jnp.float32
BF16 = jnp.bfloat16
VMEM = pl.BlockSpec(memory_space=pltpu.VMEM)
SMEM = pl.BlockSpec(memory_space=pltpu.SMEM)
ANY = pl.BlockSpec(memory_space=pl.ANY)
HBM = pl.BlockSpec(memory_space=pltpu.HBM)


def params(mib):
    return pltpu.CompilerParams(vmem_limit_bytes=mib << 20)


def dot_nt(a, b):
    return lax.dot_general(a, b, (((1,), (1,)), ((), ())), preferred_element_type=F32)


def bounds(len_ref, prompts):
    starts, ends = [], []
    at = 0
    for p in range(prompts):
        starts.append(at)
        at = at + len_ref[0, p]
        ends.append(at)
    return starts, ends


def first_row_of(position, starts, prompts):
    first = jnp.zeros_like(position)
    for p in range(1, prompts):
        first = jnp.where(position >= starts[p], starts[p], first)
    return first


def interleave(tokens, which):
    out = []
    for at in range(0, tokens.shape[1], LANES):
        wide = min(LANES, tokens.shape[1] - at)
        row = lax.broadcasted_iota(jnp.int32, (wide, 2 * wide), 0)
        column = lax.broadcasted_iota(jnp.int32, (wide, 2 * wide), 1)
        pick = jnp.where(column == 2 * row + which, 1.0, 0.0).astype(BF16)
        out.append(
            jnp.dot(tokens[:, at : at + wide], pick, preferred_element_type=F32).astype(BF16)
        )
    return jnp.concatenate(out, axis=1)


def last_rows(shape, depth, starts, ends):
    row = lax.broadcasted_iota(jnp.int32, shape, 0)
    position = lax.broadcasted_iota(jnp.int32, shape, 1)
    hit = jnp.zeros(shape, F32)
    for p in range(len(starts)):
        here = (row >= p * depth) & (row < (p + 1) * depth) & (position >= starts[p])
        hit = jnp.where(here & (position - row == ends[p] - (p + 1) * depth), 1.0, hit)
    return hit.astype(BF16)


def sigmoid(x):
    return 0.5 * jnp.tanh(0.5 * x) + 0.5


def mix_kernel(
    prompts,
    len_hbm,
    tokens_hbm,
    inner_hbm,
    conv_hbm,
    scan_hbm,
    partial_ref,
    mixed_ref,
    tail_ref,
    len_ref,
    tokens_ref,
    inner_ref,
    conv_ref,
    scan_ref,
    raw_ref,
    sems,
):
    tokens_copy = pltpu.make_async_copy(tokens_hbm, tokens_ref, sems.at[0])
    inner_copy = pltpu.make_async_copy(inner_hbm, inner_ref, sems.at[1])
    small_copies = [
        pltpu.make_async_copy(len_hbm, len_ref, sems.at[2]),
        pltpu.make_async_copy(conv_hbm, conv_ref, sems.at[3]),
        pltpu.make_async_copy(scan_hbm, scan_ref, sems.at[4]),
    ]
    tokens_copy.start()
    inner_copy.start()
    for copy in small_copies:
        copy.start()
    rows, width = tokens_ref.shape
    channels = inner_ref.shape[2]
    tokens_copy.wait()
    spread = interleave(tokens_ref[...], 0)
    inner_copy.wait()
    weight = inner_ref[...].reshape(2 * width, channels)
    raw = jnp.dot(spread, weight, preferred_element_type=F32).astype(BF16).astype(F32)
    raw_ref[pl.ds(0, 8), :] = jnp.zeros((8, channels), F32)
    raw_ref[pl.ds(8, rows), :] = raw
    for copy in small_copies:
        copy.wait()
    starts, ends = bounds(len_ref, prompts)
    position = lax.broadcasted_iota(jnp.int32, (rows, 1), 0)
    offset = position - first_row_of(position, starts, prompts)
    total = raw * conv_ref[CONV - 1 : CONV, :]
    for lag in range(1, CONV):
        shifted = raw_ref[pl.ds(8 - lag, rows), :]
        shifted = jnp.where(offset >= lag, shifted, 0.0)
        total = total + shifted * conv_ref[CONV - 1 - lag : CONV - lag, :]
    mixed = (total * sigmoid(total)).astype(BF16)
    mixed_ref[...] = mixed
    partial_ref[...] = dot_nt(scan_ref[...], mixed)
    pick = last_rows((8, rows), CONV - 1, starts, ends)
    tail_ref[...] = jnp.dot(pick, raw.astype(BF16), preferred_element_type=F32)


def attend_kernel(
    prompts,
    len_ref,
    tokens_ref,
    query_ref,
    key_ref,
    value_ref,
    inner_hbm,
    tail_ref,
    prompt_ref,
    owner_ref,
    slot_ref,
    attended_ref,
    square_ref,
    gate_ref,
    packed_ref,
    inner_ref,
    request_ref,
    sem,
):
    inner_copy = pltpu.make_async_copy(inner_hbm, inner_ref, sem)
    inner_copy.start()
    rows, width = tokens_ref.shape
    channels = inner_ref.shape[2]
    features = query_ref.shape[1]
    group = features // HEAD_DIM
    starts, ends = bounds(len_ref, prompts)
    tokens = tokens_ref[...]
    queries = jnp.dot(tokens, query_ref[...], preferred_element_type=F32).astype(BF16)
    keys = dot_nt(tokens, jnp.concatenate([key_ref[...]] * group, axis=0)).astype(BF16)
    values = dot_nt(tokens, jnp.concatenate([value_ref[...]] * group, axis=0)).astype(BF16)
    at_row = lax.broadcasted_iota(jnp.int32, (rows, rows), 0)
    at_column = lax.broadcasted_iota(jnp.int32, (rows, rows), 1)
    row_first = first_row_of(at_row, starts, prompts)
    allowed = (at_column <= at_row) & (at_row - at_column < WINDOW) & (at_column >= row_first)
    head_of = lax.broadcasted_iota(jnp.int32, (rows, features), 1) // HEAD_DIM
    zero = jnp.zeros((), BF16)
    attended = jnp.zeros((rows, features), F32)
    for head in range(group):
        mine = head_of == head
        scores = dot_nt(queries, jnp.where(mine, keys, zero)) * HEAD_DIM ** (-0.5)
        scores = jnp.where(allowed, scores, -1e30)
        top = jnp.max(scores, axis=1, keepdims=True)
        expons = jnp.exp(scores - top)
        weights = expons * (1.0 / jnp.sum(expons, axis=1, keepdims=True))
        attended = attended + jnp.dot(
            weights.astype(BF16), jnp.where(mine, values, zero), preferred_element_type=F32
        )
    attended_ref[...] = attended
    ones = jnp.ones((8, features), BF16)
    square_ref[...] = dot_nt(ones, (attended * attended).astype(BF16))
    lane = lax.broadcasted_iota(jnp.int32, (rows, LANES), 1)
    both = jnp.where(lane < HEAD_DIM, keys[:, :LANES], values[:, :LANES])
    pick = last_rows((prompts * WINDOW, rows), WINDOW, starts, ends)
    packed_ref[: prompts * WINDOW, :] = jnp.dot(pick, both, preferred_element_type=F32).astype(
        BF16
    )
    requests = owner_ref.shape[1]
    request_ref[...] = jnp.full(request_ref.shape, -1, jnp.int32)
    request_ref[0:1, 0:requests] = owner_ref[...]
    request_ref[1:2, 0:requests] = slot_ref[...]
    request_ref[2:3, 0:requests] = prompt_ref[...]
    owners = packed_ref.shape[0] - prompts * WINDOW - 8 * (channels // LANES)
    owner = lax.broadcasted_iota(jnp.int32, (owners, LANES), 0) == request_ref[0:1, :]
    slot = lax.broadcasted_iota(jnp.int32, (LANES, LANES), 0) == request_ref[1:2, :]
    number = request_ref[2:3, :] + 1
    filled = dot_nt(
        jnp.where(owner, 1.0, 0.0).astype(BF16),
        jnp.where(slot, number, 0).astype(F32).astype(BF16),
    )
    base = prompts * WINDOW
    for tile in range(0, channels // LANES, 2):
        packed_ref[base + 8 * tile : base + 8 * (tile + 2), :] = jnp.concatenate(
            [
                tail_ref[:, tile * LANES : (tile + 1) * LANES],
                tail_ref[:, (tile + 1) * LANES : (tile + 2) * LANES],
            ],
            axis=0,
        ).astype(BF16)
    packed_ref[base + 8 * (channels // LANES) :, :] = filled.astype(BF16)
    inner_copy.wait()
    spread = interleave(tokens, 1)
    gate_ref[...] = jnp.dot(
        spread, inner_ref[...].reshape(2 * width, channels), preferred_element_type=F32
    ).astype(BF16)


def scan_kernel(
    prompts,
    len_ref,
    own_ref,
    other_ref,
    mixed_ref,
    gate_ref,
    step_weight_ref,
    step_bias_ref,
    rate_ref,
    skip_ref,
    early_ref,
    square_ref,
    gated_ref,
    sums_ref,
    payload_ref,
    decay_ref,
    input_ref,
    partial_ref,
    in_map_ref,
    out_map_ref,
    begin_ref,
    final_ref,
):
    rows, channels = mixed_ref.shape
    blocks = rows // BLOCK
    starts, ends = bounds(len_ref, prompts)
    projected = own_ref[...] + other_ref[...]
    low = projected[:DT_RANK, :].T.astype(BF16)
    pre = jnp.dot(low, step_weight_ref[...], preferred_element_type=F32) + step_bias_ref[...]
    step = jnp.maximum(pre, 0.0) + jnp.log1p(jnp.exp(-jnp.abs(pre)))
    position = lax.broadcasted_iota(jnp.int32, (rows, 1), 0)
    is_first = position == 0
    for p in range(1, prompts):
        is_first = is_first | (position == starts[p])
    decay_ref[...] = jnp.where(is_first, RESET, step)
    input_ref[...] = step * mixed_ref[...].astype(F32)
    for block in range(blocks):
        columns = slice(block * BLOCK, (block + 1) * BLOCK)
        in_map_ref[block, :, 0:BLOCK] = projected[DT_RANK : DT_RANK + STATE, columns]
        out_map_ref[block, :, 0:BLOCK] = projected[DT_RANK + STATE :, columns]
    rate = rate_ref[...] * (-math.log2(math.e))

    def advance(state, block, index):
        at = pl.multiple_of(block * BLOCK, BLOCK) + index
        decay = jnp.exp2(decay_ref[pl.ds(at, 1), :] * rate)
        entering = in_map_ref[block, :, index : index + 1] * input_ref[pl.ds(at, 1), :]
        return state * decay + entering

    def step_block(block, state):
        begin_ref[block] = state
        for index in range(BLOCK):
            state = advance(state, block, index)
            leaving = out_map_ref[block, :, index : index + 1] * state
            at = pl.multiple_of(block * BLOCK * 8, BLOCK * 8) + 8 * index
            half = leaving[:8, :] + leaving[8:, :]
            for tile in range(channels // LANES):
                partial_ref[tile, pl.ds(at, 8), :] = half[:, tile * LANES : (tile + 1) * LANES]
        return state

    state = lax.fori_loop(0, blocks, step_block, jnp.zeros((STATE, channels), F32))
    for p in range(prompts):
        if p < prompts - 1:
            last = ends[p] - 1
            block = last // BLOCK
            final_ref[...] = begin_ref[block]

            def again(index, _, block=block):
                at = block * BLOCK + index
                decay = jnp.exp2(decay_ref[pl.ds(at, 1), :] * rate)
                lane = lax.broadcasted_iota(jnp.int32, (STATE, LANES), 1)
                column = jnp.sum(
                    jnp.where(lane == index, in_map_ref[block], 0.0), axis=1, keepdims=True
                )
                entering = column * input_ref[pl.ds(at, 1), :]
                final_ref[...] = final_ref[...] * decay + entering
                return 0

            lax.fori_loop(0, last - block * BLOCK + 1, again, 0)
            final = final_ref[...].astype(BF16)
        else:
            final = state.astype(BF16)
        for tile in range(channels // LANES):
            at = (p * (channels // LANES) + tile) * STATE
            payload_ref[at : at + STATE, :] = final[:, tile * LANES : (tile + 1) * LANES]
    base = prompts * channels // LANES * STATE
    payload_ref[base:, :] = early_ref[...]
    scanned = []
    for tile in range(channels // LANES):
        total = partial_ref[tile, pl.ds(0, rows, stride=8), :]
        for index in range(1, 8):
            total = total + partial_ref[tile, pl.ds(index, rows, stride=8), :]
        scanned.append(total)
    scanned = jnp.concatenate(scanned, axis=1)
    gate = gate_ref[...].astype(F32)
    gated = (scanned + skip_ref[...] * mixed_ref[...].astype(F32)) * (gate * sigmoid(gate))
    gated_ref[...] = gated
    ones = jnp.ones((8, channels), BF16)
    sums_ref[0:1, :] = square_ref[0:1, :]
    sums_ref[1:2, :] = dot_nt(ones, (gated * gated).astype(BF16))[0:1, :]


def join_kernel(held_ref, new_ref, own_ref, other_ref, joined_ref, sums_ref):
    count = held_ref.shape[0]
    joined_ref[:count] = held_ref[...]
    joined_ref[count:] = new_ref[...]
    sums_ref[...] = own_ref[...] + other_ref[...]


def norm_kernel(
    attended_ref,
    gated_ref,
    sums_ref,
    attention_gain_ref,
    mamba_gain_ref,
    attention_ref,
    mamba_ref,
):
    sums = sums_ref[...]
    sums = jnp.concatenate([sums, jnp.zeros((6, sums.shape[1]), F32)], axis=0).T
    attention_scale = lax.rsqrt(sums[:, 0:1] / (HEADS * HEAD_DIM) + EPSILON)
    attention_ref[...] = (attended_ref[...] * attention_scale * attention_gain_ref[...]).astype(
        BF16
    )
    mamba_scale = lax.rsqrt(sums[:, 1:2] / INNER + EPSILON)
    mamba_ref[...] = (gated_ref[...] * mamba_scale * mamba_gain_ref[...]).astype(BF16)


def one_hot(hit):
    return jnp.where(hit, 1.0, 0.0).astype(BF16)


def deliver_kernel(
    prompts,
    me_ref,
    held_ref,
    new_ref,
    keyval_hbm,
    state_hbm,
    conv_hbm,
    keyval_ref,
    state_ref,
    conv_ref,
    sems,
):
    me = me_ref[0]
    slots, _, channels = state_ref.shape
    tiles = channels // LANES
    half = held_ref.shape[0]
    sources = 2 * half
    window_at = prompts * tiles * STATE
    tail_at = window_at + prompts * WINDOW
    table_at = tail_at + 8 * tiles
    owners = held_ref.shape[1] - table_at

    def rows_of(source, at, size):
        ref, index = (held_ref, source) if source < half else (new_ref, source - half)
        return ref[index, at : at + size, :]

    owner = lax.broadcasted_iota(jnp.int32, (owners, LANES), 0)
    pick = jnp.zeros((1, LANES), F32)
    for source in range(sources):
        filled = rows_of(source, table_at, owners).astype(F32)
        filled = jnp.sum(jnp.where(owner == me, filled, 0.0), axis=0, keepdims=True)
        pick = pick + jnp.where(filled > 0.5, filled + float(source * prompts - 1), 0.0)
    pick = pick.astype(jnp.int32)

    chunk = min(sources, 8)
    picked_rows = slots * STATE
    row = lax.broadcasted_iota(jnp.int32, (picked_rows, LANES), 0)
    lane = lax.broadcasted_iota(jnp.int32, (picked_rows, LANES), 1)
    spread = one_hot(row // STATE == lane)
    span = chunk * prompts * STATE
    row = lax.broadcasted_iota(jnp.int32, (picked_rows, span), 0)
    lane = lax.broadcasted_iota(jnp.int32, (picked_rows, span), 1)
    same = row % STATE == lane % STATE
    states, windows, tails = None, None, None
    wide = -(-slots // 16) * 16
    row = lax.broadcasted_iota(jnp.int32, (wide, LANES), 0)
    lane = lax.broadcasted_iota(jnp.int32, (wide, LANES), 1)
    unit = one_hot(row == lane)
    depth = CONV - 1
    for first in range(0, sources, chunk):
        wanted = lax.broadcasted_iota(jnp.int32, (span, LANES), 0) // STATE + first * prompts
        take = dot_nt(spread, one_hot(wanted == pick))
        take = jnp.where(same, take, 0.0).astype(BF16)
        table = []
        for source in range(first, first + chunk):
            for p in range(prompts):
                at = p * tiles * STATE
                table.append(
                    jnp.concatenate(
                        [
                            rows_of(source, at + tile * STATE, STATE)
                            for tile in range(tiles)
                        ],
                        axis=1,
                    )
                )
        part = jnp.dot(take, jnp.concatenate(table, axis=0), preferred_element_type=F32)
        states = part if states is None else states + part
        table = []
        for source in range(first, first + chunk):
            for p in range(prompts):
                at = window_at + p * WINDOW
                table.append(
                    jnp.concatenate(
                        [
                            rows_of(source, at, WINDOW // 2),
                            rows_of(source, at + WINDOW // 2, WINDOW // 2),
                        ],
                        axis=1,
                    )
                )
        part = jnp.dot(take, jnp.concatenate(table, axis=0), preferred_element_type=F32)
        windows = part if windows is None else windows + part
        table = []
        for source in range(first, first + chunk):
            table.append(
                jnp.concatenate(
                    [rows_of(source, tail_at + 8 * tile, 16) for tile in range(0, tiles, 2)],
                    axis=1,
                )
            )
        span_rows = chunk * 16
        row = lax.broadcasted_iota(jnp.int32, (span_rows, LANES), 0)
        local = pick - first * prompts
        base = (local // prompts) * 16 + (local % prompts) * depth
        hits = [one_hot(row == base + 8 * odd + tap) for odd in (0, 1) for tap in range(depth)]
        hits = dot_nt(unit, jnp.concatenate(hits, axis=0)).astype(BF16)
        hits = jnp.concatenate(
            [hits[:, i * span_rows : (i + 1) * span_rows] for i in range(2 * depth)], axis=0
        )
        part = jnp.dot(hits, jnp.concatenate(table, axis=0), preferred_element_type=F32)
        tails = part if tails is None else tails + part

    state_ref[...] = states.astype(BF16).reshape(slots, STATE, channels)
    state_copy = pltpu.make_async_copy(state_ref, state_hbm, sems.at[0])
    state_copy.start()
    windows = windows.astype(BF16).reshape(slots, WINDOW // 2, 2 * LANES)
    for upper in range(2):
        for kind in range(2):
            at = upper * LANES + kind * HEAD_DIM
            keyval_ref[:, kind, upper * WINDOW // 2 : (upper + 1) * WINDOW // 2, :] = windows[
                :, :, at : at + HEAD_DIM
            ]
    keyval_copy = pltpu.make_async_copy(keyval_ref, keyval_hbm, sems.at[1])
    keyval_copy.start()
    for odd in range(2):
        for tap in range(depth):
            at = (odd * depth + tap) * wide
            for pair in range(tiles // 2):
                tile = 2 * pair + odd
                conv_ref[tap, :, tile * LANES : (tile + 1) * LANES] = tails[
                    at : at + slots, pair * LANES : (pair + 1) * LANES
                ].astype(BF16)
    conv_copy = pltpu.make_async_copy(conv_ref, conv_hbm, sems.at[2])
    conv_copy.start()
    state_copy.wait()
    keyval_copy.wait()
    conv_copy.wait()


def on_device(
    pr_size,
    tp_size,
    tokens,
    prompt_lengths,
    query_weight,
    key_weight,
    value_weight,
    attention_gain,
    inner_weight,
    conv_weight,
    scan_weight,
    step_weight,
    step_bias,
    mamba_rate,
    mamba_skip,
    mamba_gain,
    request_prompt,
    request_owner,
    request_slot,
):
    rows, width = tokens.shape
    prompts = prompt_lengths.shape[1]
    channels = inner_weight.shape[2]
    features = query_weight.shape[1]
    slots = request_owner.shape[0]
    tiles = channels // LANES

    def shape(dims, dtype=F32):
        return jax.ShapeDtypeStruct(dims, dtype)

    partial, mixed, tail = pl.pallas_call(
        functools.partial(mix_kernel, prompts),
        out_shape=(
            shape((DT_RANK + 2 * STATE, rows)),
            shape((rows, channels), BF16),
            shape((8, channels)),
        ),
        in_specs=[HBM] * 5,
        out_specs=(VMEM, VMEM, VMEM),
        scratch_shapes=[
            pltpu.SMEM((1, prompts), jnp.int32),
            pltpu.VMEM((rows, width), BF16),
            pltpu.VMEM((width, 2, channels), BF16),
            pltpu.VMEM(conv_weight.shape, F32),
            pltpu.VMEM(scan_weight.shape[::-1], BF16),
            pltpu.VMEM((rows + 8, channels), F32),
            pltpu.SemaphoreType.DMA((5,)),
        ],
        compiler_params=params(24),
        name="mix",
    )(prompt_lengths, tokens, inner_weight, conv_weight, scan_weight.T)

    def swap(x, axis, size, bit):
        return lax.ppermute(x, axis, [(i, i ^ bit) for i in range(size)])

    near = swap(partial, "tp", tp_size, 1)
    owners = -(-pr_size // 16) * 16
    early_rows = prompts * WINDOW + 8 * tiles + owners
    attended, square, gate, early = pl.pallas_call(
        functools.partial(attend_kernel, prompts),
        out_shape=(
            shape((rows, features)),
            shape((8, rows)),
            shape((rows, channels), BF16),
            shape((early_rows, LANES), BF16),
        ),
        in_specs=[SMEM, VMEM, VMEM, VMEM, VMEM, ANY, VMEM, VMEM, VMEM, VMEM],
        out_specs=(VMEM, VMEM, VMEM, VMEM),
        scratch_shapes=[
            pltpu.VMEM((width, 2, channels), BF16),
            pltpu.VMEM((8, LANES), jnp.int32),
            pltpu.SemaphoreType.DMA,
        ],
        compiler_params=params(32),
        cost_estimate=pl.CostEstimate(
            flops=2 * rows * width * (features + channels), bytes_accessed=4 << 20, transcendentals=0
        ),
        name="attend",
    )(
        prompt_lengths,
        tokens,
        query_weight,
        key_weight.T,
        value_weight.T,
        inner_weight,
        tail,
        request_prompt[None],
        request_owner[None],
        request_slot[None],
    )
    pair = partial + near
    bit = 2
    while bit < tp_size // 2:
        pair = pair + swap(pair, "tp", tp_size, bit)
        bit *= 2
    far = swap(pair, "tp", tp_size, bit)

    payload_rows = prompts * tiles * STATE + early_rows
    gated, sums, payload = pl.pallas_call(
        functools.partial(scan_kernel, prompts),
        out_shape=(
            shape((rows, channels)),
            shape((2, rows)),
            shape((payload_rows, LANES), BF16),
        ),
        in_specs=[SMEM] + [VMEM] * 10,
        out_specs=(VMEM, VMEM, VMEM),
        scratch_shapes=[
            pltpu.VMEM((rows, channels), F32),
            pltpu.VMEM((rows, channels), F32),
            pltpu.VMEM((tiles, rows * 8, LANES), F32),
            pltpu.VMEM((rows // BLOCK, STATE, LANES), F32),
            pltpu.VMEM((rows // BLOCK, STATE, LANES), F32),
            pltpu.VMEM((rows // BLOCK, STATE, channels), F32),
            pltpu.VMEM((STATE, channels), F32),
        ],
        compiler_params=params(32),
        name="scan",
    )(
        prompt_lengths,
        pair,
        far,
        mixed,
        gate,
        step_weight,
        step_bias[None],
        mamba_rate,
        mamba_skip[None],
        early,
        square,
    )

    me = lax.axis_index("pr").astype(jnp.int32)
    held = payload[None]
    pr_bits = [1 << i for i in reversed(range((pr_size - 1).bit_length()))]
    tp_bits = [1 << i for i in range((tp_size - 1).bit_length())]
    for index in range(max(len(pr_bits) - 1, len(tp_bits))):
        new = swap(held, "pr", pr_size, pr_bits[index]) if index < len(pr_bits) - 1 else None
        other = swap(sums, "tp", tp_size, tp_bits[index]) if index < len(tp_bits) else None
        if new is None:
            sums = sums + other
        elif other is None:
            held = jnp.concatenate([held, new], axis=0)
        else:
            held, sums = pl.pallas_call(
                join_kernel,
                out_shape=(
                    shape((2 * held.shape[0],) + held.shape[1:], BF16),
                    shape(sums.shape),
                ),
                in_specs=[VMEM] * 4,
                out_specs=(VMEM, VMEM),
                compiler_params=params(16),
                name="join",
            )(held, new, sums, other)
    new = swap(held, "pr", pr_size, pr_bits[-1])
    attention_out, mamba_out = pl.pallas_call(
        norm_kernel,
        out_shape=(shape((rows, features), BF16), shape((rows, channels), BF16)),
        in_specs=[VMEM] * 5,
        out_specs=(VMEM, VMEM),
        compiler_params=params(16),
        cost_estimate=pl.CostEstimate(flops=1 << 24, bytes_accessed=2 << 20, transcendentals=0),
        name="norm",
    )(attended, gated, sums, attention_gain[None], mamba_gain[None])
    keyval, state, conv = pl.pallas_call(
        functools.partial(deliver_kernel, prompts),
        out_shape=(
            shape((slots, 2, WINDOW, HEAD_DIM), BF16),
            shape((slots, STATE, channels), BF16),
            shape((CONV - 1, slots, channels), BF16),
        ),
        in_specs=[SMEM, VMEM, VMEM],
        out_specs=(HBM, HBM, HBM),
        scratch_shapes=[
            pltpu.VMEM((slots, 2, WINDOW, HEAD_DIM), BF16),
            pltpu.VMEM((slots, STATE, channels), BF16),
            pltpu.VMEM((CONV - 1, slots, channels), BF16),
            pltpu.SemaphoreType.DMA((3,)),
        ],
        compiler_params=params(32),
        name="deliver",
    )(me[None], held, new)
    return (attention_out, mamba_out, keyval, state, conv.transpose(1, 0, 2))


def solution(mesh):
    return jax.shard_map(
        functools.partial(on_device, mesh.shape["pr"], mesh.shape["tp"]),
        mesh=mesh,
        in_specs=(
            P("pr", None),
            P("pr", None),
            P(None, "tp"),
            P(None, "tp"),
            P(None, "tp"),
            P("tp"),
            P(None, None, "tp"),
            P(None, "tp"),
            P("tp", None),
            P(None, "tp"),
            P("tp"),
            P(None, "tp"),
            P("tp"),
            P("tp"),
            P("pr"),
            P("pr"),
            P("pr"),
        ),
        out_specs=(
            P("pr", "tp"),
            P("pr", "tp"),
            P("pr", None, None, "tp"),
            P("pr", None, "tp"),
            P("pr", None, "tp"),
        ),
        check_vma=False,
    )
```

```python
import functools
import math

import jax
import jax.numpy as jnp
from jax import lax
from jax.experimental import pallas as pl
from jax.experimental.pallas import tpu as pltpu
from jax.sharding import PartitionSpec as P

HEADS = 16
KV_HEADS = 4
HEAD_DIM = 64
INNER = 2048
STATE = 16
DT_RANK = 64
CONV = 4
WINDOW = 32
EPSILON = 1e-06
LANES = 128
BLOCK = 16
RESET = 1e30

F32 = jnp.float32
BF16 = jnp.bfloat16
VMEM = pl.BlockSpec(memory_space=pltpu.VMEM)
SMEM = pl.BlockSpec(memory_space=pltpu.SMEM)
HBM = pl.BlockSpec(memory_space=pltpu.HBM)


def params(mib):
    return pltpu.CompilerParams(vmem_limit_bytes=mib << 20)


def dot_nt(a, b):
    return lax.dot_general(a, b, (((1,), (1,)), ((), ())), preferred_element_type=F32)


def bounds(len_ref, prompts):
    starts, ends = [], []
    at = 0
    for p in range(prompts):
        starts.append(at)
        at = at + len_ref[0, p]
        ends.append(at)
    return starts, ends


def first_row_of(position, starts, prompts):
    first = jnp.zeros_like(position)
    for p in range(1, prompts):
        first = jnp.where(position >= starts[p], starts[p], first)
    return first


def last_rows(shape, depth, starts, ends):
    row = lax.broadcasted_iota(jnp.int32, shape, 0)
    position = lax.broadcasted_iota(jnp.int32, shape, 1)
    hit = jnp.zeros(shape, F32)
    for p in range(len(starts)):
        here = (row >= p * depth) & (row < (p + 1) * depth) & (position >= starts[p])
        hit = jnp.where(here & (position - row == ends[p] - (p + 1) * depth), 1.0, hit)
    return hit.astype(BF16)


def sigmoid(x):
    return 0.5 * jnp.tanh(0.5 * x) + 0.5


def mix_kernel(
    prompts,
    len_ref,
    inner_ref,
    conv_ref,
    scan_ref,
    partial_ref,
    mixed_ref,
    tail_ref,
    raw_ref,
):
    _, rows, channels = inner_ref.shape
    starts, ends = bounds(len_ref, prompts)
    raw = inner_ref[0].astype(F32)
    raw_ref[pl.ds(0, 8), :] = jnp.zeros((8, channels), F32)
    raw_ref[pl.ds(8, rows), :] = raw
    position = lax.broadcasted_iota(jnp.int32, (rows, 1), 0)
    offset = position - first_row_of(position, starts, prompts)
    total = raw * conv_ref[CONV - 1 : CONV, :]
    for lag in range(1, CONV):
        shifted = raw_ref[pl.ds(8 - lag, rows), :]
        shifted = jnp.where(offset >= lag, shifted, 0.0)
        total = total + shifted * conv_ref[CONV - 1 - lag : CONV - lag, :]
    mixed = (total * sigmoid(total)).astype(BF16)
    mixed_ref[...] = mixed
    partial_ref[...] = dot_nt(scan_ref[...], mixed)
    pick = last_rows((8, rows), CONV - 1, starts, ends)
    tail_ref[...] = jnp.dot(pick, inner_ref[0], preferred_element_type=F32)


def attend_kernel(
    prompts,
    len_ref,
    tokens_ref,
    query_ref,
    key_ref,
    value_ref,
    tail_ref,
    prompt_ref,
    owner_ref,
    slot_ref,
    attended_ref,
    square_ref,
    packed_ref,
    request_ref,
):
    rows, width = tokens_ref.shape
    channels = tail_ref.shape[1]
    features = query_ref.shape[1]
    group = features // HEAD_DIM
    starts, ends = bounds(len_ref, prompts)
    tokens = tokens_ref[...]
    queries = jnp.dot(tokens, query_ref[...], preferred_element_type=F32).astype(BF16)
    keys = dot_nt(tokens, jnp.concatenate([key_ref[...]] * group, axis=0)).astype(BF16)
    values = dot_nt(tokens, jnp.concatenate([value_ref[...]] * group, axis=0)).astype(BF16)
    at_row = lax.broadcasted_iota(jnp.int32, (rows, rows), 0)
    at_column = lax.broadcasted_iota(jnp.int32, (rows, rows), 1)
    row_first = first_row_of(at_row, starts, prompts)
    allowed = (at_column <= at_row) & (at_row - at_column < WINDOW) & (at_column >= row_first)
    head_of = lax.broadcasted_iota(jnp.int32, (rows, features), 1) // HEAD_DIM
    zero = jnp.zeros((), BF16)
    attended = jnp.zeros((rows, features), F32)
    for head in range(group):
        mine = head_of == head
        scores = dot_nt(queries, jnp.where(mine, keys, zero)) * HEAD_DIM ** (-0.5)
        scores = jnp.where(allowed, scores, -1e30)
        top = jnp.max(scores, axis=1, keepdims=True)
        expons = jnp.exp(scores - top)
        weights = expons * (1.0 / jnp.sum(expons, axis=1, keepdims=True))
        attended = attended + jnp.dot(
            weights.astype(BF16), jnp.where(mine, values, zero), preferred_element_type=F32
        )
    attended_ref[...] = attended
    ones = jnp.ones((8, features), BF16)
    square_ref[...] = dot_nt(ones, (attended * attended).astype(BF16))
    lane = lax.broadcasted_iota(jnp.int32, (rows, LANES), 1)
    both = jnp.where(lane < HEAD_DIM, keys[:, :LANES], values[:, :LANES])
    pick = last_rows((prompts * WINDOW, rows), WINDOW, starts, ends)
    packed_ref[: prompts * WINDOW, :] = jnp.dot(pick, both, preferred_element_type=F32).astype(
        BF16
    )
    requests = owner_ref.shape[1]
    request_ref[...] = jnp.full(request_ref.shape, -1, jnp.int32)
    request_ref[0:1, 0:requests] = owner_ref[...]
    request_ref[1:2, 0:requests] = slot_ref[...]
    request_ref[2:3, 0:requests] = prompt_ref[...]
    owners = packed_ref.shape[0] - prompts * WINDOW - 8 * (channels // LANES)
    owner = lax.broadcasted_iota(jnp.int32, (owners, LANES), 0) == request_ref[0:1, :]
    slot = lax.broadcasted_iota(jnp.int32, (LANES, LANES), 0) == request_ref[1:2, :]
    number = request_ref[2:3, :] + 1
    filled = dot_nt(
        jnp.where(owner, 1.0, 0.0).astype(BF16),
        jnp.where(slot, number, 0).astype(F32).astype(BF16),
    )
    base = prompts * WINDOW
    for tile in range(0, channels // LANES, 2):
        packed_ref[base + 8 * tile : base + 8 * (tile + 2), :] = jnp.concatenate(
            [
                tail_ref[:, tile * LANES : (tile + 1) * LANES],
                tail_ref[:, (tile + 1) * LANES : (tile + 2) * LANES],
            ],
            axis=0,
        ).astype(BF16)
    packed_ref[base + 8 * (channels // LANES) :, :] = filled.astype(BF16)


def scan_kernel(
    prompts,
    len_ref,
    own_ref,
    other_ref,
    mixed_ref,
    gate_ref,
    step_weight_ref,
    step_bias_ref,
    rate_ref,
    skip_ref,
    early_ref,
    square_ref,
    gated_ref,
    sums_ref,
    payload_ref,
    decay_ref,
    input_ref,
    partial_ref,
    in_map_ref,
    out_map_ref,
    begin_ref,
    final_ref,
):
    rows, channels = mixed_ref.shape
    blocks = rows // BLOCK
    starts, ends = bounds(len_ref, prompts)
    projected = own_ref[...] + other_ref[...]
    low = projected[:DT_RANK, :].T.astype(BF16)
    pre = jnp.dot(low, step_weight_ref[...], preferred_element_type=F32) + step_bias_ref[...]
    step = jnp.maximum(pre, 0.0) + jnp.log1p(jnp.exp(-jnp.abs(pre)))
    position = lax.broadcasted_iota(jnp.int32, (rows, 1), 0)
    is_first = position == 0
    for p in range(1, prompts):
        is_first = is_first | (position == starts[p])
    decay_ref[...] = jnp.where(is_first, RESET, step)
    input_ref[...] = step * mixed_ref[...].astype(F32)
    for block in range(blocks):
        columns = slice(block * BLOCK, (block + 1) * BLOCK)
        in_map_ref[block, :, 0:BLOCK] = projected[DT_RANK : DT_RANK + STATE, columns]
        out_map_ref[block, :, 0:BLOCK] = projected[DT_RANK + STATE :, columns]
    rate = rate_ref[...] * (-math.log2(math.e))

    def advance(state, block, index):
        at = pl.multiple_of(block * BLOCK, BLOCK) + index
        decay = jnp.exp2(decay_ref[pl.ds(at, 1), :] * rate)
        entering = in_map_ref[block, :, index : index + 1] * input_ref[pl.ds(at, 1), :]
        return state * decay + entering

    def step_block(block, state):
        begin_ref[block] = state
        for index in range(BLOCK):
            state = advance(state, block, index)
            leaving = out_map_ref[block, :, index : index + 1] * state
            at = pl.multiple_of(block * BLOCK * 8, BLOCK * 8) + 8 * index
            half = leaving[:8, :] + leaving[8:, :]
            for tile in range(channels // LANES):
                partial_ref[tile, pl.ds(at, 8), :] = half[:, tile * LANES : (tile + 1) * LANES]
        return state

    state = lax.fori_loop(0, blocks, step_block, jnp.zeros((STATE, channels), F32))
    for p in range(prompts):
        if p < prompts - 1:
            last = ends[p] - 1
            block = last // BLOCK
            final_ref[...] = begin_ref[block]

            def again(index, _, block=block):
                at = block * BLOCK + index
                decay = jnp.exp2(decay_ref[pl.ds(at, 1), :] * rate)
                lane = lax.broadcasted_iota(jnp.int32, (STATE, LANES), 1)
                column = jnp.sum(
                    jnp.where(lane == index, in_map_ref[block], 0.0), axis=1, keepdims=True
                )
                entering = column * input_ref[pl.ds(at, 1), :]
                final_ref[...] = final_ref[...] * decay + entering
                return 0

            lax.fori_loop(0, last - block * BLOCK + 1, again, 0)
            final = final_ref[...].astype(BF16)
        else:
            final = state.astype(BF16)
        for tile in range(channels // LANES):
            at = (p * (channels // LANES) + tile) * STATE
            payload_ref[at : at + STATE, :] = final[:, tile * LANES : (tile + 1) * LANES]
    base = prompts * channels // LANES * STATE
    payload_ref[base:, :] = early_ref[...]
    scanned = []
    for tile in range(channels // LANES):
        total = partial_ref[tile, pl.ds(0, rows, stride=8), :]
        for index in range(1, 8):
            total = total + partial_ref[tile, pl.ds(index, rows, stride=8), :]
        scanned.append(total)
    scanned = jnp.concatenate(scanned, axis=1)
    gate = gate_ref[1].astype(F32)
    gated = (scanned + skip_ref[...] * mixed_ref[...].astype(F32)) * (gate * sigmoid(gate))
    gated_ref[...] = gated
    ones = jnp.ones((8, channels), BF16)
    sums_ref[0:1, :] = square_ref[0:1, :]
    sums_ref[1:2, :] = dot_nt(ones, (gated * gated).astype(BF16))[0:1, :]


def join_kernel(held_ref, new_ref, own_ref, other_ref, *refs):
    across_refs, (joined_ref, fresh_ref, sums_ref, crossed_ref) = refs[:-4], refs[-4:]
    count = held_ref.shape[0]
    joined_ref[:count] = held_ref[...]
    joined_ref[count:] = new_ref[...]
    fresh_ref[...] = new_ref[...]
    sums_ref[...] = own_ref[...] + other_ref[...]
    at = 0
    for across_ref in across_refs:
        crossed_ref[at : at + across_ref.shape[0]] = across_ref[...]
        at += across_ref.shape[0]


def norm_kernel(
    attended_ref,
    gated_ref,
    sums_ref,
    attention_gain_ref,
    mamba_gain_ref,
    attention_ref,
    mamba_ref,
):
    sums = sums_ref[...]
    sums = jnp.concatenate([sums, jnp.zeros((6, sums.shape[1]), F32)], axis=0).T
    attention_scale = lax.rsqrt(sums[:, 0:1] / (HEADS * HEAD_DIM) + EPSILON)
    attention_ref[...] = (attended_ref[...] * attention_scale * attention_gain_ref[...]).astype(
        BF16
    )
    mamba_scale = lax.rsqrt(sums[:, 1:2] / INNER + EPSILON)
    mamba_ref[...] = (gated_ref[...] * mamba_scale * mamba_gain_ref[...]).astype(BF16)


def one_hot(hit):
    return jnp.where(hit, 1.0, 0.0).astype(BF16)


def deliver_kernel(
    prompts,
    pieces,
    me_ref,
    *refs,
):
    keyval_hbm, state_hbm, conv_hbm, keyval_ref, state_ref, conv_ref, sems = refs[pieces:]
    me = me_ref[0]
    slots, _, channels = state_ref.shape
    tiles = channels // LANES
    blocks = [(ref, index) for ref in refs[:pieces] for index in range(ref.shape[0])]
    sources = len(blocks)
    window_at = prompts * tiles * STATE
    tail_at = window_at + prompts * WINDOW
    table_at = tail_at + 8 * tiles
    owners = refs[0].shape[1] - table_at

    def rows_of(source, at, size):
        ref, index = blocks[source]
        return ref[index, at : at + size, :]

    owner = lax.broadcasted_iota(jnp.int32, (owners, LANES), 0)
    pick = jnp.zeros((1, LANES), F32)
    for source in range(sources):
        filled = rows_of(source, table_at, owners).astype(F32)
        filled = jnp.sum(jnp.where(owner == me, filled, 0.0), axis=0, keepdims=True)
        pick = pick + jnp.where(filled > 0.5, filled + float(source * prompts - 1), 0.0)
    pick = pick.astype(jnp.int32)

    chunk = min(sources, 8)
    picked_rows = slots * STATE
    row = lax.broadcasted_iota(jnp.int32, (picked_rows, LANES), 0)
    lane = lax.broadcasted_iota(jnp.int32, (picked_rows, LANES), 1)
    spread = one_hot(row // STATE == lane)
    span = chunk * prompts * STATE
    row = lax.broadcasted_iota(jnp.int32, (picked_rows, span), 0)
    lane = lax.broadcasted_iota(jnp.int32, (picked_rows, span), 1)
    same = row % STATE == lane % STATE
    states, windows, tails = None, None, None
    wide = -(-slots // 16) * 16
    row = lax.broadcasted_iota(jnp.int32, (wide, LANES), 0)
    lane = lax.broadcasted_iota(jnp.int32, (wide, LANES), 1)
    unit = one_hot(row == lane)
    depth = CONV - 1
    for first in range(0, sources, chunk):
        wanted = lax.broadcasted_iota(jnp.int32, (span, LANES), 0) // STATE + first * prompts
        take = dot_nt(spread, one_hot(wanted == pick))
        take = jnp.where(same, take, 0.0).astype(BF16)
        table = []
        for source in range(first, first + chunk):
            for p in range(prompts):
                at = p * tiles * STATE
                table.append(
                    jnp.concatenate(
                        [
                            rows_of(source, at + tile * STATE, STATE)
                            for tile in range(tiles)
                        ],
                        axis=1,
                    )
                )
        part = jnp.dot(take, jnp.concatenate(table, axis=0), preferred_element_type=F32)
        states = part if states is None else states + part
        table = []
        for source in range(first, first + chunk):
            for p in range(prompts):
                at = window_at + p * WINDOW
                table.append(
                    jnp.concatenate(
                        [
                            rows_of(source, at, WINDOW // 2),
                            rows_of(source, at + WINDOW // 2, WINDOW // 2),
                        ],
                        axis=1,
                    )
                )
        part = jnp.dot(take, jnp.concatenate(table, axis=0), preferred_element_type=F32)
        windows = part if windows is None else windows + part
        table = []
        for source in range(first, first + chunk):
            table.append(
                jnp.concatenate(
                    [rows_of(source, tail_at + 8 * tile, 16) for tile in range(0, tiles, 2)],
                    axis=1,
                )
            )
        span_rows = chunk * 16
        row = lax.broadcasted_iota(jnp.int32, (span_rows, LANES), 0)
        local = pick - first * prompts
        base = (local // prompts) * 16 + (local % prompts) * depth
        hits = [one_hot(row == base + 8 * odd + tap) for odd in (0, 1) for tap in range(depth)]
        hits = dot_nt(unit, jnp.concatenate(hits, axis=0)).astype(BF16)
        hits = jnp.concatenate(
            [hits[:, i * span_rows : (i + 1) * span_rows] for i in range(2 * depth)], axis=0
        )
        part = jnp.dot(hits, jnp.concatenate(table, axis=0), preferred_element_type=F32)
        tails = part if tails is None else tails + part

    state_ref[...] = states.astype(BF16).reshape(slots, STATE, channels)
    state_copy = pltpu.make_async_copy(state_ref, state_hbm, sems.at[0])
    state_copy.start()
    windows = windows.astype(BF16).reshape(slots, WINDOW // 2, 2 * LANES)
    for upper in range(2):
        for kind in range(2):
            at = upper * LANES + kind * HEAD_DIM
            keyval_ref[:, kind, upper * WINDOW // 2 : (upper + 1) * WINDOW // 2, :] = windows[
                :, :, at : at + HEAD_DIM
            ]
    keyval_copy = pltpu.make_async_copy(keyval_ref, keyval_hbm, sems.at[1])
    keyval_copy.start()
    for odd in range(2):
        for tap in range(depth):
            at = (odd * depth + tap) * wide
            for pair in range(tiles // 2):
                tile = 2 * pair + odd
                conv_ref[tap, :, tile * LANES : (tile + 1) * LANES] = tails[
                    at : at + slots, pair * LANES : (pair + 1) * LANES
                ].astype(BF16)
    conv_copy = pltpu.make_async_copy(conv_ref, conv_hbm, sems.at[2])
    conv_copy.start()
    state_copy.wait()
    keyval_copy.wait()
    conv_copy.wait()


def on_device(
    pr_size,
    tp_size,
    tokens,
    prompt_lengths,
    query_weight,
    key_weight,
    value_weight,
    attention_gain,
    inner_weight,
    conv_weight,
    scan_weight,
    step_weight,
    step_bias,
    mamba_rate,
    mamba_skip,
    mamba_gain,
    request_prompt,
    request_owner,
    request_slot,
):
    rows, width = tokens.shape
    prompts = prompt_lengths.shape[1]
    channels = inner_weight.shape[2]
    features = query_weight.shape[1]
    slots = request_owner.shape[0]
    tiles = channels // LANES

    def shape(dims, dtype=F32):
        return jax.ShapeDtypeStruct(dims, dtype)

    inner = jnp.einsum("td,dgc->gtc", tokens, inner_weight, preferred_element_type=F32)
    inner = inner.astype(BF16)
    partial, mixed, tail = pl.pallas_call(
        functools.partial(mix_kernel, prompts),
        out_shape=(
            shape((DT_RANK + 2 * STATE, rows)),
            shape((rows, channels), BF16),
            shape((8, channels)),
        ),
        in_specs=[SMEM] + [VMEM] * 3,
        out_specs=(VMEM, VMEM, VMEM),
        scratch_shapes=[pltpu.VMEM((rows + 8, channels), F32)],
        compiler_params=params(16),
        name="mix",
    )(prompt_lengths, inner, conv_weight, scan_weight.T)

    def swap(x, axis, size, bit):
        return lax.ppermute(x, axis, [(i, i ^ bit) for i in range(size)])

    near = swap(partial, "tp", tp_size, 1)
    owners = -(-pr_size // 16) * 16
    early_rows = prompts * WINDOW + 8 * tiles + owners
    attended, square, early = pl.pallas_call(
        functools.partial(attend_kernel, prompts),
        out_shape=(
            shape((rows, features)),
            shape((8, rows)),
            shape((early_rows, LANES), BF16),
        ),
        in_specs=[SMEM] + [VMEM] * 8,
        out_specs=(VMEM, VMEM, VMEM),
        scratch_shapes=[
            pltpu.VMEM((8, LANES), jnp.int32),
        ],
        compiler_params=params(16),
        cost_estimate=pl.CostEstimate(
            flops=2 * rows * width * (features + channels), bytes_accessed=4 << 20, transcendentals=0
        ),
        name="attend",
    )(
        prompt_lengths,
        tokens,
        query_weight,
        key_weight.T,
        value_weight.T,
        tail,
        request_prompt[None],
        request_owner[None],
        request_slot[None],
    )
    pair = partial + near
    bit = 2
    while bit < tp_size // 2:
        pair = pair + swap(pair, "tp", tp_size, bit)
        bit *= 2
    far = swap(pair, "tp", tp_size, bit)

    payload_rows = prompts * tiles * STATE + early_rows
    gated, sums, payload = pl.pallas_call(
        functools.partial(scan_kernel, prompts),
        out_shape=(
            shape((rows, channels)),
            shape((2, rows)),
            shape((payload_rows, LANES), BF16),
        ),
        in_specs=[SMEM] + [VMEM] * 10,
        out_specs=(VMEM, VMEM, VMEM),
        scratch_shapes=[
            pltpu.VMEM((rows, channels), F32),
            pltpu.VMEM((rows, channels), F32),
            pltpu.VMEM((tiles, rows * 8, LANES), F32),
            pltpu.VMEM((rows // BLOCK, STATE, LANES), F32),
            pltpu.VMEM((rows // BLOCK, STATE, LANES), F32),
            pltpu.VMEM((rows // BLOCK, STATE, channels), F32),
            pltpu.VMEM((STATE, channels), F32),
        ],
        compiler_params=params(32),
        name="scan",
    )(
        prompt_lengths,
        pair,
        far,
        mixed,
        inner,
        step_weight,
        step_bias[None],
        mamba_rate,
        mamba_skip[None],
        early,
        square,
    )

    me = lax.axis_index("pr").astype(jnp.int32)
    held = payload[None]
    pr_bits = [1 << i for i in reversed(range((pr_size - 1).bit_length()))]
    tp_bits = [1 << i for i in range((tp_size - 1).bit_length())]
    fresh, crossed = held, []
    for index in range(max(len(pr_bits) - 1, len(tp_bits))):
        other = swap(sums, "tp", tp_size, tp_bits[index]) if index < len(tp_bits) else None
        if index < len(pr_bits) - 1:
            new = swap(held, "pr", pr_size, pr_bits[index])
            crossed.append(swap(fresh, "pr", pr_size, pr_bits[-1]))
            count = held.shape[0]
            held, fresh, sums, across = pl.pallas_call(
                join_kernel,
                out_shape=(
                    shape((2 * count,) + held.shape[1:], BF16),
                    shape((count,) + held.shape[1:], BF16),
                    shape(sums.shape),
                    shape((count,) + held.shape[1:], BF16),
                ),
                in_specs=[VMEM] * (4 + len(crossed)),
                out_specs=(VMEM,) * 4,
                compiler_params=params(16),
                name="join",
            )(held, new, sums, jnp.zeros_like(sums) if other is None else other, *crossed)
            crossed = [across]
        else:
            sums = sums + other
    crossed.append(swap(fresh, "pr", pr_size, pr_bits[-1]))
    pieces = [held] + crossed
    attention_out, mamba_out = pl.pallas_call(
        norm_kernel,
        out_shape=(shape((rows, features), BF16), shape((rows, channels), BF16)),
        in_specs=[VMEM] * 5,
        out_specs=(VMEM, VMEM),
        compiler_params=params(16),
        cost_estimate=pl.CostEstimate(flops=1 << 24, bytes_accessed=2 << 20, transcendentals=0),
        name="norm",
    )(attended, gated, sums, attention_gain[None], mamba_gain[None])
    keyval, state, conv = pl.pallas_call(
        functools.partial(deliver_kernel, prompts, len(pieces)),
        out_shape=(
            shape((slots, 2, WINDOW, HEAD_DIM), BF16),
            shape((slots, STATE, channels), BF16),
            shape((CONV - 1, slots, channels), BF16),
        ),
        in_specs=[SMEM] + [VMEM] * len(pieces),
        out_specs=(HBM, HBM, HBM),
        scratch_shapes=[
            pltpu.VMEM((slots, 2, WINDOW, HEAD_DIM), BF16),
            pltpu.VMEM((slots, STATE, channels), BF16),
            pltpu.VMEM((CONV - 1, slots, channels), BF16),
            pltpu.SemaphoreType.DMA((3,)),
        ],
        compiler_params=params(32),
        name="deliver",
    )(me[None], *pieces)
    return (attention_out, mamba_out, keyval, state, conv.transpose(1, 0, 2))


def solution(mesh):
    return jax.shard_map(
        functools.partial(on_device, mesh.shape["pr"], mesh.shape["tp"]),
        mesh=mesh,
        in_specs=(
            P("pr", None),
            P("pr", None),
            P(None, "tp"),
            P(None, "tp"),
            P(None, "tp"),
            P("tp"),
            P(None, None, "tp"),
            P(None, "tp"),
            P("tp", None),
            P(None, "tp"),
            P("tp"),
            P(None, "tp"),
            P("tp"),
            P("tp"),
            P("pr"),
            P("pr"),
            P("pr"),
        ),
        out_specs=(
            P("pr", "tp"),
            P("pr", "tp"),
            P("pr", None, None, "tp"),
            P("pr", None, "tp"),
            P("pr", None, "tp"),
        ),
        check_vma=False,
    )
```

```python
import functools
import math

import jax
import jax.numpy as jnp
from jax import lax
from jax.experimental import pallas as pl
from jax.experimental.pallas import tpu as pltpu
from jax.sharding import PartitionSpec as P

HEADS = 16
KV_HEADS = 4
HEAD_DIM = 64
INNER = 2048
STATE = 16
DT_RANK = 64
CONV = 4
WINDOW = 32
EPSILON = 1e-06
LANES = 128
BLOCK = 16
RESET = 1e30

F32 = jnp.float32
BF16 = jnp.bfloat16
VMEM = pl.BlockSpec(memory_space=pltpu.VMEM)
SMEM = pl.BlockSpec(memory_space=pltpu.SMEM)
HBM = pl.BlockSpec(memory_space=pltpu.HBM)


def params(mib):
    return pltpu.CompilerParams(vmem_limit_bytes=mib << 20)


def dot_nt(a, b):
    return lax.dot_general(a, b, (((1,), (1,)), ((), ())), preferred_element_type=F32)


def bounds(len_ref, prompts):
    starts, ends = [], []
    at = 0
    for p in range(prompts):
        starts.append(at)
        at = at + len_ref[0, p]
        ends.append(at)
    return starts, ends


def first_row_of(position, starts, prompts):
    first = jnp.zeros_like(position)
    for p in range(1, prompts):
        first = jnp.where(position >= starts[p], starts[p], first)
    return first


def last_rows(shape, depth, starts, ends):
    row = lax.broadcasted_iota(jnp.int32, shape, 0)
    position = lax.broadcasted_iota(jnp.int32, shape, 1)
    hit = jnp.zeros(shape, F32)
    for p in range(len(starts)):
        here = (row >= p * depth) & (row < (p + 1) * depth) & (position >= starts[p])
        hit = jnp.where(here & (position - row == ends[p] - (p + 1) * depth), 1.0, hit)
    return hit.astype(BF16)


def row_sums(squares):
    total = squares[:, :LANES]
    for at in range(LANES, squares.shape[1], LANES):
        total = total + squares[:, at : at + LANES]
    return jnp.sum(total.T, axis=0, keepdims=True)


def sigmoid(x):
    return 0.5 * jnp.tanh(0.5 * x) + 0.5


def mix_kernel(
    prompts,
    len_ref,
    inner_ref,
    conv_ref,
    scan_ref,
    partial_ref,
    mixed_ref,
    tail_ref,
    raw_ref,
):
    _, rows, channels = inner_ref.shape
    starts, ends = bounds(len_ref, prompts)
    raw = inner_ref[0].astype(F32)
    raw_ref[pl.ds(0, 8), :] = jnp.zeros((8, channels), F32)
    raw_ref[pl.ds(8, rows), :] = raw
    position = lax.broadcasted_iota(jnp.int32, (rows, 1), 0)
    offset = position - first_row_of(position, starts, prompts)
    total = raw * conv_ref[CONV - 1 : CONV, :]
    for lag in range(1, CONV):
        shifted = raw_ref[pl.ds(8 - lag, rows), :]
        shifted = jnp.where(offset >= lag, shifted, 0.0)
        total = total + shifted * conv_ref[CONV - 1 - lag : CONV - lag, :]
    mixed = (total * sigmoid(total)).astype(BF16)
    mixed_ref[...] = mixed
    partial_ref[...] = dot_nt(scan_ref[...], mixed)
    pick = last_rows((8, rows), CONV - 1, starts, ends)
    tail_ref[...] = jnp.dot(pick, inner_ref[0], preferred_element_type=F32)


def attend_kernel(
    prompts,
    len_ref,
    tokens_ref,
    query_ref,
    key_ref,
    value_ref,
    tail_ref,
    prompt_ref,
    owner_ref,
    slot_ref,
    attended_ref,
    square_ref,
    packed_ref,
    request_ref,
):
    rows, width = tokens_ref.shape
    channels = tail_ref.shape[1]
    features = query_ref.shape[1]
    group = features // HEAD_DIM
    starts, ends = bounds(len_ref, prompts)
    tokens = tokens_ref[...]
    queries = jnp.dot(tokens, query_ref[...], preferred_element_type=F32).astype(BF16)
    keys = dot_nt(tokens, jnp.concatenate([key_ref[...]] * group, axis=0)).astype(BF16)
    values = dot_nt(tokens, jnp.concatenate([value_ref[...]] * group, axis=0)).astype(BF16)
    at_row = lax.broadcasted_iota(jnp.int32, (rows, rows), 0)
    at_column = lax.broadcasted_iota(jnp.int32, (rows, rows), 1)
    row_first = first_row_of(at_row, starts, prompts)
    allowed = (at_column <= at_row) & (at_row - at_column < WINDOW) & (at_column >= row_first)
    head_of = lax.broadcasted_iota(jnp.int32, (rows, features), 1) // HEAD_DIM
    zero = jnp.zeros((), BF16)
    attended = jnp.zeros((rows, features), F32)
    for head in range(group):
        mine = head_of == head
        scores = dot_nt(queries, jnp.where(mine, keys, zero)) * HEAD_DIM ** (-0.5)
        scores = jnp.where(allowed, scores, -1e30)
        top = jnp.max(scores, axis=1, keepdims=True)
        expons = jnp.exp(scores - top)
        weights = expons * (1.0 / jnp.sum(expons, axis=1, keepdims=True))
        attended = attended + jnp.dot(
            weights.astype(BF16), jnp.where(mine, values, zero), preferred_element_type=F32
        )
    attended_ref[...] = attended
    square_ref[...] = jnp.broadcast_to(row_sums(attended * attended), square_ref.shape)
    lane = lax.broadcasted_iota(jnp.int32, (rows, LANES), 1)
    both = jnp.where(lane < HEAD_DIM, keys[:, :LANES], values[:, :LANES])
    pick = last_rows((prompts * WINDOW, rows), WINDOW, starts, ends)
    packed_ref[: prompts * WINDOW, :] = jnp.dot(pick, both, preferred_element_type=F32).astype(
        BF16
    )
    requests = owner_ref.shape[1]
    request_ref[...] = jnp.full(request_ref.shape, -1, jnp.int32)
    request_ref[0:1, 0:requests] = owner_ref[...]
    request_ref[1:2, 0:requests] = slot_ref[...]
    request_ref[2:3, 0:requests] = prompt_ref[...]
    depth = prompts * (CONV - 1)
    groups = channels // LANES // 2
    spare = 16 - 2 * depth
    owners = packed_ref.shape[0] - prompts * WINDOW - 16 * groups + spare * groups
    owner = lax.broadcasted_iota(jnp.int32, (owners, LANES), 0) == request_ref[0:1, :]
    slot = lax.broadcasted_iota(jnp.int32, (LANES, LANES), 0) == request_ref[1:2, :]
    number = request_ref[2:3, :] + 1
    filled = dot_nt(
        jnp.where(owner, 1.0, 0.0).astype(BF16),
        jnp.where(slot, number, 0).astype(F32).astype(BF16),
    )
    base = prompts * WINDOW
    for group in range(groups):
        at = 2 * group * LANES
        packed_ref[base + 16 * group : base + 16 * (group + 1), :] = jnp.concatenate(
            [
                tail_ref[:depth, at : at + LANES],
                tail_ref[:depth, at + LANES : at + 2 * LANES],
                filled[spare * group : spare * (group + 1), :],
            ],
            axis=0,
        ).astype(BF16)
    if owners > spare * groups:
        packed_ref[base + 16 * groups :, :] = filled[spare * groups :, :].astype(BF16)


def scan_kernel(
    prompts,
    len_ref,
    own_ref,
    other_ref,
    mixed_ref,
    gate_ref,
    step_weight_ref,
    step_bias_ref,
    rate_ref,
    skip_ref,
    early_ref,
    square_ref,
    gated_ref,
    sums_ref,
    payload_ref,
    decay_ref,
    input_ref,
    in_map_ref,
    out_map_ref,
    scanned_ref,
    states_even_ref,
    states_odd_ref,
):
    rows, channels = mixed_ref.shape
    span = BLOCK * STATE
    pairs = rows // BLOCK // 2
    starts, ends = bounds(len_ref, prompts)
    projected = own_ref[...] + other_ref[...].astype(F32)
    low = projected[:DT_RANK, :].T.astype(BF16)
    pre = jnp.dot(low, step_weight_ref[...], preferred_element_type=F32) + step_bias_ref[...]
    step = jnp.maximum(pre, 0.0) + jnp.log1p(jnp.exp(-jnp.abs(pre)))
    position = lax.broadcasted_iota(jnp.int32, (rows, 1), 0)
    is_first = position == 0
    for p in range(1, prompts):
        is_first = is_first | (position == starts[p])
    decay_ref[...] = jnp.where(is_first, RESET, step)
    input_ref[...] = step * mixed_ref[...].astype(F32)
    for block in range(rows // BLOCK):
        columns = slice(block * BLOCK, (block + 1) * BLOCK)
        in_map_ref[block, :, 0:BLOCK] = projected[DT_RANK : DT_RANK + STATE, columns]
    row = lax.broadcasted_iota(jnp.int32, (STATE, span), 0)
    column = lax.broadcasted_iota(jnp.int32, (STATE, span), 1)
    tiled = jnp.dot(
        projected[DT_RANK + STATE :, :].T.astype(BF16),
        jnp.where(column % STATE == row, 1.0, 0.0).astype(BF16),
        preferred_element_type=F32,
    )
    row = lax.broadcasted_iota(jnp.int32, (rows, span), 0)
    column = lax.broadcasted_iota(jnp.int32, (rows, span), 1)
    out_map_ref[...] = jnp.where(column // STATE == row % BLOCK, tiled, 0.0).astype(BF16)
    rate = rate_ref[...] * (-math.log2(math.e))

    def leave(block, states):
        at = pl.multiple_of(block * BLOCK, BLOCK)
        scanned_ref[pl.ds(at, BLOCK), :] = jnp.dot(
            out_map_ref[pl.ds(at, BLOCK), :], states, preferred_element_type=F32
        )

    def advance(block, state, states_ref, index):
        at = pl.multiple_of(block * BLOCK, BLOCK)
        for token in range(BLOCK):
            decay = jnp.exp2(decay_ref[pl.ds(at + token, 1), :] * rate)
            entering = in_map_ref[block, :, token : token + 1] * input_ref[pl.ds(at + token, 1), :]
            state = state * decay + entering
            states_ref[index, token * STATE : (token + 1) * STATE, :] = state.astype(BF16)
        return state


    def two_blocks(pair, state):
        before = jnp.maximum(pair - 1, 0)
        leave(2 * before + 1, states_odd_ref[before])
        state = advance(2 * pair, state, states_even_ref, pair)
        leave(2 * pair, states_even_ref[pair])
        return advance(2 * pair + 1, state, states_odd_ref, pair)

    lax.fori_loop(0, pairs, two_blocks, jnp.zeros((STATE, channels), F32))
    leave(2 * pairs - 1, states_odd_ref[pairs - 1])
    for p in range(prompts):
        last = ends[p] - 1
        block = last // BLOCK
        at = pl.multiple_of((last - block * BLOCK) * STATE, STATE)
        final = jnp.where(
            block % 2 == 0,
            states_even_ref[block // 2, pl.ds(at, STATE), :],
            states_odd_ref[block // 2, pl.ds(at, STATE), :],
        )
        for tile in range(channels // LANES):
            at = (p * (channels // LANES) + tile) * STATE
            payload_ref[at : at + STATE, :] = final[:, tile * LANES : (tile + 1) * LANES]
    base = prompts * channels // LANES * STATE
    payload_ref[base:, :] = early_ref[...]
    gate = gate_ref[1].astype(F32)
    gated = (scanned_ref[...] + skip_ref[...] * mixed_ref[...].astype(F32)) * (
        gate * sigmoid(gate)
    )
    gated_ref[...] = gated
    sums_ref[0:1, :] = square_ref[0:1, :]
    sums_ref[1:2, :] = row_sums(gated * gated)


def scan_call(prompts, lengths, own, other, mixed, inner, *rest):
    rows, channels = mixed.shape
    tiles = channels // LANES
    payload_rows = prompts * tiles * STATE + rest[-2].shape[0]
    return pl.pallas_call(
        functools.partial(scan_kernel, prompts),
        out_shape=(
            jax.ShapeDtypeStruct((rows, channels), F32),
            jax.ShapeDtypeStruct((2, rows), F32),
            jax.ShapeDtypeStruct((payload_rows, LANES), BF16),
        ),
        in_specs=[SMEM] + [VMEM] * 10,
        out_specs=(VMEM, VMEM, VMEM),
        scratch_shapes=[
            pltpu.VMEM((rows, channels), F32),
            pltpu.VMEM((rows, channels), F32),
            pltpu.VMEM((rows // BLOCK, STATE, LANES), F32),
            pltpu.VMEM((rows, BLOCK * STATE), BF16),
            pltpu.VMEM((rows, channels), F32),
            pltpu.VMEM((rows // BLOCK // 2, BLOCK * STATE, channels), BF16),
            pltpu.VMEM((rows // BLOCK // 2, BLOCK * STATE, channels), BF16),
        ],
        compiler_params=params(32),
        name="scan",
    )(lengths, own, other, mixed, inner, *rest)


def join_kernel(held_ref, new_ref, own_ref, other_ref, joined_ref, sums_ref):
    count = held_ref.shape[0]
    joined_ref[:count] = held_ref[...]
    joined_ref[count:] = new_ref[...]
    sums_ref[...] = own_ref[...] + other_ref[...]


def hold_kernel(new_ref, far_ref, crossed_hbm, fresh_ref, sums_ref):
    fresh_ref[...] = new_ref[...]
    sums_ref[...] = far_ref[...]


def norm_kernel(
    attended_ref,
    gated_ref,
    own_ref,
    other_ref,
    attention_gain_ref,
    mamba_gain_ref,
    attention_ref,
    mamba_ref,
):
    sums = own_ref[...] + other_ref[...]
    sums = jnp.concatenate([sums, jnp.zeros((6, sums.shape[1]), F32)], axis=0).T
    attention_scale = lax.rsqrt(sums[:, 0:1] / (HEADS * HEAD_DIM) + EPSILON)
    attention_ref[...] = (attended_ref[...] * attention_scale * attention_gain_ref[...]).astype(
        BF16
    )
    mamba_scale = lax.rsqrt(sums[:, 1:2] / INNER + EPSILON)
    mamba_ref[...] = (gated_ref[...] * mamba_scale * mamba_gain_ref[...]).astype(BF16)


def one_hot(hit):
    return jnp.where(hit, 1.0, 0.0).astype(BF16)


def deliver_kernel(
    prompts,
    pieces,
    me_ref,
    *refs,
):
    keyval_hbm, state_hbm, conv_hbm, keyval_ref, state_ref, conv_ref, sems = refs[pieces:]
    me = me_ref[0]
    slots, _, channels = state_ref.shape
    tiles = channels // LANES
    blocks = [(ref, index) for ref in refs[:pieces] for index in range(ref.shape[0])]
    sources = len(blocks)
    window_at = prompts * tiles * STATE
    tail_at = window_at + prompts * WINDOW
    depth = CONV - 1
    spare = 16 - 2 * prompts * depth
    table_rows = refs[0].shape[1] - tail_at

    def rows_of(source, at, size):
        ref, index = blocks[source]
        return ref[index, at : at + size, :]

    row = lax.broadcasted_iota(jnp.int32, (table_rows, LANES), 0)
    grouped = row < 8 * tiles
    owner = jnp.where(
        grouped, row // 16 * spare + row % 16 - (16 - spare), row - 8 * tiles + spare * (tiles // 2)
    )
    owner = jnp.where(grouped & (row % 16 < 16 - spare), -1, owner)
    pick = jnp.zeros((1, LANES), F32)
    for source in range(sources):
        filled = rows_of(source, tail_at, table_rows).astype(F32)
        filled = jnp.sum(jnp.where(owner == me, filled, 0.0), axis=0, keepdims=True)
        pick = pick + jnp.where(filled > 0.5, filled + float(source * prompts - 1), 0.0)
    pick = pick.astype(jnp.int32)

    chunk = min(sources, 8)
    picked_rows = slots * STATE
    row = lax.broadcasted_iota(jnp.int32, (picked_rows, LANES), 0)
    lane = lax.broadcasted_iota(jnp.int32, (picked_rows, LANES), 1)
    spread = one_hot(row // STATE == lane)
    span = chunk * prompts * STATE
    row = lax.broadcasted_iota(jnp.int32, (picked_rows, span), 0)
    lane = lax.broadcasted_iota(jnp.int32, (picked_rows, span), 1)
    same = row % STATE == lane % STATE
    states, windows, tails = None, None, None
    wide = -(-slots // 16) * 16
    row = lax.broadcasted_iota(jnp.int32, (wide, LANES), 0)
    lane = lax.broadcasted_iota(jnp.int32, (wide, LANES), 1)
    unit = one_hot(row == lane)
    for first in range(0, sources, chunk):
        wanted = lax.broadcasted_iota(jnp.int32, (span, LANES), 0) // STATE + first * prompts
        take = dot_nt(spread, one_hot(wanted == pick))
        take = jnp.where(same, take, 0.0).astype(BF16)
        table = []
        for source in range(first, first + chunk):
            for p in range(prompts):
                at = p * tiles * STATE
                table.append(
                    jnp.concatenate(
                        [
                            rows_of(source, at + tile * STATE, STATE)
                            for tile in range(tiles)
                        ],
                        axis=1,
                    )
                )
        part = jnp.dot(take, jnp.concatenate(table, axis=0), preferred_element_type=F32)
        states = part if states is None else states + part
        table = []
        for source in range(first, first + chunk):
            for p in range(prompts):
                at = window_at + p * WINDOW
                table.append(
                    jnp.concatenate(
                        [
                            rows_of(source, at, WINDOW // 2),
                            rows_of(source, at + WINDOW // 2, WINDOW // 2),
                        ],
                        axis=1,
                    )
                )
        part = jnp.dot(take, jnp.concatenate(table, axis=0), preferred_element_type=F32)
        windows = part if windows is None else windows + part
        table = []
        for source in range(first, first + chunk):
            table.append(
                jnp.concatenate(
                    [rows_of(source, tail_at + 8 * tile, 16) for tile in range(0, tiles, 2)],
                    axis=1,
                )
            )
        span_rows = chunk * 16
        row = lax.broadcasted_iota(jnp.int32, (span_rows, LANES), 0)
        local = pick - first * prompts
        base = (local // prompts) * 16 + (local % prompts) * depth
        hits = [one_hot(row == base + prompts * depth * odd + tap) for odd in (0, 1) for tap in range(depth)]
        hits = dot_nt(unit, jnp.concatenate(hits, axis=0)).astype(BF16)
        hits = jnp.concatenate(
            [hits[:, i * span_rows : (i + 1) * span_rows] for i in range(2 * depth)], axis=0
        )
        part = jnp.dot(hits, jnp.concatenate(table, axis=0), preferred_element_type=F32)
        tails = part if tails is None else tails + part

    state_ref[...] = states.astype(BF16).reshape(slots, STATE, channels)
    state_copy = pltpu.make_async_copy(state_ref, state_hbm, sems.at[0])
    state_copy.start()
    windows = windows.astype(BF16).reshape(slots, WINDOW // 2, 2 * LANES)
    for upper in range(2):
        for kind in range(2):
            at = upper * LANES + kind * HEAD_DIM
            keyval_ref[:, kind, upper * WINDOW // 2 : (upper + 1) * WINDOW // 2, :] = windows[
                :, :, at : at + HEAD_DIM
            ]
    keyval_copy = pltpu.make_async_copy(keyval_ref, keyval_hbm, sems.at[1])
    keyval_copy.start()
    for odd in range(2):
        for tap in range(depth):
            at = (odd * depth + tap) * wide
            for pair in range(tiles // 2):
                tile = 2 * pair + odd
                conv_ref[tap, :, tile * LANES : (tile + 1) * LANES] = tails[
                    at : at + slots, pair * LANES : (pair + 1) * LANES
                ].astype(BF16)
    conv_copy = pltpu.make_async_copy(conv_ref, conv_hbm, sems.at[2])
    conv_copy.start()
    state_copy.wait()
    keyval_copy.wait()
    conv_copy.wait()


def on_device(
    pr_size,
    tp_size,
    tokens,
    prompt_lengths,
    query_weight,
    key_weight,
    value_weight,
    attention_gain,
    inner_weight,
    conv_weight,
    scan_weight,
    step_weight,
    step_bias,
    mamba_rate,
    mamba_skip,
    mamba_gain,
    request_prompt,
    request_owner,
    request_slot,
):
    rows, width = tokens.shape
    prompts = prompt_lengths.shape[1]
    channels = inner_weight.shape[2]
    features = query_weight.shape[1]
    slots = request_owner.shape[0]
    tiles = channels // LANES

    def shape(dims, dtype=F32):
        return jax.ShapeDtypeStruct(dims, dtype)

    inner = jnp.einsum("td,dgc->gtc", tokens, inner_weight, preferred_element_type=F32)
    inner = inner.astype(BF16)
    partial, mixed, tail = pl.pallas_call(
        functools.partial(mix_kernel, prompts),
        out_shape=(
            shape((DT_RANK + 2 * STATE, rows)),
            shape((rows, channels), BF16),
            shape((8, channels)),
        ),
        in_specs=[SMEM] + [VMEM] * 3,
        out_specs=(VMEM, VMEM, VMEM),
        scratch_shapes=[pltpu.VMEM((rows + 8, channels), F32)],
        compiler_params=params(16),
        name="mix",
    )(prompt_lengths, inner, conv_weight, scan_weight.T)

    def swap(x, axis, size, bit):
        return lax.ppermute(x, axis, [(i, i ^ bit) for i in range(size)])

    near = swap(partial, "tp", tp_size, 1)
    spare = (16 - 2 * prompts * (CONV - 1)) * (tiles // 2)
    early_rows = prompts * WINDOW + 8 * tiles + -(-max(pr_size - spare, 0) // 16) * 16
    attended, square, early = pl.pallas_call(
        functools.partial(attend_kernel, prompts),
        out_shape=(
            shape((rows, features)),
            shape((8, rows)),
            shape((early_rows, LANES), BF16),
        ),
        in_specs=[SMEM] + [VMEM] * 8,
        out_specs=(VMEM, VMEM, VMEM),
        scratch_shapes=[
            pltpu.VMEM((8, LANES), jnp.int32),
        ],
        compiler_params=params(16),
        cost_estimate=pl.CostEstimate(
            flops=2 * rows * width * (features + channels), bytes_accessed=4 << 20, transcendentals=0
        ),
        name="attend",
    )(
        prompt_lengths,
        tokens,
        query_weight,
        key_weight.T,
        value_weight.T,
        tail,
        request_prompt[None],
        request_owner[None],
        request_slot[None],
    )
    pair = partial + near
    bit = 2
    while bit < tp_size // 2:
        pair = pair + swap(pair, "tp", tp_size, bit)
        bit *= 2
    far = swap(pair.astype(BF16), "tp", tp_size, bit)

    gated, sums, payload = scan_call(
        prompts,
        prompt_lengths,
        pair,
        far,
        mixed,
        inner,
        step_weight,
        step_bias[None],
        mamba_rate,
        mamba_skip[None],
        early,
        square,
    )

    me = lax.axis_index("pr").astype(jnp.int32)
    held = payload[None]
    pr_bits = [1 << i for i in reversed(range((pr_size - 1).bit_length()))]
    tp_bits = [1 << i for i in range((tp_size - 1).bit_length())]
    main, last = pr_bits[:-1], pr_bits[-1]
    near, far = tp_bits[:-1], tp_bits[-1]
    for index in range(max(len(main) - 1, len(near))):
        other = swap(sums, "tp", tp_size, near[index]) if index < len(near) else None
        if index >= len(main) - 1:
            sums = sums + other
            continue
        new = swap(held, "pr", pr_size, main[index])
        held, sums = pl.pallas_call(
            join_kernel,
            out_shape=(
                shape((2 * held.shape[0],) + held.shape[1:], BF16),
                shape(sums.shape),
            ),
            in_specs=[VMEM] * 4,
            out_specs=(VMEM, VMEM),
            compiler_params=params(16),
            name="join",
        )(held, new, sums, jnp.zeros_like(sums) if other is None else other)
    fresh = swap(held, "pr", pr_size, main[-1])
    crossed = swap(held, "pr", pr_size, last)
    sums_far = swap(sums, "tp", tp_size, far)
    fresh, sums_far = pl.pallas_call(
        hold_kernel,
        out_shape=(shape(fresh.shape, BF16), shape(sums.shape)),
        in_specs=[VMEM, VMEM, HBM],
        out_specs=(VMEM, VMEM),
        compiler_params=params(16),
        name="hold",
    )(fresh, sums_far, crossed)
    pieces = [held, fresh, crossed, swap(fresh, "pr", pr_size, last)]
    attention_out, mamba_out = pl.pallas_call(
        norm_kernel,
        out_shape=(shape((rows, features), BF16), shape((rows, channels), BF16)),
        in_specs=[VMEM] * 6,
        out_specs=(VMEM, VMEM),
        compiler_params=params(16),
        cost_estimate=pl.CostEstimate(flops=1 << 24, bytes_accessed=2 << 20, transcendentals=0),
        name="norm",
    )(attended, gated, sums, sums_far, attention_gain[None], mamba_gain[None])
    keyval, state, conv = pl.pallas_call(
        functools.partial(deliver_kernel, prompts, len(pieces)),
        out_shape=(
            shape((slots, 2, WINDOW, HEAD_DIM), BF16),
            shape((slots, STATE, channels), BF16),
            shape((CONV - 1, slots, channels), BF16),
        ),
        in_specs=[SMEM] + [VMEM] * len(pieces),
        out_specs=(HBM, HBM, HBM),
        scratch_shapes=[
            pltpu.VMEM((slots, 2, WINDOW, HEAD_DIM), BF16),
            pltpu.VMEM((slots, STATE, channels), BF16),
            pltpu.VMEM((CONV - 1, slots, channels), BF16),
            pltpu.SemaphoreType.DMA((3,)),
        ],
        compiler_params=params(32),
        name="deliver",
    )(me[None], *pieces)
    return (attention_out, mamba_out, keyval, state, conv.transpose(1, 0, 2))


def solution(mesh):
    return jax.shard_map(
        functools.partial(on_device, mesh.shape["pr"], mesh.shape["tp"]),
        mesh=mesh,
        in_specs=(
            P("pr", None),
            P("pr", None),
            P(None, "tp"),
            P(None, "tp"),
            P(None, "tp"),
            P("tp"),
            P(None, None, "tp"),
            P(None, "tp"),
            P("tp", None),
            P(None, "tp"),
            P("tp"),
            P(None, "tp"),
            P("tp"),
            P("tp"),
            P("pr"),
            P("pr"),
            P("pr"),
        ),
        out_specs=(
            P("pr", "tp"),
            P("pr", "tp"),
            P("pr", None, None, "tp"),
            P("pr", None, "tp"),
            P("pr", None, "tp"),
        ),
        check_vma=False,
    )
```

```python
import functools
import math

import jax
import jax.numpy as jnp
from jax import lax
from jax.experimental import pallas as pl
from jax.experimental.pallas import tpu as pltpu
from jax.sharding import PartitionSpec as P

HEADS = 16
KV_HEADS = 4
HEAD_DIM = 64
INNER = 2048
STATE = 16
DT_RANK = 64
CONV = 4
WINDOW = 32
EPSILON = 1e-06
LANES = 128
BLOCK = 16
RESET = 1e30

F32 = jnp.float32
BF16 = jnp.bfloat16
VMEM = pl.BlockSpec(memory_space=pltpu.VMEM)
SMEM = pl.BlockSpec(memory_space=pltpu.SMEM)
HBM = pl.BlockSpec(memory_space=pltpu.HBM)


def params(mib):
    return pltpu.CompilerParams(vmem_limit_bytes=mib << 20)


def dot_nt(a, b):
    return lax.dot_general(a, b, (((1,), (1,)), ((), ())), preferred_element_type=F32)


def bounds(len_ref, prompts):
    starts, ends = [], []
    at = 0
    for p in range(prompts):
        starts.append(at)
        at = at + len_ref[0, p]
        ends.append(at)
    return starts, ends


def first_row_of(position, starts, prompts):
    first = jnp.zeros_like(position)
    for p in range(1, prompts):
        first = jnp.where(position >= starts[p], starts[p], first)
    return first


def last_rows(shape, depth, starts, ends):
    row = lax.broadcasted_iota(jnp.int32, shape, 0)
    position = lax.broadcasted_iota(jnp.int32, shape, 1)
    hit = jnp.zeros(shape, F32)
    for p in range(len(starts)):
        here = (row >= p * depth) & (row < (p + 1) * depth) & (position >= starts[p])
        hit = jnp.where(here & (position - row == ends[p] - (p + 1) * depth), 1.0, hit)
    return hit.astype(BF16)


def row_sums(squares):
    total = squares[:, :LANES]
    for at in range(LANES, squares.shape[1], LANES):
        total = total + squares[:, at : at + LANES]
    return jnp.sum(total.T, axis=0, keepdims=True)


def sigmoid(x):
    return 0.5 * jnp.tanh(0.5 * x) + 0.5


def mix_kernel(
    prompts,
    len_ref,
    inner_ref,
    conv_ref,
    scan_ref,
    partial_ref,
    mixed_ref,
    raw_ref,
):
    _, rows, channels = inner_ref.shape
    starts, _ = bounds(len_ref, prompts)
    raw = inner_ref[0].astype(F32)
    raw_ref[pl.ds(0, 8), :] = jnp.zeros((8, channels), F32)
    raw_ref[pl.ds(8, rows), :] = raw
    position = lax.broadcasted_iota(jnp.int32, (rows, 1), 0)
    offset = position - first_row_of(position, starts, prompts)
    total = raw * conv_ref[CONV - 1 : CONV, :]
    for lag in range(1, CONV):
        shifted = raw_ref[pl.ds(8 - lag, rows), :]
        shifted = jnp.where(offset >= lag, shifted, 0.0)
        total = total + shifted * conv_ref[CONV - 1 - lag : CONV - lag, :]
    mixed = (total * sigmoid(total)).astype(BF16)
    mixed_ref[...] = mixed
    partial_ref[...] = dot_nt(scan_ref[...], mixed)


def attend_kernel(
    prompts,
    len_ref,
    tokens_ref,
    query_ref,
    key_ref,
    value_ref,
    inner_ref,
    prompt_ref,
    owner_ref,
    slot_ref,
    attended_ref,
    square_ref,
    packed_ref,
    request_ref,
):
    rows, width = tokens_ref.shape
    channels = inner_ref.shape[2]
    features = query_ref.shape[1]
    group = features // HEAD_DIM
    starts, ends = bounds(len_ref, prompts)
    tokens = tokens_ref[...]
    queries = jnp.dot(tokens, query_ref[...], preferred_element_type=F32).astype(BF16)
    keys = dot_nt(tokens, jnp.concatenate([key_ref[...]] * group, axis=0)).astype(BF16)
    values = dot_nt(tokens, jnp.concatenate([value_ref[...]] * group, axis=0)).astype(BF16)
    at_row = lax.broadcasted_iota(jnp.int32, (rows, rows), 0)
    at_column = lax.broadcasted_iota(jnp.int32, (rows, rows), 1)
    row_first = first_row_of(at_row, starts, prompts)
    allowed = (at_column <= at_row) & (at_row - at_column < WINDOW) & (at_column >= row_first)
    head_of = lax.broadcasted_iota(jnp.int32, (rows, features), 1) // HEAD_DIM
    zero = jnp.zeros((), BF16)
    attended = jnp.zeros((rows, features), F32)
    for head in range(group):
        mine = head_of == head
        scores = dot_nt(queries, jnp.where(mine, keys, zero)) * HEAD_DIM ** (-0.5)
        scores = jnp.where(allowed, scores, -1e30)
        top = jnp.max(scores, axis=1, keepdims=True)
        expons = jnp.exp(scores - top)
        weights = expons * (1.0 / jnp.sum(expons, axis=1, keepdims=True))
        attended = attended + jnp.dot(
            weights.astype(BF16), jnp.where(mine, values, zero), preferred_element_type=F32
        )
    attended_ref[...] = attended
    square_ref[...] = jnp.broadcast_to(row_sums(attended * attended), square_ref.shape)
    lane = lax.broadcasted_iota(jnp.int32, (rows, LANES), 1)
    both = jnp.where(lane < HEAD_DIM, keys[:, :LANES], values[:, :LANES])
    pick = last_rows((prompts * WINDOW, rows), WINDOW, starts, ends)
    packed_ref[: prompts * WINDOW, :] = jnp.dot(pick, both, preferred_element_type=F32).astype(
        BF16
    )
    requests = owner_ref.shape[1]
    request_ref[...] = jnp.full(request_ref.shape, -1, jnp.int32)
    request_ref[0:1, 0:requests] = owner_ref[...]
    request_ref[1:2, 0:requests] = slot_ref[...]
    request_ref[2:3, 0:requests] = prompt_ref[...]
    depth = prompts * (CONV - 1)
    groups = channels // LANES // 2
    spare = 16 - 2 * depth
    owners = packed_ref.shape[0] - prompts * WINDOW - 16 * groups + spare * groups
    owner = lax.broadcasted_iota(jnp.int32, (owners, LANES), 0) == request_ref[0:1, :]
    slot = lax.broadcasted_iota(jnp.int32, (LANES, LANES), 0) == request_ref[1:2, :]
    number = request_ref[2:3, :] + 1
    filled = dot_nt(
        jnp.where(owner, 1.0, 0.0).astype(BF16),
        jnp.where(slot, number, 0).astype(F32).astype(BF16),
    )
    pick = last_rows((8, rows), CONV - 1, starts, ends)
    tail = jnp.dot(pick, inner_ref[0], preferred_element_type=F32)
    base = prompts * WINDOW
    for group in range(groups):
        at = 2 * group * LANES
        packed_ref[base + 16 * group : base + 16 * (group + 1), :] = jnp.concatenate(
            [
                tail[:depth, at : at + LANES],
                tail[:depth, at + LANES : at + 2 * LANES],
                filled[spare * group : spare * (group + 1), :],
            ],
            axis=0,
        ).astype(BF16)
    if owners > spare * groups:
        packed_ref[base + 16 * groups :, :] = filled[spare * groups :, :].astype(BF16)


def scan_kernel(
    prompts,
    len_ref,
    own_ref,
    other_ref,
    mixed_ref,
    step_weight_ref,
    step_bias_ref,
    rate_ref,
    early_ref,
    payload_ref,
    states_even_ref,
    states_odd_ref,
    decay_ref,
    input_ref,
    in_map_ref,
):
    rows, channels = mixed_ref.shape
    pairs = rows // BLOCK // 2
    starts, ends = bounds(len_ref, prompts)
    projected = own_ref[...] + other_ref[...].astype(F32)
    low = projected[:DT_RANK, :].T.astype(BF16)
    pre = jnp.dot(low, step_weight_ref[...], preferred_element_type=F32) + step_bias_ref[...]
    step = jnp.maximum(pre, 0.0) + jnp.log1p(jnp.exp(-jnp.abs(pre)))
    position = lax.broadcasted_iota(jnp.int32, (rows, 1), 0)
    is_first = position == 0
    for p in range(1, prompts):
        is_first = is_first | (position == starts[p])
    decay_ref[...] = jnp.where(is_first, RESET, step)
    input_ref[...] = step * mixed_ref[...].astype(F32)
    for block in range(rows // BLOCK):
        columns = slice(block * BLOCK, (block + 1) * BLOCK)
        in_map_ref[block, :, 0:BLOCK] = projected[DT_RANK : DT_RANK + STATE, columns]
    rate = rate_ref[...] * (-math.log2(math.e))

    def advance(block, state, states_ref, index):
        at = pl.multiple_of(block * BLOCK, BLOCK)
        for token in range(BLOCK):
            decay = jnp.exp2(decay_ref[pl.ds(at + token, 1), :] * rate)
            entering = in_map_ref[block, :, token : token + 1] * input_ref[pl.ds(at + token, 1), :]
            state = state * decay + entering
            states_ref[index, token * STATE : (token + 1) * STATE, :] = state.astype(BF16)
        return state

    def two_blocks(pair, state):
        state = advance(2 * pair, state, states_even_ref, pair)
        return advance(2 * pair + 1, state, states_odd_ref, pair)

    lax.fori_loop(0, pairs, two_blocks, jnp.zeros((STATE, channels), F32))
    for p in range(prompts):
        last = ends[p] - 1
        block = last // BLOCK
        at = pl.multiple_of((last - block * BLOCK) * STATE, STATE)
        final = jnp.where(
            block % 2 == 0,
            states_even_ref[block // 2, pl.ds(at, STATE), :],
            states_odd_ref[block // 2, pl.ds(at, STATE), :],
        )
        for tile in range(channels // LANES):
            at = (p * (channels // LANES) + tile) * STATE
            payload_ref[at : at + STATE, :] = final[:, tile * LANES : (tile + 1) * LANES]
    base = prompts * channels // LANES * STATE
    payload_ref[base:, :] = early_ref[...]


def scan_call(prompts, lengths, own, other, mixed, *rest):
    rows, channels = mixed.shape
    tiles = channels // LANES
    payload_rows = prompts * tiles * STATE + rest[-1].shape[0]
    states = jax.ShapeDtypeStruct((rows // BLOCK // 2, BLOCK * STATE, channels), BF16)
    return pl.pallas_call(
        functools.partial(scan_kernel, prompts),
        out_shape=(jax.ShapeDtypeStruct((payload_rows, LANES), BF16), states, states),
        in_specs=[SMEM] + [VMEM] * 7,
        out_specs=(VMEM,) * 3,
        scratch_shapes=[
            pltpu.VMEM((rows, channels), F32),
            pltpu.VMEM((rows, channels), F32),
            pltpu.VMEM((rows // BLOCK, STATE, LANES), F32),
        ],
        compiler_params=params(16),
        name="scan",
    )(lengths, own, other, mixed, *rest)


def gate_kernel(
    own_ref,
    other_ref,
    states_even_ref,
    states_odd_ref,
    mixed_ref,
    inner_ref,
    skip_ref,
    square_ref,
    gated_ref,
    sums_ref,
    out_map_ref,
    scanned_ref,
):
    rows, channels = mixed_ref.shape
    span = BLOCK * STATE
    maps = slice(DT_RANK + STATE, DT_RANK + 2 * STATE)
    out_map = own_ref[maps, :] + other_ref[maps, :].astype(F32)
    row = lax.broadcasted_iota(jnp.int32, (STATE, span), 0)
    column = lax.broadcasted_iota(jnp.int32, (STATE, span), 1)
    tiled = jnp.dot(
        out_map.T.astype(BF16),
        jnp.where(column % STATE == row, 1.0, 0.0).astype(BF16),
        preferred_element_type=F32,
    )
    row = lax.broadcasted_iota(jnp.int32, (rows, span), 0)
    column = lax.broadcasted_iota(jnp.int32, (rows, span), 1)
    out_map_ref[...] = jnp.where(column // STATE == row % BLOCK, tiled, 0.0).astype(BF16)
    for block in range(rows // BLOCK):
        states_ref = states_odd_ref if block % 2 else states_even_ref
        at = slice(block * BLOCK, (block + 1) * BLOCK)
        scanned_ref[at, :] = jnp.dot(
            out_map_ref[at, :], states_ref[block // 2], preferred_element_type=F32
        )
    gate = inner_ref[1].astype(F32)
    gated = (scanned_ref[...] + skip_ref[...] * mixed_ref[...].astype(F32)) * (
        gate * sigmoid(gate)
    )
    gated_ref[...] = gated
    sums_ref[0:1, :] = square_ref[0:1, :]
    sums_ref[1:2, :] = row_sums(gated * gated)


def join_kernel(held_ref, new_ref, sums_ref, joined_ref, same_ref):
    count = held_ref.shape[0]
    joined_ref[:count] = held_ref[...]
    joined_ref[count:] = new_ref[...]
    same_ref[...] = sums_ref[...]


def hold_kernel(new_ref, own_ref, other_ref, crossed_hbm, fresh_ref, sums_ref):
    fresh_ref[...] = new_ref[...]
    sums_ref[...] = own_ref[...] + other_ref[...]


def norm_kernel(
    attended_ref,
    gated_ref,
    own_ref,
    other_ref,
    attention_gain_ref,
    mamba_gain_ref,
    attention_ref,
    mamba_ref,
):
    sums = own_ref[...] + other_ref[...]
    sums = jnp.concatenate([sums, jnp.zeros((6, sums.shape[1]), F32)], axis=0).T
    attention_scale = lax.rsqrt(sums[:, 0:1] / (HEADS * HEAD_DIM) + EPSILON)
    attention_ref[...] = (attended_ref[...] * attention_scale * attention_gain_ref[...]).astype(
        BF16
    )
    mamba_scale = lax.rsqrt(sums[:, 1:2] / INNER + EPSILON)
    mamba_ref[...] = (gated_ref[...] * mamba_scale * mamba_gain_ref[...]).astype(BF16)


def one_hot(hit):
    return jnp.where(hit, 1.0, 0.0).astype(BF16)


def deliver_kernel(
    prompts,
    pieces,
    me_ref,
    *refs,
):
    keyval_hbm, state_hbm, conv_hbm, keyval_ref, state_ref, conv_ref, sems = refs[pieces:]
    me = me_ref[0]
    slots, _, channels = state_ref.shape
    tiles = channels // LANES
    blocks = [(ref, index) for ref in refs[:pieces] for index in range(ref.shape[0])]
    sources = len(blocks)
    window_at = prompts * tiles * STATE
    tail_at = window_at + prompts * WINDOW
    depth = CONV - 1
    spare = 16 - 2 * prompts * depth
    table_rows = refs[0].shape[1] - tail_at

    def rows_of(source, at, size):
        ref, index = blocks[source]
        return ref[index, at : at + size, :]

    row = lax.broadcasted_iota(jnp.int32, (table_rows, LANES), 0)
    grouped = row < 8 * tiles
    owner = jnp.where(
        grouped, row // 16 * spare + row % 16 - (16 - spare), row - 8 * tiles + spare * (tiles // 2)
    )
    owner = jnp.where(grouped & (row % 16 < 16 - spare), -1, owner)
    pick = jnp.zeros((1, LANES), F32)
    for source in range(sources):
        filled = rows_of(source, tail_at, table_rows).astype(F32)
        filled = jnp.sum(jnp.where(owner == me, filled, 0.0), axis=0, keepdims=True)
        pick = pick + jnp.where(filled > 0.5, filled + float(source * prompts - 1), 0.0)
    pick = pick.astype(jnp.int32)

    chunk = min(sources, 8)
    picked_rows = slots * STATE
    row = lax.broadcasted_iota(jnp.int32, (picked_rows, LANES), 0)
    lane = lax.broadcasted_iota(jnp.int32, (picked_rows, LANES), 1)
    spread = one_hot(row // STATE == lane)
    span = chunk * prompts * STATE
    row = lax.broadcasted_iota(jnp.int32, (picked_rows, span), 0)
    lane = lax.broadcasted_iota(jnp.int32, (picked_rows, span), 1)
    same = row % STATE == lane % STATE
    states, windows, tails = None, None, None
    wide = -(-slots // 16) * 16
    row = lax.broadcasted_iota(jnp.int32, (wide, LANES), 0)
    lane = lax.broadcasted_iota(jnp.int32, (wide, LANES), 1)
    unit = one_hot(row == lane)
    for first in range(0, sources, chunk):
        wanted = lax.broadcasted_iota(jnp.int32, (span, LANES), 0) // STATE + first * prompts
        take = dot_nt(spread, one_hot(wanted == pick))
        take = jnp.where(same, take, 0.0).astype(BF16)
        table = []
        for source in range(first, first + chunk):
            for p in range(prompts):
                at = p * tiles * STATE
                table.append(
                    jnp.concatenate(
                        [
                            rows_of(source, at + tile * STATE, STATE)
                            for tile in range(tiles)
                        ],
                        axis=1,
                    )
                )
        part = jnp.dot(take, jnp.concatenate(table, axis=0), preferred_element_type=F32)
        states = part if states is None else states + part
        table = []
        for source in range(first, first + chunk):
            for p in range(prompts):
                at = window_at + p * WINDOW
                table.append(
                    jnp.concatenate(
                        [
                            rows_of(source, at, WINDOW // 2),
                            rows_of(source, at + WINDOW // 2, WINDOW // 2),
                        ],
                        axis=1,
                    )
                )
        part = jnp.dot(take, jnp.concatenate(table, axis=0), preferred_element_type=F32)
        windows = part if windows is None else windows + part
        table = []
        for source in range(first, first + chunk):
            table.append(
                jnp.concatenate(
                    [rows_of(source, tail_at + 8 * tile, 16) for tile in range(0, tiles, 2)],
                    axis=1,
                )
            )
        span_rows = chunk * 16
        row = lax.broadcasted_iota(jnp.int32, (span_rows, LANES), 0)
        local = pick - first * prompts
        base = (local // prompts) * 16 + (local % prompts) * depth
        hits = [one_hot(row == base + prompts * depth * odd + tap) for odd in (0, 1) for tap in range(depth)]
        hits = dot_nt(unit, jnp.concatenate(hits, axis=0)).astype(BF16)
        hits = jnp.concatenate(
            [hits[:, i * span_rows : (i + 1) * span_rows] for i in range(2 * depth)], axis=0
        )
        part = jnp.dot(hits, jnp.concatenate(table, axis=0), preferred_element_type=F32)
        tails = part if tails is None else tails + part

    state_ref[...] = states.astype(BF16).reshape(slots, STATE, channels)
    state_copy = pltpu.make_async_copy(state_ref, state_hbm, sems.at[0])
    state_copy.start()
    windows = windows.astype(BF16).reshape(slots, WINDOW // 2, 2 * LANES)
    for upper in range(2):
        for kind in range(2):
            at = upper * LANES + kind * HEAD_DIM
            keyval_ref[:, kind, upper * WINDOW // 2 : (upper + 1) * WINDOW // 2, :] = windows[
                :, :, at : at + HEAD_DIM
            ]
    keyval_copy = pltpu.make_async_copy(keyval_ref, keyval_hbm, sems.at[1])
    keyval_copy.start()
    for odd in range(2):
        for tap in range(depth):
            at = (odd * depth + tap) * wide
            for pair in range(tiles // 2):
                tile = 2 * pair + odd
                conv_ref[tap, :, tile * LANES : (tile + 1) * LANES] = tails[
                    at : at + slots, pair * LANES : (pair + 1) * LANES
                ].astype(BF16)
    conv_copy = pltpu.make_async_copy(conv_ref, conv_hbm, sems.at[2])
    conv_copy.start()
    state_copy.wait()
    keyval_copy.wait()
    conv_copy.wait()


def on_device(
    pr_size,
    tp_size,
    tokens,
    prompt_lengths,
    query_weight,
    key_weight,
    value_weight,
    attention_gain,
    inner_weight,
    conv_weight,
    scan_weight,
    step_weight,
    step_bias,
    mamba_rate,
    mamba_skip,
    mamba_gain,
    request_prompt,
    request_owner,
    request_slot,
):
    rows, width = tokens.shape
    prompts = prompt_lengths.shape[1]
    channels = inner_weight.shape[2]
    features = query_weight.shape[1]
    slots = request_owner.shape[0]
    tiles = channels // LANES

    def shape(dims, dtype=F32):
        return jax.ShapeDtypeStruct(dims, dtype)

    inner = jnp.einsum("td,dgc->gtc", tokens, inner_weight, preferred_element_type=F32)
    inner = inner.astype(BF16)
    partial, mixed = pl.pallas_call(
        functools.partial(mix_kernel, prompts),
        out_shape=(
            shape((DT_RANK + 2 * STATE, rows)),
            shape((rows, channels), BF16),
        ),
        in_specs=[SMEM] + [VMEM] * 3,
        out_specs=(VMEM, VMEM),
        scratch_shapes=[pltpu.VMEM((rows + 8, channels), F32)],
        compiler_params=params(16),
        name="mix",
    )(prompt_lengths, inner, conv_weight, scan_weight.T)

    def swap(x, axis, size, bit):
        return lax.ppermute(x, axis, [(i, i ^ bit) for i in range(size)])

    near = swap(partial, "tp", tp_size, 1)
    spare = (16 - 2 * prompts * (CONV - 1)) * (tiles // 2)
    early_rows = prompts * WINDOW + 8 * tiles + -(-max(pr_size - spare, 0) // 16) * 16
    attended, square, early = pl.pallas_call(
        functools.partial(attend_kernel, prompts),
        out_shape=(
            shape((rows, features)),
            shape((8, rows)),
            shape((early_rows, LANES), BF16),
        ),
        in_specs=[SMEM] + [VMEM] * 8,
        out_specs=(VMEM, VMEM, VMEM),
        scratch_shapes=[
            pltpu.VMEM((8, LANES), jnp.int32),
        ],
        compiler_params=params(16),
        cost_estimate=pl.CostEstimate(
            flops=2 * rows * width * (features + channels), bytes_accessed=4 << 20, transcendentals=0
        ),
        name="attend",
    )(
        prompt_lengths,
        tokens,
        query_weight,
        key_weight.T,
        value_weight.T,
        inner,
        request_prompt[None],
        request_owner[None],
        request_slot[None],
    )
    pair = partial + near
    bit = 2
    while bit < tp_size // 2:
        pair = pair + swap(pair, "tp", tp_size, bit)
        bit *= 2
    far = swap(pair.astype(BF16), "tp", tp_size, bit)

    payload, states_even, states_odd = scan_call(
        prompts,
        prompt_lengths,
        pair,
        far,
        mixed,
        step_weight,
        step_bias[None],
        mamba_rate,
        early,
    )
    gated, sums = pl.pallas_call(
        gate_kernel,
        out_shape=(shape((rows, channels)), shape((2, rows))),
        in_specs=[VMEM] * 8,
        out_specs=(VMEM, VMEM),
        scratch_shapes=[
            pltpu.VMEM((rows, BLOCK * STATE), BF16),
            pltpu.VMEM((rows, channels), F32),
        ],
        compiler_params=params(16),
        cost_estimate=pl.CostEstimate(flops=1 << 24, bytes_accessed=4 << 20, transcendentals=0),
        name="gate",
    )(pair, far, states_even, states_odd, mixed, inner, mamba_skip[None], square)

    me = lax.axis_index("pr").astype(jnp.int32)
    held = payload[None]
    pr_bits = [1 << i for i in reversed(range((pr_size - 1).bit_length()))]
    tp_bits = [1 << i for i in range((tp_size - 1).bit_length())]
    main, last = pr_bits[:-1], pr_bits[-1]
    for bit in main[:-1]:
        new = swap(held, "pr", pr_size, bit)
        held, sums = pl.pallas_call(
            join_kernel,
            out_shape=(
                shape((2 * held.shape[0],) + held.shape[1:], BF16),
                shape(sums.shape),
            ),
            in_specs=[VMEM] * 3,
            out_specs=(VMEM, VMEM),
            compiler_params=params(16),
            name="join",
        )(held, new, sums)
    for bit in tp_bits[:-2]:
        sums = sums + swap(sums, "tp", tp_size, bit)
    crossed = swap(held, "pr", pr_size, last)
    fresh = swap(held, "pr", pr_size, main[-1])
    other = swap(sums, "tp", tp_size, tp_bits[-2])
    fresh, sums = pl.pallas_call(
        hold_kernel,
        out_shape=(shape(fresh.shape, BF16), shape(sums.shape)),
        in_specs=[VMEM, VMEM, VMEM, HBM],
        out_specs=(VMEM, VMEM),
        compiler_params=params(16),
        name="hold",
    )(fresh, sums, other, crossed)
    pieces = [held, fresh, crossed, swap(fresh, "pr", pr_size, last)]
    sums_far = swap(sums, "tp", tp_size, tp_bits[-1])
    attention_out, mamba_out = pl.pallas_call(
        norm_kernel,
        out_shape=(shape((rows, features), BF16), shape((rows, channels), BF16)),
        in_specs=[VMEM] * 6,
        out_specs=(VMEM, VMEM),
        compiler_params=params(16),
        cost_estimate=pl.CostEstimate(flops=1 << 24, bytes_accessed=2 << 20, transcendentals=0),
        name="norm",
    )(attended, gated, sums, sums_far, attention_gain[None], mamba_gain[None])
    keyval, state, conv = pl.pallas_call(
        functools.partial(deliver_kernel, prompts, len(pieces)),
        out_shape=(
            shape((slots, 2, WINDOW, HEAD_DIM), BF16),
            shape((slots, STATE, channels), BF16),
            shape((CONV - 1, slots, channels), BF16),
        ),
        in_specs=[SMEM] + [VMEM] * len(pieces),
        out_specs=(HBM, HBM, HBM),
        scratch_shapes=[
            pltpu.VMEM((slots, 2, WINDOW, HEAD_DIM), BF16),
            pltpu.VMEM((slots, STATE, channels), BF16),
            pltpu.VMEM((CONV - 1, slots, channels), BF16),
            pltpu.SemaphoreType.DMA((3,)),
        ],
        compiler_params=params(32),
        name="deliver",
    )(me[None], *pieces)
    return (attention_out, mamba_out, keyval, state, conv.transpose(1, 0, 2))


def solution(mesh):
    return jax.shard_map(
        functools.partial(on_device, mesh.shape["pr"], mesh.shape["tp"]),
        mesh=mesh,
        in_specs=(
            P("pr", None),
            P("pr", None),
            P(None, "tp"),
            P(None, "tp"),
            P(None, "tp"),
            P("tp"),
            P(None, None, "tp"),
            P(None, "tp"),
            P("tp", None),
            P(None, "tp"),
            P("tp"),
            P(None, "tp"),
            P("tp"),
            P("tp"),
            P("pr"),
            P("pr"),
            P("pr"),
        ),
        out_specs=(
            P("pr", "tp"),
            P("pr", "tp"),
            P("pr", None, None, "tp"),
            P("pr", None, "tp"),
            P("pr", None, "tp"),
        ),
        check_vma=False,
    )
```

```python
import functools
import math

import jax
import jax.numpy as jnp
from jax import lax
from jax.experimental import pallas as pl
from jax.experimental.pallas import tpu as pltpu
from jax.sharding import PartitionSpec as P

HEADS = 16
KV_HEADS = 4
HEAD_DIM = 64
INNER = 2048
STATE = 16
DT_RANK = 64
CONV = 4
WINDOW = 32
EPSILON = 1e-06
LANES = 128
BLOCK = 16
RESET = 1e30

F32 = jnp.float32
BF16 = jnp.bfloat16
VMEM = pl.BlockSpec(memory_space=pltpu.VMEM)
SMEM = pl.BlockSpec(memory_space=pltpu.SMEM)
HBM = pl.BlockSpec(memory_space=pltpu.HBM)


def params(mib):
    return pltpu.CompilerParams(vmem_limit_bytes=mib << 20)


def dot_nt(a, b):
    return lax.dot_general(a, b, (((1,), (1,)), ((), ())), preferred_element_type=F32)


def bounds(len_ref, prompts):
    starts, ends = [], []
    at = 0
    for p in range(prompts):
        starts.append(at)
        at = at + len_ref[0, p]
        ends.append(at)
    return starts, ends


def first_row_of(position, starts, prompts):
    first = jnp.zeros_like(position)
    for p in range(1, prompts):
        first = jnp.where(position >= starts[p], starts[p], first)
    return first


def last_rows(shape, depth, starts, ends):
    row = lax.broadcasted_iota(jnp.int32, shape, 0)
    position = lax.broadcasted_iota(jnp.int32, shape, 1)
    hit = jnp.zeros(shape, F32)
    for p in range(len(starts)):
        here = (row >= p * depth) & (row < (p + 1) * depth) & (position >= starts[p])
        hit = jnp.where(here & (position - row == ends[p] - (p + 1) * depth), 1.0, hit)
    return hit.astype(BF16)


def row_sums(squares):
    total = squares[:, :LANES]
    for at in range(LANES, squares.shape[1], LANES):
        total = total + squares[:, at : at + LANES]
    return jnp.sum(total.T, axis=0, keepdims=True)


def sigmoid(x):
    return 0.5 * jnp.tanh(0.5 * x) + 0.5


def mix_kernel(
    prompts,
    len_ref,
    inner_ref,
    conv_ref,
    scan_ref,
    partial_ref,
    mixed_ref,
    raw_ref,
):
    _, rows, channels = inner_ref.shape
    starts, _ = bounds(len_ref, prompts)
    raw = inner_ref[0].astype(F32)
    raw_ref[pl.ds(0, 8), :] = jnp.zeros((8, channels), F32)
    raw_ref[pl.ds(8, rows), :] = raw
    position = lax.broadcasted_iota(jnp.int32, (rows, 1), 0)
    offset = position - first_row_of(position, starts, prompts)
    total = raw * conv_ref[CONV - 1 : CONV, :]
    for lag in range(1, CONV):
        shifted = raw_ref[pl.ds(8 - lag, rows), :]
        shifted = jnp.where(offset >= lag, shifted, 0.0)
        total = total + shifted * conv_ref[CONV - 1 - lag : CONV - lag, :]
    mixed = (total * sigmoid(total)).astype(BF16)
    mixed_ref[...] = mixed
    partial_ref[...] = dot_nt(scan_ref[...], mixed)


def attend_kernel(
    prompts,
    len_ref,
    tokens_ref,
    query_ref,
    key_ref,
    value_ref,
    inner_ref,
    prompt_ref,
    owner_ref,
    slot_ref,
    attended_ref,
    square_ref,
    packed_ref,
    request_ref,
):
    rows, width = tokens_ref.shape
    channels = inner_ref.shape[2]
    features = query_ref.shape[1]
    group = features // HEAD_DIM
    starts, ends = bounds(len_ref, prompts)
    tokens = tokens_ref[...]
    queries = jnp.dot(tokens, query_ref[...], preferred_element_type=F32).astype(BF16)
    keys = dot_nt(tokens, jnp.concatenate([key_ref[...]] * group, axis=0)).astype(BF16)
    values = dot_nt(tokens, jnp.concatenate([value_ref[...]] * group, axis=0)).astype(BF16)
    at_row = lax.broadcasted_iota(jnp.int32, (rows, rows), 0)
    at_column = lax.broadcasted_iota(jnp.int32, (rows, rows), 1)
    row_first = first_row_of(at_row, starts, prompts)
    allowed = (at_column <= at_row) & (at_row - at_column < WINDOW) & (at_column >= row_first)
    head_of = lax.broadcasted_iota(jnp.int32, (rows, features), 1) // HEAD_DIM
    zero = jnp.zeros((), BF16)
    attended = jnp.zeros((rows, features), F32)
    for head in range(group):
        mine = head_of == head
        scores = dot_nt(queries, jnp.where(mine, keys, zero)) * HEAD_DIM ** (-0.5)
        scores = jnp.where(allowed, scores, -1e30)
        top = jnp.max(scores, axis=1, keepdims=True)
        expons = jnp.exp(scores - top)
        weights = expons * (1.0 / jnp.sum(expons, axis=1, keepdims=True))
        attended = attended + jnp.dot(
            weights.astype(BF16), jnp.where(mine, values, zero), preferred_element_type=F32
        )
    attended_ref[...] = attended
    square_ref[...] = jnp.broadcast_to(row_sums(attended * attended), square_ref.shape)
    lane = lax.broadcasted_iota(jnp.int32, (rows, LANES), 1)
    both = jnp.where(lane < HEAD_DIM, keys[:, :LANES], values[:, :LANES])
    pick = last_rows((prompts * WINDOW, rows), WINDOW, starts, ends)
    packed_ref[: prompts * WINDOW, :] = jnp.dot(pick, both, preferred_element_type=F32).astype(
        BF16
    )
    requests = owner_ref.shape[1]
    request_ref[...] = jnp.full(request_ref.shape, -1, jnp.int32)
    request_ref[0:1, 0:requests] = owner_ref[...]
    request_ref[1:2, 0:requests] = slot_ref[...]
    request_ref[2:3, 0:requests] = prompt_ref[...]
    depth = prompts * (CONV - 1)
    groups = channels // LANES // 2
    spare = 16 - 2 * depth
    owners = packed_ref.shape[0] - prompts * WINDOW - 16 * groups + spare * groups
    owner = lax.broadcasted_iota(jnp.int32, (owners, LANES), 0) == request_ref[0:1, :]
    slot = lax.broadcasted_iota(jnp.int32, (LANES, LANES), 0) == request_ref[1:2, :]
    number = request_ref[2:3, :] + 1
    filled = dot_nt(
        jnp.where(owner, 1.0, 0.0).astype(BF16),
        jnp.where(slot, number, 0).astype(F32).astype(BF16),
    )
    pick = last_rows((8, rows), CONV - 1, starts, ends)
    tail = jnp.dot(pick, inner_ref[0], preferred_element_type=F32)
    base = prompts * WINDOW
    for group in range(groups):
        at = 2 * group * LANES
        packed_ref[base + 16 * group : base + 16 * (group + 1), :] = jnp.concatenate(
            [
                tail[:depth, at : at + LANES],
                tail[:depth, at + LANES : at + 2 * LANES],
                filled[spare * group : spare * (group + 1), :],
            ],
            axis=0,
        ).astype(BF16)
    if owners > spare * groups:
        packed_ref[base + 16 * groups :, :] = filled[spare * groups :, :].astype(BF16)


def scan_kernel(
    prompts,
    len_ref,
    own_ref,
    other_ref,
    mixed_ref,
    step_weight_ref,
    step_bias_ref,
    rate_ref,
    early_ref,
    payload_ref,
    states_even_ref,
    states_odd_ref,
    decay_ref,
    input_ref,
    in_map_ref,
):
    rows, channels = mixed_ref.shape
    pairs = rows // BLOCK // 2
    starts, ends = bounds(len_ref, prompts)
    projected = own_ref[...] + other_ref[...].astype(F32)
    low = projected[:DT_RANK, :].T.astype(BF16)
    pre = jnp.dot(low, step_weight_ref[...], preferred_element_type=F32) + step_bias_ref[...]
    step = jnp.maximum(pre, 0.0) + jnp.log1p(jnp.exp(-jnp.abs(pre)))
    position = lax.broadcasted_iota(jnp.int32, (rows, 1), 0)
    is_first = position == 0
    for p in range(1, prompts):
        is_first = is_first | (position == starts[p])
    decay_ref[...] = jnp.where(is_first, RESET, step)
    input_ref[...] = step * mixed_ref[...].astype(F32)
    for block in range(rows // BLOCK):
        columns = slice(block * BLOCK, (block + 1) * BLOCK)
        in_map_ref[block, :, 0:BLOCK] = projected[DT_RANK : DT_RANK + STATE, columns]
    rate = rate_ref[...] * (-math.log2(math.e))

    def advance(block, state, states_ref, index):
        at = pl.multiple_of(block * BLOCK, BLOCK)
        for token in range(BLOCK):
            decay = jnp.exp2(decay_ref[pl.ds(at + token, 1), :] * rate)
            entering = in_map_ref[block, :, token : token + 1] * input_ref[pl.ds(at + token, 1), :]
            state = state * decay + entering
            states_ref[index, token * STATE : (token + 1) * STATE, :] = state.astype(BF16)
        return state

    def two_blocks(pair, state):
        state = advance(2 * pair, state, states_even_ref, pair)
        return advance(2 * pair + 1, state, states_odd_ref, pair)

    lax.fori_loop(0, pairs, two_blocks, jnp.zeros((STATE, channels), F32))
    for p in range(prompts):
        last = ends[p] - 1
        block = last // BLOCK
        at = pl.multiple_of((last - block * BLOCK) * STATE, STATE)
        final = jnp.where(
            block % 2 == 0,
            states_even_ref[block // 2, pl.ds(at, STATE), :],
            states_odd_ref[block // 2, pl.ds(at, STATE), :],
        )
        for tile in range(channels // LANES):
            at = (p * (channels // LANES) + tile) * STATE
            payload_ref[at : at + STATE, :] = final[:, tile * LANES : (tile + 1) * LANES]
    base = prompts * channels // LANES * STATE
    payload_ref[base:, :] = early_ref[...]


def scan_call(prompts, lengths, own, other, mixed, *rest):
    rows, channels = mixed.shape
    tiles = channels // LANES
    payload_rows = prompts * tiles * STATE + rest[-1].shape[0]
    states = jax.ShapeDtypeStruct((rows // BLOCK // 2, BLOCK * STATE, channels), BF16)
    return pl.pallas_call(
        functools.partial(scan_kernel, prompts),
        out_shape=(jax.ShapeDtypeStruct((payload_rows, LANES), BF16), states, states),
        in_specs=[SMEM] + [VMEM] * 7,
        out_specs=(VMEM,) * 3,
        scratch_shapes=[
            pltpu.VMEM((rows, channels), F32),
            pltpu.VMEM((rows, channels), F32),
            pltpu.VMEM((rows // BLOCK, STATE, LANES), F32),
        ],
        compiler_params=params(16),
        name="scan",
    )(lengths, own, other, mixed, *rest)


def gate_kernel(
    own_ref,
    other_ref,
    states_even_ref,
    states_odd_ref,
    mixed_ref,
    inner_ref,
    skip_ref,
    square_ref,
    gated_ref,
    sums_ref,
    out_map_ref,
    scanned_ref,
):
    rows, channels = mixed_ref.shape
    span = BLOCK * STATE
    maps = slice(DT_RANK + STATE, DT_RANK + 2 * STATE)
    out_map = own_ref[maps, :] + other_ref[maps, :].astype(F32)
    row = lax.broadcasted_iota(jnp.int32, (STATE, span), 0)
    column = lax.broadcasted_iota(jnp.int32, (STATE, span), 1)
    tiled = jnp.dot(
        out_map.T.astype(BF16),
        jnp.where(column % STATE == row, 1.0, 0.0).astype(BF16),
        preferred_element_type=F32,
    )
    row = lax.broadcasted_iota(jnp.int32, (rows, span), 0)
    column = lax.broadcasted_iota(jnp.int32, (rows, span), 1)
    out_map_ref[...] = jnp.where(column // STATE == row % BLOCK, tiled, 0.0).astype(BF16)
    for block in range(rows // BLOCK):
        states_ref = states_odd_ref if block % 2 else states_even_ref
        at = slice(block * BLOCK, (block + 1) * BLOCK)
        scanned_ref[at, :] = jnp.dot(
            out_map_ref[at, :], states_ref[block // 2], preferred_element_type=F32
        )
    gate = inner_ref[1].astype(F32)
    gated = (scanned_ref[...] + skip_ref[...] * mixed_ref[...].astype(F32)) * (
        gate * sigmoid(gate)
    )
    gated_ref[...] = gated
    sums_ref[0:1, :] = square_ref[0:1, :]
    sums_ref[1:2, :] = row_sums(gated * gated)


def join_kernel(held_ref, new_ref, own_ref, other_ref, joined_ref, sums_ref):
    count = held_ref.shape[0]
    joined_ref[:count] = held_ref[...]
    joined_ref[count:] = new_ref[...]
    sums_ref[...] = own_ref[...] + other_ref[...]


def hold_kernel(new_ref, own_ref, other_ref, fresh_ref, sums_ref):
    fresh_ref[...] = new_ref[...]
    sums_ref[...] = own_ref[...] + other_ref[...]


def norm_kernel(
    attended_ref,
    gated_ref,
    sums_ref,
    attention_gain_ref,
    mamba_gain_ref,
    crossed_hbm,
    attention_ref,
    mamba_ref,
):
    sums = sums_ref[...]
    sums = jnp.concatenate([sums, jnp.zeros((6, sums.shape[1]), F32)], axis=0).T
    attention_scale = lax.rsqrt(sums[:, 0:1] / (HEADS * HEAD_DIM) + EPSILON)
    attention_ref[...] = (attended_ref[...] * attention_scale * attention_gain_ref[...]).astype(
        BF16
    )
    mamba_scale = lax.rsqrt(sums[:, 1:2] / INNER + EPSILON)
    mamba_ref[...] = (gated_ref[...] * mamba_scale * mamba_gain_ref[...]).astype(BF16)


def one_hot(hit):
    return jnp.where(hit, 1.0, 0.0).astype(BF16)


def deliver_kernel(
    prompts,
    pieces,
    me_ref,
    *refs,
):
    keyval_hbm, state_hbm, conv_hbm, keyval_ref, state_ref, conv_ref, sems = refs[pieces:]
    me = me_ref[0]
    slots, _, channels = state_ref.shape
    tiles = channels // LANES
    blocks = [(ref, index) for ref in refs[:pieces] for index in range(ref.shape[0])]
    sources = len(blocks)
    window_at = prompts * tiles * STATE
    tail_at = window_at + prompts * WINDOW
    depth = CONV - 1
    spare = 16 - 2 * prompts * depth
    table_rows = refs[0].shape[1] - tail_at

    def rows_of(source, at, size):
        ref, index = blocks[source]
        return ref[index, at : at + size, :]

    row = lax.broadcasted_iota(jnp.int32, (table_rows, LANES), 0)
    grouped = row < 8 * tiles
    owner = jnp.where(
        grouped, row // 16 * spare + row % 16 - (16 - spare), row - 8 * tiles + spare * (tiles // 2)
    )
    owner = jnp.where(grouped & (row % 16 < 16 - spare), -1, owner)
    pick = jnp.zeros((1, LANES), F32)
    for source in range(sources):
        filled = rows_of(source, tail_at, table_rows).astype(F32)
        filled = jnp.sum(jnp.where(owner == me, filled, 0.0), axis=0, keepdims=True)
        pick = pick + jnp.where(filled > 0.5, filled + float(source * prompts - 1), 0.0)
    pick = pick.astype(jnp.int32)

    chunk = min(sources, 8)
    picked_rows = slots * STATE
    row = lax.broadcasted_iota(jnp.int32, (picked_rows, LANES), 0)
    lane = lax.broadcasted_iota(jnp.int32, (picked_rows, LANES), 1)
    spread = one_hot(row // STATE == lane)
    span = chunk * prompts * STATE
    row = lax.broadcasted_iota(jnp.int32, (picked_rows, span), 0)
    lane = lax.broadcasted_iota(jnp.int32, (picked_rows, span), 1)
    same = row % STATE == lane % STATE
    states, windows, tails = None, None, None
    wide = -(-slots // 16) * 16
    row = lax.broadcasted_iota(jnp.int32, (wide, LANES), 0)
    lane = lax.broadcasted_iota(jnp.int32, (wide, LANES), 1)
    unit = one_hot(row == lane)
    for first in range(0, sources, chunk):
        wanted = lax.broadcasted_iota(jnp.int32, (span, LANES), 0) // STATE + first * prompts
        take = dot_nt(spread, one_hot(wanted == pick))
        take = jnp.where(same, take, 0.0).astype(BF16)
        table = []
        for source in range(first, first + chunk):
            for p in range(prompts):
                at = p * tiles * STATE
                table.append(
                    jnp.concatenate(
                        [
                            rows_of(source, at + tile * STATE, STATE)
                            for tile in range(tiles)
                        ],
                        axis=1,
                    )
                )
        part = jnp.dot(take, jnp.concatenate(table, axis=0), preferred_element_type=F32)
        states = part if states is None else states + part
        table = []
        for source in range(first, first + chunk):
            for p in range(prompts):
                at = window_at + p * WINDOW
                table.append(
                    jnp.concatenate(
                        [
                            rows_of(source, at, WINDOW // 2),
                            rows_of(source, at + WINDOW // 2, WINDOW // 2),
                        ],
                        axis=1,
                    )
                )
        part = jnp.dot(take, jnp.concatenate(table, axis=0), preferred_element_type=F32)
        windows = part if windows is None else windows + part
        table = []
        for source in range(first, first + chunk):
            table.append(
                jnp.concatenate(
                    [rows_of(source, tail_at + 8 * tile, 16) for tile in range(0, tiles, 2)],
                    axis=1,
                )
            )
        span_rows = chunk * 16
        row = lax.broadcasted_iota(jnp.int32, (span_rows, LANES), 0)
        local = pick - first * prompts
        base = (local // prompts) * 16 + (local % prompts) * depth
        hits = [one_hot(row == base + prompts * depth * odd + tap) for odd in (0, 1) for tap in range(depth)]
        hits = dot_nt(unit, jnp.concatenate(hits, axis=0)).astype(BF16)
        hits = jnp.concatenate(
            [hits[:, i * span_rows : (i + 1) * span_rows] for i in range(2 * depth)], axis=0
        )
        part = jnp.dot(hits, jnp.concatenate(table, axis=0), preferred_element_type=F32)
        tails = part if tails is None else tails + part

    state_ref[...] = states.astype(BF16).reshape(slots, STATE, channels)
    state_copy = pltpu.make_async_copy(state_ref, state_hbm, sems.at[0])
    state_copy.start()
    windows = windows.astype(BF16).reshape(slots, WINDOW // 2, 2 * LANES)
    for upper in range(2):
        for kind in range(2):
            at = upper * LANES + kind * HEAD_DIM
            keyval_ref[:, kind, upper * WINDOW // 2 : (upper + 1) * WINDOW // 2, :] = windows[
                :, :, at : at + HEAD_DIM
            ]
    keyval_copy = pltpu.make_async_copy(keyval_ref, keyval_hbm, sems.at[1])
    keyval_copy.start()
    for odd in range(2):
        for tap in range(depth):
            at = (odd * depth + tap) * wide
            for pair in range(tiles // 2):
                tile = 2 * pair + odd
                conv_ref[tap, :, tile * LANES : (tile + 1) * LANES] = tails[
                    at : at + slots, pair * LANES : (pair + 1) * LANES
                ].astype(BF16)
    conv_copy = pltpu.make_async_copy(conv_ref, conv_hbm, sems.at[2])
    conv_copy.start()
    state_copy.wait()
    keyval_copy.wait()
    conv_copy.wait()


def on_device(
    pr_size,
    tp_size,
    tokens,
    prompt_lengths,
    query_weight,
    key_weight,
    value_weight,
    attention_gain,
    inner_weight,
    conv_weight,
    scan_weight,
    step_weight,
    step_bias,
    mamba_rate,
    mamba_skip,
    mamba_gain,
    request_prompt,
    request_owner,
    request_slot,
):
    rows, width = tokens.shape
    prompts = prompt_lengths.shape[1]
    channels = inner_weight.shape[2]
    features = query_weight.shape[1]
    slots = request_owner.shape[0]
    tiles = channels // LANES

    def shape(dims, dtype=F32):
        return jax.ShapeDtypeStruct(dims, dtype)

    inner = jnp.einsum("td,dgc->gtc", tokens, inner_weight, preferred_element_type=F32)
    inner = inner.astype(BF16)
    partial, mixed = pl.pallas_call(
        functools.partial(mix_kernel, prompts),
        out_shape=(
            shape((DT_RANK + 2 * STATE, rows)),
            shape((rows, channels), BF16),
        ),
        in_specs=[SMEM] + [VMEM] * 3,
        out_specs=(VMEM, VMEM),
        scratch_shapes=[pltpu.VMEM((rows + 8, channels), F32)],
        compiler_params=params(16),
        name="mix",
    )(prompt_lengths, inner, conv_weight, scan_weight.T)

    def swap(x, axis, size, bit):
        return lax.ppermute(x, axis, [(i, i ^ bit) for i in range(size)])

    near = swap(partial, "tp", tp_size, 1)
    spare = (16 - 2 * prompts * (CONV - 1)) * (tiles // 2)
    early_rows = prompts * WINDOW + 8 * tiles + -(-max(pr_size - spare, 0) // 16) * 16
    attended, square, early = pl.pallas_call(
        functools.partial(attend_kernel, prompts),
        out_shape=(
            shape((rows, features)),
            shape((8, rows)),
            shape((early_rows, LANES), BF16),
        ),
        in_specs=[SMEM] + [VMEM] * 8,
        out_specs=(VMEM, VMEM, VMEM),
        scratch_shapes=[
            pltpu.VMEM((8, LANES), jnp.int32),
        ],
        compiler_params=params(16),
        cost_estimate=pl.CostEstimate(
            flops=2 * rows * width * (features + channels), bytes_accessed=4 << 20, transcendentals=0
        ),
        name="attend",
    )(
        prompt_lengths,
        tokens,
        query_weight,
        key_weight.T,
        value_weight.T,
        inner,
        request_prompt[None],
        request_owner[None],
        request_slot[None],
    )
    pair = partial + near
    bit = 2
    while bit < tp_size // 2:
        pair = pair + swap(pair, "tp", tp_size, bit)
        bit *= 2
    far = swap(pair.astype(BF16), "tp", tp_size, bit)

    payload, states_even, states_odd = scan_call(
        prompts,
        prompt_lengths,
        pair,
        far,
        mixed,
        step_weight,
        step_bias[None],
        mamba_rate,
        early,
    )
    gated, sums = pl.pallas_call(
        gate_kernel,
        out_shape=(shape((rows, channels)), shape((2, rows))),
        in_specs=[VMEM] * 8,
        out_specs=(VMEM, VMEM),
        scratch_shapes=[
            pltpu.VMEM((rows, BLOCK * STATE), BF16),
            pltpu.VMEM((rows, channels), F32),
        ],
        compiler_params=params(16),
        cost_estimate=pl.CostEstimate(flops=1 << 24, bytes_accessed=4 << 20, transcendentals=0),
        name="gate",
    )(pair, far, states_even, states_odd, mixed, inner, mamba_skip[None], square)

    me = lax.axis_index("pr").astype(jnp.int32)
    held = payload[None]
    pr_bits = [1 << i for i in reversed(range((pr_size - 1).bit_length()))]
    tp_bits = [1 << i for i in range((tp_size - 1).bit_length())]
    main, last = pr_bits[:-1], pr_bits[-1]
    near, far = list(tp_bits[:-1]), tp_bits[-1]
    for bit in main[:-1]:
        new = swap(held, "pr", pr_size, bit)
        other = swap(sums, "tp", tp_size, near.pop(0)) if near else jnp.zeros_like(sums)
        held, sums = pl.pallas_call(
            join_kernel,
            out_shape=(
                shape((2 * held.shape[0],) + held.shape[1:], BF16),
                shape(sums.shape),
            ),
            in_specs=[VMEM] * 4,
            out_specs=(VMEM, VMEM),
            compiler_params=params(16),
            name="join",
        )(held, new, sums, other)
    for bit in near:
        sums = sums + swap(sums, "tp", tp_size, bit)
    crossed = swap(held, "pr", pr_size, last)
    fresh = swap(held, "pr", pr_size, main[-1])
    other = swap(sums, "tp", tp_size, far)
    fresh, sums = pl.pallas_call(
        hold_kernel,
        out_shape=(shape(fresh.shape, BF16), shape(sums.shape)),
        in_specs=[VMEM] * 3,
        out_specs=(VMEM, VMEM),
        compiler_params=params(16),
        name="hold",
    )(fresh, sums, other)
    pieces = [held, fresh, crossed, swap(fresh, "pr", pr_size, last)]
    attention_out, mamba_out = pl.pallas_call(
        norm_kernel,
        out_shape=(shape((rows, features), BF16), shape((rows, channels), BF16)),
        in_specs=[VMEM] * 5 + [HBM],
        out_specs=(VMEM, VMEM),
        compiler_params=params(16),
        cost_estimate=pl.CostEstimate(flops=1 << 24, bytes_accessed=2 << 20, transcendentals=0),
        name="norm",
    )(attended, gated, sums, attention_gain[None], mamba_gain[None], crossed)
    keyval, state, conv = pl.pallas_call(
        functools.partial(deliver_kernel, prompts, len(pieces)),
        out_shape=(
            shape((slots, 2, WINDOW, HEAD_DIM), BF16),
            shape((slots, STATE, channels), BF16),
            shape((CONV - 1, slots, channels), BF16),
        ),
        in_specs=[SMEM] + [VMEM] * len(pieces),
        out_specs=(HBM, HBM, HBM),
        scratch_shapes=[
            pltpu.VMEM((slots, 2, WINDOW, HEAD_DIM), BF16),
            pltpu.VMEM((slots, STATE, channels), BF16),
            pltpu.VMEM((CONV - 1, slots, channels), BF16),
            pltpu.SemaphoreType.DMA((3,)),
        ],
        compiler_params=params(32),
        name="deliver",
    )(me[None], *pieces)
    return (attention_out, mamba_out, keyval, state, conv.transpose(1, 0, 2))


def solution(mesh):
    return jax.shard_map(
        functools.partial(on_device, mesh.shape["pr"], mesh.shape["tp"]),
        mesh=mesh,
        in_specs=(
            P("pr", None),
            P("pr", None),
            P(None, "tp"),
            P(None, "tp"),
            P(None, "tp"),
            P("tp"),
            P(None, None, "tp"),
            P(None, "tp"),
            P("tp", None),
            P(None, "tp"),
            P("tp"),
            P(None, "tp"),
            P("tp"),
            P("tp"),
            P("pr"),
            P("pr"),
            P("pr"),
        ),
        out_specs=(
            P("pr", "tp"),
            P("pr", "tp"),
            P("pr", None, None, "tp"),
            P("pr", None, "tp"),
            P("pr", None, "tp"),
        ),
        check_vma=False,
    )
```

```python
import functools
import math

import jax
import jax.numpy as jnp
from jax import lax
from jax.experimental import pallas as pl
from jax.experimental.pallas import tpu as pltpu
from jax.sharding import PartitionSpec as P

HEADS = 16
KV_HEADS = 4
HEAD_DIM = 64
INNER = 2048
STATE = 16
DT_RANK = 64
CONV = 4
WINDOW = 32
EPSILON = 1e-06
LANES = 128
BLOCK = 16
PARTS = 2
RESET = 1e30

F32 = jnp.float32
BF16 = jnp.bfloat16
VMEM = pl.BlockSpec(memory_space=pltpu.VMEM)
SMEM = pl.BlockSpec(memory_space=pltpu.SMEM)
HBM = pl.BlockSpec(memory_space=pltpu.HBM)


def params(mib):
    return pltpu.CompilerParams(vmem_limit_bytes=mib << 20)


def dot_nt(a, b):
    return lax.dot_general(a, b, (((1,), (1,)), ((), ())), preferred_element_type=F32)


def bounds(len_ref, prompts):
    starts, ends = [], []
    at = 0
    for p in range(prompts):
        starts.append(at)
        at = at + len_ref[0, p]
        ends.append(at)
    return starts, ends


def first_row_of(position, starts, prompts):
    first = jnp.zeros_like(position)
    for p in range(1, prompts):
        first = jnp.where(position >= starts[p], starts[p], first)
    return first


def last_rows(shape, depth, starts, ends):
    row = lax.broadcasted_iota(jnp.int32, shape, 0)
    position = lax.broadcasted_iota(jnp.int32, shape, 1)
    hit = jnp.zeros(shape, F32)
    for p in range(len(starts)):
        here = (row >= p * depth) & (row < (p + 1) * depth) & (position >= starts[p])
        hit = jnp.where(here & (position - row == ends[p] - (p + 1) * depth), 1.0, hit)
    return hit.astype(BF16)


def row_sums(squares):
    total = squares[:, :LANES]
    for at in range(LANES, squares.shape[1], LANES):
        total = total + squares[:, at : at + LANES]
    return jnp.sum(total.T, axis=0, keepdims=True)


def sigmoid(x):
    return 0.5 * jnp.tanh(0.5 * x) + 0.5


def mix_kernel(
    prompts,
    len_ref,
    inner_ref,
    conv_ref,
    scan_ref,
    partial_ref,
    mixed_ref,
    raw_ref,
):
    _, rows, channels = inner_ref.shape
    starts, _ = bounds(len_ref, prompts)
    raw = inner_ref[0].astype(F32)
    raw_ref[pl.ds(0, 8), :] = jnp.zeros((8, channels), F32)
    raw_ref[pl.ds(8, rows), :] = raw
    position = lax.broadcasted_iota(jnp.int32, (rows, 1), 0)
    offset = position - first_row_of(position, starts, prompts)
    total = raw * conv_ref[CONV - 1 : CONV, :]
    for lag in range(1, CONV):
        shifted = raw_ref[pl.ds(8 - lag, rows), :]
        shifted = jnp.where(offset >= lag, shifted, 0.0)
        total = total + shifted * conv_ref[CONV - 1 - lag : CONV - lag, :]
    mixed = (total * sigmoid(total)).astype(BF16)
    mixed_ref[...] = mixed
    partial_ref[...] = dot_nt(scan_ref[...], mixed)


def attend_kernel(
    prompts,
    len_ref,
    tokens_ref,
    query_ref,
    key_ref,
    value_ref,
    inner_ref,
    prompt_ref,
    owner_ref,
    slot_ref,
    attended_ref,
    square_ref,
    packed_ref,
    request_ref,
):
    rows, width = tokens_ref.shape
    channels = inner_ref.shape[2]
    features = query_ref.shape[1]
    group = features // HEAD_DIM
    starts, ends = bounds(len_ref, prompts)
    tokens = tokens_ref[...]
    queries = jnp.dot(tokens, query_ref[...], preferred_element_type=F32).astype(BF16)
    keys = dot_nt(tokens, jnp.concatenate([key_ref[...]] * group, axis=0)).astype(BF16)
    values = dot_nt(tokens, jnp.concatenate([value_ref[...]] * group, axis=0)).astype(BF16)
    at_row = lax.broadcasted_iota(jnp.int32, (rows, rows), 0)
    at_column = lax.broadcasted_iota(jnp.int32, (rows, rows), 1)
    row_first = first_row_of(at_row, starts, prompts)
    allowed = (at_column <= at_row) & (at_row - at_column < WINDOW) & (at_column >= row_first)
    head_of = lax.broadcasted_iota(jnp.int32, (rows, features), 1) // HEAD_DIM
    zero = jnp.zeros((), BF16)
    attended = jnp.zeros((rows, features), F32)
    for head in range(group):
        mine = head_of == head
        scores = dot_nt(queries, jnp.where(mine, keys, zero)) * HEAD_DIM ** (-0.5)
        scores = jnp.where(allowed, scores, -1e30)
        top = jnp.max(scores, axis=1, keepdims=True)
        expons = jnp.exp(scores - top)
        weights = expons * (1.0 / jnp.sum(expons, axis=1, keepdims=True))
        attended = attended + jnp.dot(
            weights.astype(BF16), jnp.where(mine, values, zero), preferred_element_type=F32
        )
    attended_ref[...] = attended
    square_ref[...] = jnp.broadcast_to(row_sums(attended * attended), square_ref.shape)
    lane = lax.broadcasted_iota(jnp.int32, (rows, LANES), 1)
    both = jnp.where(lane < HEAD_DIM, keys[:, :LANES], values[:, :LANES])
    pick = last_rows((prompts * WINDOW, rows), WINDOW, starts, ends)
    packed_ref[: prompts * WINDOW, :] = jnp.dot(pick, both, preferred_element_type=F32).astype(
        BF16
    )
    requests = owner_ref.shape[1]
    request_ref[...] = jnp.full(request_ref.shape, -1, jnp.int32)
    request_ref[0:1, 0:requests] = owner_ref[...]
    request_ref[1:2, 0:requests] = slot_ref[...]
    request_ref[2:3, 0:requests] = prompt_ref[...]
    depth = prompts * (CONV - 1)
    groups = channels // LANES // 2
    spare = 16 - 2 * depth
    owners = packed_ref.shape[0] - prompts * WINDOW - 16 * groups + spare * groups
    owner = lax.broadcasted_iota(jnp.int32, (owners, LANES), 0) == request_ref[0:1, :]
    slot = lax.broadcasted_iota(jnp.int32, (LANES, LANES), 0) == request_ref[1:2, :]
    number = request_ref[2:3, :] + 1
    filled = dot_nt(
        jnp.where(owner, 1.0, 0.0).astype(BF16),
        jnp.where(slot, number, 0).astype(F32).astype(BF16),
    )
    pick = last_rows((8, rows), CONV - 1, starts, ends)
    tail = jnp.dot(pick, inner_ref[0], preferred_element_type=F32)
    base = prompts * WINDOW
    for group in range(groups):
        at = 2 * group * LANES
        packed_ref[base + 16 * group : base + 16 * (group + 1), :] = jnp.concatenate(
            [
                tail[:depth, at : at + LANES],
                tail[:depth, at + LANES : at + 2 * LANES],
                filled[spare * group : spare * (group + 1), :],
            ],
            axis=0,
        ).astype(BF16)
    if owners > spare * groups:
        packed_ref[base + 16 * groups :, :] = filled[spare * groups :, :].astype(BF16)


def scan_kernel(
    prompts,
    len_ref,
    own_ref,
    other_ref,
    mixed_ref,
    step_weight_ref,
    step_bias_ref,
    rate_ref,
    early_ref,
    payload_ref,
    states_even_ref,
    states_odd_ref,
    decay_ref,
    input_ref,
    in_map_ref,
):
    rows, channels = mixed_ref.shape
    pairs = rows // BLOCK // 2
    starts, ends = bounds(len_ref, prompts)
    projected = own_ref[...] + other_ref[...].astype(F32)
    low = projected[:DT_RANK, :].T.astype(BF16)
    pre = jnp.dot(low, step_weight_ref[...], preferred_element_type=F32) + step_bias_ref[...]
    step = jnp.maximum(pre, 0.0) + jnp.log1p(jnp.exp(-jnp.abs(pre)))
    position = lax.broadcasted_iota(jnp.int32, (rows, 1), 0)
    is_first = position == 0
    for p in range(1, prompts):
        is_first = is_first | (position == starts[p])
    decay_ref[...] = jnp.where(is_first, RESET, step)
    input_ref[...] = step * mixed_ref[...].astype(F32)
    for block in range(rows // BLOCK):
        columns = slice(block * BLOCK, (block + 1) * BLOCK)
        in_map_ref[block, :, 0:BLOCK] = projected[DT_RANK : DT_RANK + STATE, columns]
    rate = rate_ref[...] * (-math.log2(math.e))

    def advance(block, state, states_ref, index):
        at = pl.multiple_of(block * BLOCK, BLOCK)
        for token in range(BLOCK):
            decay = jnp.exp2(decay_ref[pl.ds(at + token, 1), :] * rate)
            entering = in_map_ref[block, :, token : token + 1] * input_ref[pl.ds(at + token, 1), :]
            state = state * decay + entering
            states_ref[index, token * STATE : (token + 1) * STATE, :] = state.astype(BF16)
        return state

    def two_blocks(pair, state):
        state = advance(2 * pair, state, states_even_ref, pair)
        return advance(2 * pair + 1, state, states_odd_ref, pair)

    lax.fori_loop(0, pairs, two_blocks, jnp.zeros((STATE, channels), F32))
    for p in range(prompts):
        last = ends[p] - 1
        block = last // BLOCK
        at = pl.multiple_of((last - block * BLOCK) * STATE, STATE)
        final = jnp.where(
            block % 2 == 0,
            states_even_ref[block // 2, pl.ds(at, STATE), :],
            states_odd_ref[block // 2, pl.ds(at, STATE), :],
        )
        for tile in range(channels // LANES):
            at = (p * (channels // LANES) + tile) * STATE
            payload_ref[at : at + STATE, :] = final[:, tile * LANES : (tile + 1) * LANES]
    base = prompts * channels // LANES * STATE
    payload_ref[base:, :] = early_ref[...]


def scan_call(prompts, lengths, own, other, mixed, *rest):
    rows, channels = mixed.shape
    tiles = channels // LANES
    payload_rows = prompts * tiles * STATE + rest[-1].shape[0]
    states = jax.ShapeDtypeStruct((rows // BLOCK // 2, BLOCK * STATE, channels), BF16)
    return pl.pallas_call(
        functools.partial(scan_kernel, prompts),
        out_shape=(jax.ShapeDtypeStruct((payload_rows, LANES), BF16), states, states),
        in_specs=[SMEM] + [VMEM] * 7,
        out_specs=(VMEM,) * 3,
        scratch_shapes=[
            pltpu.VMEM((rows, channels), F32),
            pltpu.VMEM((rows, channels), F32),
            pltpu.VMEM((rows // BLOCK, STATE, LANES), F32),
        ],
        compiler_params=params(16),
        name="scan",
    )(lengths, own, other, mixed, *rest)


def gate_kernel(
    own_ref,
    other_ref,
    states_even_ref,
    states_odd_ref,
    mixed_ref,
    inner_ref,
    skip_ref,
    square_ref,
    gated_ref,
    sums_ref,
    out_map_ref,
    scanned_ref,
):
    rows, channels = mixed_ref.shape
    span = BLOCK * STATE
    maps = slice(DT_RANK + STATE, DT_RANK + 2 * STATE)
    out_map = own_ref[maps, :] + other_ref[maps, :].astype(F32)
    row = lax.broadcasted_iota(jnp.int32, (STATE, span), 0)
    column = lax.broadcasted_iota(jnp.int32, (STATE, span), 1)
    tiled = jnp.dot(
        out_map.T.astype(BF16),
        jnp.where(column % STATE == row, 1.0, 0.0).astype(BF16),
        preferred_element_type=F32,
    )
    row = lax.broadcasted_iota(jnp.int32, (rows, span), 0)
    column = lax.broadcasted_iota(jnp.int32, (rows, span), 1)
    out_map_ref[...] = jnp.where(column // STATE == row % BLOCK, tiled, 0.0).astype(BF16)
    for block in range(rows // BLOCK):
        states_ref = states_odd_ref if block % 2 else states_even_ref
        at = slice(block * BLOCK, (block + 1) * BLOCK)
        scanned_ref[at, :] = jnp.dot(
            out_map_ref[at, :], states_ref[block // 2], preferred_element_type=F32
        )
    gate = inner_ref[1].astype(F32)
    gated = (scanned_ref[...] + skip_ref[...] * mixed_ref[...].astype(F32)) * (
        gate * sigmoid(gate)
    )
    gated_ref[...] = gated
    sums_ref[0:1, :] = square_ref[0:1, :]
    sums_ref[1:2, :] = row_sums(gated * gated)


def join_kernel(held_ref, new_ref, own_ref, other_ref, joined_ref, sums_ref):
    count = held_ref.shape[0]
    joined_ref[:count] = held_ref[...]
    joined_ref[count:] = new_ref[...]
    sums_ref[...] = own_ref[...] + other_ref[...]


def hold_kernel(new_ref, own_ref, other_ref, fresh_ref, sums_ref):
    fresh_ref[...] = new_ref[...]
    sums_ref[...] = own_ref[...] + other_ref[...]


def norm_kernel(
    attended_ref,
    gated_ref,
    sums_ref,
    attention_gain_ref,
    mamba_gain_ref,
    crossed_hbm,
    inner_hbm,
    attention_ref,
    mamba_ref,
):
    sums = sums_ref[...]
    sums = jnp.concatenate([sums, jnp.zeros((6, sums.shape[1]), F32)], axis=0).T
    attention_scale = lax.rsqrt(sums[:, 0:1] / (HEADS * HEAD_DIM) + EPSILON)
    attention_ref[...] = (attended_ref[...] * attention_scale * attention_gain_ref[...]).astype(
        BF16
    )
    mamba_scale = lax.rsqrt(sums[:, 1:2] / INNER + EPSILON)
    mamba_ref[...] = (gated_ref[...] * mamba_scale * mamba_gain_ref[...]).astype(BF16)


def one_hot(hit):
    return jnp.where(hit, 1.0, 0.0).astype(BF16)


def deliver_kernel(
    prompts,
    pieces,
    me_ref,
    *refs,
):
    keyval_hbm, state_hbm, conv_hbm, keyval_ref, state_ref, conv_ref, sems = refs[pieces:]
    me = me_ref[0]
    slots, _, channels = state_ref.shape
    tiles = channels // LANES
    blocks = [(ref, index) for ref in refs[:pieces] for index in range(ref.shape[0])]
    sources = len(blocks)
    window_at = prompts * tiles * STATE
    tail_at = window_at + prompts * WINDOW
    depth = CONV - 1
    spare = 16 - 2 * prompts * depth
    table_rows = refs[0].shape[1] - tail_at

    def rows_of(source, at, size):
        ref, index = blocks[source]
        return ref[index, at : at + size, :]

    row = lax.broadcasted_iota(jnp.int32, (table_rows, LANES), 0)
    grouped = row < 8 * tiles
    owner = jnp.where(
        grouped, row // 16 * spare + row % 16 - (16 - spare), row - 8 * tiles + spare * (tiles // 2)
    )
    owner = jnp.where(grouped & (row % 16 < 16 - spare), -1, owner)
    pick = jnp.zeros((1, LANES), F32)
    for source in range(sources):
        filled = rows_of(source, tail_at, table_rows).astype(F32)
        filled = jnp.sum(jnp.where(owner == me, filled, 0.0), axis=0, keepdims=True)
        pick = pick + jnp.where(filled > 0.5, filled + float(source * prompts - 1), 0.0)
    pick = pick.astype(jnp.int32)

    span = sources * prompts * STATE
    wanted = one_hot(lax.broadcasted_iota(jnp.int32, (span, LANES), 0) // STATE == pick)
    states, windows, tails = [], [], []
    for source in range(sources):
        for p in range(prompts):
            at = p * tiles * STATE
            states.append(
                jnp.concatenate(
                    [rows_of(source, at + tile * STATE, STATE) for tile in range(tiles)], axis=1
                )
            )
            at = window_at + p * WINDOW
            windows.append(
                jnp.concatenate(
                    [
                        rows_of(source, at, WINDOW // 2),
                        rows_of(source, at + WINDOW // 2, WINDOW // 2),
                    ],
                    axis=1,
                )
            )
        tails.append(
            jnp.concatenate(
                [rows_of(source, tail_at + 8 * tile, 16) for tile in range(0, tiles, 2)], axis=1
            )
        )
    states = jnp.concatenate(states, axis=0)
    windows = jnp.concatenate(windows, axis=0)
    part = slots // PARTS
    picked = part * STATE
    row = lax.broadcasted_iota(jnp.int32, (picked, LANES), 0)
    lane = lax.broadcasted_iota(jnp.int32, (picked, LANES), 1)
    slot_of = row // STATE - lane
    row = lax.broadcasted_iota(jnp.int32, (picked, span), 0)
    lane = lax.broadcasted_iota(jnp.int32, (picked, span), 1)
    same = row % STATE == lane % STATE
    copies = []

    def send(source_ref, target_ref):
        copies.append(pltpu.make_async_copy(source_ref, target_ref, sems.at[len(copies)]))
        copies[-1].start()

    for first in range(0, slots, part):
        here = slice(first, first + part)
        take = dot_nt(one_hot(slot_of == -first), wanted)
        take = jnp.where(same, take, 0.0).astype(BF16)
        moved = jnp.dot(take, states, preferred_element_type=F32)
        state_ref[here] = moved.astype(BF16).reshape(part, STATE, channels)
        send(state_ref.at[here], state_hbm.at[here])
        moved = jnp.dot(take, windows, preferred_element_type=F32)
        moved = moved.astype(BF16).reshape(part, WINDOW // 2, 2 * LANES)
        for upper in range(2):
            for kind in range(2):
                at = upper * LANES + kind * HEAD_DIM
                keyval_ref[here, kind, upper * WINDOW // 2 : (upper + 1) * WINDOW // 2, :] = moved[
                    :, :, at : at + HEAD_DIM
                ]
        send(keyval_ref.at[here], keyval_hbm.at[here])

    wide = -(-slots // 16) * 16
    row = lax.broadcasted_iota(jnp.int32, (wide, LANES), 0)
    lane = lax.broadcasted_iota(jnp.int32, (wide, LANES), 1)
    unit = one_hot(row == lane)
    span = sources * 16
    row = lax.broadcasted_iota(jnp.int32, (span, LANES), 0)
    base = (pick // prompts) * 16 + (pick % prompts) * depth
    hits = [
        one_hot(row == base + prompts * depth * odd + tap) for odd in (0, 1) for tap in range(depth)
    ]
    hits = dot_nt(unit, jnp.concatenate(hits, axis=0)).astype(BF16)
    hits = jnp.concatenate([hits[:, i * span : (i + 1) * span] for i in range(2 * depth)], axis=0)
    moved = jnp.dot(hits, jnp.concatenate(tails, axis=0), preferred_element_type=F32)
    for odd in range(2):
        for tap in range(depth):
            at = (odd * depth + tap) * wide
            for pair in range(tiles // 2):
                tile = 2 * pair + odd
                conv_ref[tap, :, tile * LANES : (tile + 1) * LANES] = moved[
                    at : at + slots, pair * LANES : (pair + 1) * LANES
                ].astype(BF16)
    send(conv_ref, conv_hbm)
    for copy in copies:
        copy.wait()


def on_device(
    pr_size,
    tp_size,
    tokens,
    prompt_lengths,
    query_weight,
    key_weight,
    value_weight,
    attention_gain,
    inner_weight,
    conv_weight,
    scan_weight,
    step_weight,
    step_bias,
    mamba_rate,
    mamba_skip,
    mamba_gain,
    request_prompt,
    request_owner,
    request_slot,
):
    rows, width = tokens.shape
    prompts = prompt_lengths.shape[1]
    channels = inner_weight.shape[2]
    features = query_weight.shape[1]
    slots = request_owner.shape[0]
    tiles = channels // LANES

    def shape(dims, dtype=F32):
        return jax.ShapeDtypeStruct(dims, dtype)

    inner = jnp.einsum("td,dgc->gtc", tokens, inner_weight, preferred_element_type=F32)
    inner = inner.astype(BF16)
    partial, mixed = pl.pallas_call(
        functools.partial(mix_kernel, prompts),
        out_shape=(
            shape((DT_RANK + 2 * STATE, rows)),
            shape((rows, channels), BF16),
        ),
        in_specs=[SMEM] + [VMEM] * 3,
        out_specs=(VMEM, VMEM),
        scratch_shapes=[pltpu.VMEM((rows + 8, channels), F32)],
        compiler_params=params(16),
        name="mix",
    )(prompt_lengths, inner, conv_weight, scan_weight.T)

    def swap(x, axis, size, bit):
        return lax.ppermute(x, axis, [(i, i ^ bit) for i in range(size)])

    near = swap(partial, "tp", tp_size, 1)
    spare = (16 - 2 * prompts * (CONV - 1)) * (tiles // 2)
    early_rows = prompts * WINDOW + 8 * tiles + -(-max(pr_size - spare, 0) // 16) * 16
    attended, square, early = pl.pallas_call(
        functools.partial(attend_kernel, prompts),
        out_shape=(
            shape((rows, features)),
            shape((8, rows)),
            shape((early_rows, LANES), BF16),
        ),
        in_specs=[SMEM] + [VMEM] * 8,
        out_specs=(VMEM, VMEM, VMEM),
        scratch_shapes=[
            pltpu.VMEM((8, LANES), jnp.int32),
        ],
        compiler_params=params(16),
        cost_estimate=pl.CostEstimate(
            flops=2 * rows * width * (features + channels), bytes_accessed=4 << 20, transcendentals=0
        ),
        name="attend",
    )(
        prompt_lengths,
        tokens,
        query_weight,
        key_weight.T,
        value_weight.T,
        inner,
        request_prompt[None],
        request_owner[None],
        request_slot[None],
    )
    pair = partial + near
    bit = 2
    while bit < tp_size // 2:
        pair = pair + swap(pair, "tp", tp_size, bit)
        bit *= 2
    far = swap(pair.astype(BF16), "tp", tp_size, bit)

    payload, states_even, states_odd = scan_call(
        prompts,
        prompt_lengths,
        pair,
        far,
        mixed,
        step_weight,
        step_bias[None],
        mamba_rate,
        early,
    )
    gated, sums = pl.pallas_call(
        gate_kernel,
        out_shape=(shape((rows, channels)), shape((2, rows))),
        in_specs=[VMEM] * 8,
        out_specs=(VMEM, VMEM),
        scratch_shapes=[
            pltpu.VMEM((rows, BLOCK * STATE), BF16),
            pltpu.VMEM((rows, channels), F32),
        ],
        compiler_params=params(16),
        cost_estimate=pl.CostEstimate(flops=1 << 24, bytes_accessed=4 << 20, transcendentals=0),
        name="gate",
    )(pair, far, states_even, states_odd, mixed, inner, mamba_skip[None], square)

    me = lax.axis_index("pr").astype(jnp.int32)
    held = payload[None]
    pr_bits = [1 << i for i in reversed(range((pr_size - 1).bit_length()))]
    tp_bits = [1 << i for i in range((tp_size - 1).bit_length())]
    main, last = pr_bits[:-1], pr_bits[-1]
    near, far = list(tp_bits[:-1]), tp_bits[-1]
    for bit in main[:-1]:
        new = swap(held, "pr", pr_size, bit)
        other = swap(sums, "tp", tp_size, near.pop(0)) if near else jnp.zeros_like(sums)
        held, sums = pl.pallas_call(
            join_kernel,
            out_shape=(
                shape((2 * held.shape[0],) + held.shape[1:], BF16),
                shape(sums.shape),
            ),
            in_specs=[VMEM] * 4,
            out_specs=(VMEM, VMEM),
            compiler_params=params(16),
            name="join",
        )(held, new, sums, other)
    for bit in near:
        sums = sums + swap(sums, "tp", tp_size, bit)
    crossed = swap(held, "pr", pr_size, last)
    fresh = swap(held, "pr", pr_size, main[-1])
    other = swap(sums, "tp", tp_size, far)
    fresh, sums = pl.pallas_call(
        hold_kernel,
        out_shape=(shape(fresh.shape, BF16), shape(sums.shape)),
        in_specs=[VMEM] * 3,
        out_specs=(VMEM, VMEM),
        compiler_params=params(16),
        name="hold",
    )(fresh, sums, other)
    pieces = [held, fresh, crossed, swap(fresh, "pr", pr_size, last)]
    attention_out, mamba_out = pl.pallas_call(
        norm_kernel,
        out_shape=(shape((rows, features), BF16), shape((rows, channels), BF16)),
        in_specs=[VMEM] * 5 + [HBM] * 2,
        out_specs=(VMEM, VMEM),
        compiler_params=params(16),
        cost_estimate=pl.CostEstimate(flops=1 << 24, bytes_accessed=2 << 20, transcendentals=0),
        name="norm",
    )(attended, gated, sums, attention_gain[None], mamba_gain[None], crossed, inner_weight)
    keyval, state, conv = pl.pallas_call(
        functools.partial(deliver_kernel, prompts, len(pieces)),
        out_shape=(
            shape((slots, 2, WINDOW, HEAD_DIM), BF16),
            shape((slots, STATE, channels), BF16),
            shape((CONV - 1, slots, channels), BF16),
        ),
        in_specs=[SMEM] + [VMEM] * len(pieces),
        out_specs=(HBM, HBM, HBM),
        scratch_shapes=[
            pltpu.VMEM((slots, 2, WINDOW, HEAD_DIM), BF16),
            pltpu.VMEM((slots, STATE, channels), BF16),
            pltpu.VMEM((CONV - 1, slots, channels), BF16),
            pltpu.SemaphoreType.DMA((2 * PARTS + 1,)),
        ],
        compiler_params=params(32),
        name="deliver",
    )(me[None], *pieces)
    return (attention_out, mamba_out, keyval, state, conv.transpose(1, 0, 2))


def solution(mesh):
    return jax.shard_map(
        functools.partial(on_device, mesh.shape["pr"], mesh.shape["tp"]),
        mesh=mesh,
        in_specs=(
            P("pr", None),
            P("pr", None),
            P(None, "tp"),
            P(None, "tp"),
            P(None, "tp"),
            P("tp"),
            P(None, None, "tp"),
            P(None, "tp"),
            P("tp", None),
            P(None, "tp"),
            P("tp"),
            P(None, "tp"),
            P("tp"),
            P("tp"),
            P("pr"),
            P("pr"),
            P("pr"),
        ),
        out_specs=(
            P("pr", "tp"),
            P("pr", "tp"),
            P("pr", None, None, "tp"),
            P("pr", None, "tp"),
            P("pr", None, "tp"),
        ),
        check_vma=False,
    )
```

```python
import functools
import math

import jax
import jax.numpy as jnp
from jax import lax
from jax.experimental import pallas as pl
from jax.experimental.pallas import tpu as pltpu
from jax.sharding import PartitionSpec as P

HEADS = 16
KV_HEADS = 4
HEAD_DIM = 64
INNER = 2048
STATE = 16
DT_RANK = 64
CONV = 4
WINDOW = 32
EPSILON = 1e-06
LANES = 128
BLOCK = 16
PARTS = 2
RESET = 1e30

F32 = jnp.float32
BF16 = jnp.bfloat16
VMEM = pl.BlockSpec(memory_space=pltpu.VMEM)
SMEM = pl.BlockSpec(memory_space=pltpu.SMEM)
HBM = pl.BlockSpec(memory_space=pltpu.HBM)


def params(mib):
    return pltpu.CompilerParams(vmem_limit_bytes=mib << 20)


def dot_nt(a, b):
    return lax.dot_general(a, b, (((1,), (1,)), ((), ())), preferred_element_type=F32)


def bounds(len_ref, prompts):
    starts, ends = [], []
    at = 0
    for p in range(prompts):
        starts.append(at)
        at = at + len_ref[0, p]
        ends.append(at)
    return starts, ends


def first_row_of(position, starts, prompts):
    first = jnp.zeros_like(position)
    for p in range(1, prompts):
        first = jnp.where(position >= starts[p], starts[p], first)
    return first


def last_rows(shape, depth, starts, ends):
    row = lax.broadcasted_iota(jnp.int32, shape, 0)
    position = lax.broadcasted_iota(jnp.int32, shape, 1)
    hit = jnp.zeros(shape, F32)
    for p in range(len(starts)):
        here = (row >= p * depth) & (row < (p + 1) * depth) & (position >= starts[p])
        hit = jnp.where(here & (position - row == ends[p] - (p + 1) * depth), 1.0, hit)
    return hit.astype(BF16)


def row_sums(squares):
    total = squares[:, :LANES]
    for at in range(LANES, squares.shape[1], LANES):
        total = total + squares[:, at : at + LANES]
    return jnp.sum(total.T, axis=0, keepdims=True)


def sigmoid(x):
    return 0.5 * jnp.tanh(0.5 * x) + 0.5


def mix_kernel(
    prompts,
    len_ref,
    inner_ref,
    conv_ref,
    scan_ref,
    partial_ref,
    mixed_ref,
    raw_ref,
):
    _, rows, channels = inner_ref.shape
    starts, _ = bounds(len_ref, prompts)
    raw = inner_ref[0].astype(F32)
    raw_ref[pl.ds(0, 8), :] = jnp.zeros((8, channels), F32)
    raw_ref[pl.ds(8, rows), :] = raw
    position = lax.broadcasted_iota(jnp.int32, (rows, 1), 0)
    offset = position - first_row_of(position, starts, prompts)
    total = raw * conv_ref[CONV - 1 : CONV, :]
    for lag in range(1, CONV):
        shifted = raw_ref[pl.ds(8 - lag, rows), :]
        shifted = jnp.where(offset >= lag, shifted, 0.0)
        total = total + shifted * conv_ref[CONV - 1 - lag : CONV - lag, :]
    mixed = (total * sigmoid(total)).astype(BF16)
    mixed_ref[...] = mixed
    partial_ref[...] = dot_nt(scan_ref[...], mixed)


def attend_kernel(
    prompts,
    len_ref,
    tokens_ref,
    query_ref,
    key_ref,
    value_ref,
    inner_ref,
    prompt_ref,
    owner_ref,
    slot_ref,
    attended_ref,
    square_ref,
    packed_ref,
    request_ref,
):
    rows, width = tokens_ref.shape
    channels = inner_ref.shape[2]
    features = query_ref.shape[1]
    group = features // HEAD_DIM
    starts, ends = bounds(len_ref, prompts)
    tokens = tokens_ref[...]
    queries = jnp.dot(tokens, query_ref[...], preferred_element_type=F32).astype(BF16)
    keys = dot_nt(tokens, jnp.concatenate([key_ref[...]] * group, axis=0)).astype(BF16)
    values = dot_nt(tokens, jnp.concatenate([value_ref[...]] * group, axis=0)).astype(BF16)
    at_row = lax.broadcasted_iota(jnp.int32, (rows, rows), 0)
    at_column = lax.broadcasted_iota(jnp.int32, (rows, rows), 1)
    row_first = first_row_of(at_row, starts, prompts)
    allowed = (at_column <= at_row) & (at_row - at_column < WINDOW) & (at_column >= row_first)
    head_of = lax.broadcasted_iota(jnp.int32, (rows, features), 1) // HEAD_DIM
    zero = jnp.zeros((), BF16)
    attended = jnp.zeros((rows, features), F32)
    for head in range(group):
        mine = head_of == head
        scores = dot_nt(queries, jnp.where(mine, keys, zero)) * HEAD_DIM ** (-0.5)
        scores = jnp.where(allowed, scores, -1e30)
        top = jnp.max(scores, axis=1, keepdims=True)
        expons = jnp.exp(scores - top)
        weights = expons * (1.0 / jnp.sum(expons, axis=1, keepdims=True))
        attended = attended + jnp.dot(
            weights.astype(BF16), jnp.where(mine, values, zero), preferred_element_type=F32
        )
    attended_ref[...] = attended
    square_ref[...] = jnp.broadcast_to(row_sums(attended * attended), square_ref.shape)
    lane = lax.broadcasted_iota(jnp.int32, (rows, LANES), 1)
    both = jnp.where(lane < HEAD_DIM, keys[:, :LANES], values[:, :LANES])
    pick = last_rows((prompts * WINDOW, rows), WINDOW, starts, ends)
    packed_ref[: prompts * WINDOW, :] = jnp.dot(pick, both, preferred_element_type=F32).astype(
        BF16
    )
    requests = owner_ref.shape[1]
    request_ref[...] = jnp.full(request_ref.shape, -1, jnp.int32)
    request_ref[0:1, 0:requests] = owner_ref[...]
    request_ref[1:2, 0:requests] = slot_ref[...]
    request_ref[2:3, 0:requests] = prompt_ref[...]
    depth = prompts * (CONV - 1)
    groups = channels // LANES // 2
    spare = 16 - 2 * depth
    owners = packed_ref.shape[0] - prompts * WINDOW - 16 * groups + spare * groups
    owner = lax.broadcasted_iota(jnp.int32, (owners, LANES), 0) == request_ref[0:1, :]
    slot = lax.broadcasted_iota(jnp.int32, (LANES, LANES), 0) == request_ref[1:2, :]
    number = request_ref[2:3, :] + 1
    filled = dot_nt(
        jnp.where(owner, 1.0, 0.0).astype(BF16),
        jnp.where(slot, number, 0).astype(F32).astype(BF16),
    )
    pick = last_rows((8, rows), CONV - 1, starts, ends)
    tail = jnp.dot(pick, inner_ref[0], preferred_element_type=F32)
    base = prompts * WINDOW
    for group in range(groups):
        at = 2 * group * LANES
        packed_ref[base + 16 * group : base + 16 * (group + 1), :] = jnp.concatenate(
            [
                tail[:depth, at : at + LANES],
                tail[:depth, at + LANES : at + 2 * LANES],
                filled[spare * group : spare * (group + 1), :],
            ],
            axis=0,
        ).astype(BF16)
    if owners > spare * groups:
        packed_ref[base + 16 * groups :, :] = filled[spare * groups :, :].astype(BF16)


def scan_kernel(
    prompts,
    len_ref,
    own_ref,
    other_ref,
    mixed_ref,
    step_weight_ref,
    step_bias_ref,
    rate_ref,
    early_ref,
    payload_ref,
    states_even_ref,
    states_odd_ref,
    decay_ref,
    input_ref,
    in_map_ref,
):
    rows, channels = mixed_ref.shape
    pairs = rows // BLOCK // 2
    starts, ends = bounds(len_ref, prompts)
    projected = own_ref[...] + other_ref[...].astype(F32)
    low = projected[:DT_RANK, :].T.astype(BF16)
    pre = jnp.dot(low, step_weight_ref[...], preferred_element_type=F32) + step_bias_ref[...]
    step = jnp.maximum(pre, 0.0) + jnp.log1p(jnp.exp(-jnp.abs(pre)))
    position = lax.broadcasted_iota(jnp.int32, (rows, 1), 0)
    is_first = position == 0
    for p in range(1, prompts):
        is_first = is_first | (position == starts[p])
    decay_ref[...] = jnp.where(is_first, RESET, step)
    input_ref[...] = step * mixed_ref[...].astype(F32)
    for block in range(rows // BLOCK):
        columns = slice(block * BLOCK, (block + 1) * BLOCK)
        in_map_ref[block, :, 0:BLOCK] = projected[DT_RANK : DT_RANK + STATE, columns]
    rate = rate_ref[...] * (-math.log2(math.e))

    def advance(block, state, states_ref, index):
        at = pl.multiple_of(block * BLOCK, BLOCK)
        for token in range(BLOCK):
            decay = jnp.exp2(decay_ref[pl.ds(at + token, 1), :] * rate)
            entering = in_map_ref[block, :, token : token + 1] * input_ref[pl.ds(at + token, 1), :]
            state = state * decay + entering
            states_ref[index, token * STATE : (token + 1) * STATE, :] = state.astype(BF16)
        return state

    def two_blocks(pair, state):
        state = advance(2 * pair, state, states_even_ref, pair)
        return advance(2 * pair + 1, state, states_odd_ref, pair)

    lax.fori_loop(0, pairs, two_blocks, jnp.zeros((STATE, channels), F32))
    for p in range(prompts):
        last = ends[p] - 1
        block = last // BLOCK
        at = pl.multiple_of((last - block * BLOCK) * STATE, STATE)
        final = jnp.where(
            block % 2 == 0,
            states_even_ref[block // 2, pl.ds(at, STATE), :],
            states_odd_ref[block // 2, pl.ds(at, STATE), :],
        )
        for tile in range(channels // LANES):
            at = (p * (channels // LANES) + tile) * STATE
            payload_ref[at : at + STATE, :] = final[:, tile * LANES : (tile + 1) * LANES]
    base = prompts * channels // LANES * STATE
    payload_ref[base:, :] = early_ref[...]


def scan_call(prompts, lengths, own, other, mixed, *rest):
    rows, channels = mixed.shape
    tiles = channels // LANES
    payload_rows = prompts * tiles * STATE + rest[-1].shape[0]
    states = jax.ShapeDtypeStruct((rows // BLOCK // 2, BLOCK * STATE, channels), BF16)
    return pl.pallas_call(
        functools.partial(scan_kernel, prompts),
        out_shape=(jax.ShapeDtypeStruct((payload_rows, LANES), BF16), states, states),
        in_specs=[SMEM] + [VMEM] * 7,
        out_specs=(VMEM,) * 3,
        scratch_shapes=[
            pltpu.VMEM((rows, channels), F32),
            pltpu.VMEM((rows, channels), F32),
            pltpu.VMEM((rows // BLOCK, STATE, LANES), F32),
        ],
        compiler_params=params(16),
        name="scan",
    )(lengths, own, other, mixed, *rest)


def gate_kernel(
    own_ref,
    other_ref,
    states_even_ref,
    states_odd_ref,
    mixed_ref,
    inner_ref,
    skip_ref,
    square_ref,
    gated_ref,
    sums_ref,
    out_map_ref,
    scanned_ref,
):
    rows, channels = mixed_ref.shape
    span = BLOCK * STATE
    maps = slice(DT_RANK + STATE, DT_RANK + 2 * STATE)
    out_map = own_ref[maps, :] + other_ref[maps, :].astype(F32)
    row = lax.broadcasted_iota(jnp.int32, (STATE, span), 0)
    column = lax.broadcasted_iota(jnp.int32, (STATE, span), 1)
    tiled = jnp.dot(
        out_map.T.astype(BF16),
        jnp.where(column % STATE == row, 1.0, 0.0).astype(BF16),
        preferred_element_type=F32,
    )
    row = lax.broadcasted_iota(jnp.int32, (rows, span), 0)
    column = lax.broadcasted_iota(jnp.int32, (rows, span), 1)
    out_map_ref[...] = jnp.where(column // STATE == row % BLOCK, tiled, 0.0).astype(BF16)
    for block in range(rows // BLOCK):
        states_ref = states_odd_ref if block % 2 else states_even_ref
        at = slice(block * BLOCK, (block + 1) * BLOCK)
        scanned_ref[at, :] = jnp.dot(
            out_map_ref[at, :], states_ref[block // 2], preferred_element_type=F32
        )
    gate = inner_ref[1].astype(F32)
    gated = (scanned_ref[...] + skip_ref[...] * mixed_ref[...].astype(F32)) * (
        gate * sigmoid(gate)
    )
    gated_ref[...] = gated
    sums_ref[0:1, :] = square_ref[0:1, :]
    sums_ref[1:2, :] = row_sums(gated * gated)


def join_kernel(held_ref, new_ref, own_ref, other_ref, joined_ref, sums_ref):
    count = held_ref.shape[0]
    joined_ref[:count] = held_ref[...]
    joined_ref[count:] = new_ref[...]
    sums_ref[...] = own_ref[...] + other_ref[...]


def hold_kernel(new_ref, own_ref, other_ref, fresh_ref, sums_ref):
    fresh_ref[...] = new_ref[...]
    sums_ref[...] = own_ref[...] + other_ref[...]


def norm_kernel(
    attended_ref,
    gated_ref,
    sums_ref,
    attention_gain_ref,
    mamba_gain_ref,
    inner_hbm,
    crossed_hbm,
    collected_hbm,
    attention_ref,
    mamba_ref,
):
    sums = sums_ref[...]
    sums = jnp.concatenate([sums, jnp.zeros((6, sums.shape[1]), F32)], axis=0).T
    attention_scale = lax.rsqrt(sums[:, 0:1] / (HEADS * HEAD_DIM) + EPSILON)
    attention_ref[...] = (attended_ref[...] * attention_scale * attention_gain_ref[...]).astype(
        BF16
    )
    mamba_scale = lax.rsqrt(sums[:, 1:2] / INNER + EPSILON)
    mamba_ref[...] = (gated_ref[...] * mamba_scale * mamba_gain_ref[...]).astype(BF16)


def one_hot(hit):
    return jnp.where(hit, 1.0, 0.0).astype(BF16)


class Gathered:
    def __init__(self, prompts, tiles, refs, me):
        self.blocks = [(ref, index) for ref in refs for index in range(ref.shape[0])]
        self.prompts, self.tiles = prompts, tiles
        self.window_at = prompts * tiles * STATE
        self.tail_at = self.window_at + prompts * WINDOW
        self.depth = CONV - 1
        spare = 16 - 2 * prompts * self.depth
        rows = refs[0].shape[1] - self.tail_at
        row = lax.broadcasted_iota(jnp.int32, (rows, LANES), 0)
        grouped = row < 8 * tiles
        owner = jnp.where(
            grouped, row // 16 * spare + row % 16 - (16 - spare), row - 8 * tiles + spare * (tiles // 2)
        )
        owner = jnp.where(grouped & (row % 16 < 16 - spare), -1, owner)
        pick = jnp.full((1, LANES), -1.0, F32)
        for source in range(len(self.blocks)):
            filled = self.rows_of(source, self.tail_at, rows).astype(F32)
            filled = jnp.sum(jnp.where(owner == me, filled, 0.0), axis=0, keepdims=True)
            pick = jnp.where(filled > 0.5, filled + float(source * prompts - 1), pick)
        self.pick = pick.astype(jnp.int32)
        span = len(self.blocks) * prompts * STATE
        row = lax.broadcasted_iota(jnp.int32, (span, LANES), 0)
        self.wanted = one_hot(row // STATE == self.pick)

    def rows_of(self, source, at, size):
        ref, index = self.blocks[source]
        return ref[index, at : at + size, :]

    def take(self, first, count):
        row = lax.broadcasted_iota(jnp.int32, (count * STATE, LANES), 0)
        lane = lax.broadcasted_iota(jnp.int32, (count * STATE, LANES), 1)
        take = dot_nt(one_hot(row // STATE + first == lane), self.wanted)
        row = lax.broadcasted_iota(jnp.int32, take.shape, 0)
        lane = lax.broadcasted_iota(jnp.int32, take.shape, 1)
        return jnp.where(row % STATE == lane % STATE, take, 0.0).astype(BF16)

    def table(self, rows_list):
        rows = []
        for source in range(len(self.blocks)):
            for p in range(self.prompts):
                parts = [self.rows_of(source, at, 16) for at in rows_list(p)]
                rows.append(jnp.concatenate(parts, axis=1))
        return jnp.concatenate(rows, axis=0)

    def states(self):
        return self.table(lambda p: [(p * self.tiles + i) * STATE for i in range(self.tiles)])

    def windows(self):
        return self.table(
            lambda p: [self.window_at + p * WINDOW + i for i in range(0, WINDOW, 16)]
        )

    def tails(self, slots):
        table = [
            jnp.concatenate(
                [self.rows_of(source, self.tail_at + 8 * i, 16) for i in range(0, self.tiles, 2)],
                axis=1,
            )
            for source in range(len(self.blocks))
        ]
        row = lax.broadcasted_iota(jnp.int32, (slots, LANES), 0)
        lane = lax.broadcasted_iota(jnp.int32, (slots, LANES), 1)
        unit = one_hot(row == lane)
        span = max(len(self.blocks) * 16, LANES)
        if span > len(self.blocks) * 16:
            table.append(jnp.zeros((span - len(self.blocks) * 16, table[0].shape[1]), BF16))
        row = lax.broadcasted_iota(jnp.int32, (span, LANES), 0)
        step = self.prompts * self.depth
        base = (self.pick // self.prompts) * 16 + (self.pick % self.prompts) * self.depth
        base = jnp.where(self.pick < 0, -span, base)
        hits = [one_hot(row == base + step * odd + tap) for odd in (0, 1) for tap in range(self.depth)]
        hits = dot_nt(unit, jnp.concatenate(hits, axis=0)).astype(BF16)
        hits = [hits[:, i * span : (i + 1) * span] for i in range(2 * self.depth)]
        return jnp.dot(
            jnp.concatenate(hits, axis=0),
            jnp.concatenate(table, axis=0),
            preferred_element_type=F32,
        )


def collect_kernel(prompts, slots, me_ref, *refs):
    states_ref, windows_ref, tails_ref = refs[-3:]
    channels = states_ref.shape[1]
    gathered = Gathered(prompts, channels // LANES, refs[:-3], me_ref[0])
    take = gathered.take(0, slots)
    states_ref[...] = jnp.dot(
        take, gathered.states(), preferred_element_type=F32
    ).astype(BF16)
    windows_ref[...] = jnp.dot(
        take, gathered.windows(), preferred_element_type=F32
    ).astype(BF16)
    wide = tails_ref.shape[0] // (2 * (CONV - 1))
    tails_ref[...] = gathered.tails(wide).astype(BF16)


def deliver_kernel(prompts, pieces, me_ref, states_ref, windows_ref, tails_ref, *refs):
    keyval_hbm, state_hbm, conv_ref, keyval_ref, state_ref, sems = refs[pieces:]
    slots, _, channels = state_ref.shape
    tiles = channels // LANES
    gathered = Gathered(prompts, tiles, refs[:pieces], me_ref[0])
    states, windows = gathered.states(), gathered.windows()
    copies = []

    def send(source_ref, target_ref):
        copies.append(pltpu.make_async_copy(source_ref, target_ref, sems.at[len(copies)]))
        copies[-1].start()

    part = slots // PARTS
    for first in range(0, slots, part):
        here = slice(first, first + part)
        rows = slice(first * STATE, (first + part) * STATE)
        take = gathered.take(first, part)
        moved = jnp.dot(take, states, preferred_element_type=F32) + states_ref[rows, :].astype(F32)
        state_ref[here] = moved.astype(BF16).reshape(part, STATE, channels)
        send(state_ref.at[here], state_hbm.at[here])
        moved = jnp.dot(take, windows, preferred_element_type=F32)
        moved = moved + windows_ref[rows, :].astype(F32)
        moved = moved.astype(BF16).reshape(part, 16, 2 * LANES)
        for upper in range(2):
            for kind in range(2):
                at = upper * LANES + kind * HEAD_DIM
                keyval_ref[here, kind, upper * 16 : (upper + 1) * 16, :] = moved[
                    :, :, at : at + HEAD_DIM
                ]
        send(keyval_ref.at[here], keyval_hbm.at[here])
    wide = tails_ref.shape[0] // (2 * (CONV - 1))
    moved = gathered.tails(wide) + tails_ref[...].astype(F32)
    for odd in range(2):
        for tap in range(CONV - 1):
            at = (odd * (CONV - 1) + tap) * wide
            for pair in range(tiles // 2):
                tile = 2 * pair + odd
                conv_ref[tap, :, tile * LANES : (tile + 1) * LANES] = moved[
                    at : at + slots, pair * LANES : (pair + 1) * LANES
                ].astype(BF16)
    for copy in copies:
        copy.wait()


def on_device(
    pr_size,
    tp_size,
    tokens,
    prompt_lengths,
    query_weight,
    key_weight,
    value_weight,
    attention_gain,
    inner_weight,
    conv_weight,
    scan_weight,
    step_weight,
    step_bias,
    mamba_rate,
    mamba_skip,
    mamba_gain,
    request_prompt,
    request_owner,
    request_slot,
):
    rows, width = tokens.shape
    prompts = prompt_lengths.shape[1]
    channels = inner_weight.shape[2]
    features = query_weight.shape[1]
    slots = request_owner.shape[0]
    tiles = channels // LANES

    def shape(dims, dtype=F32):
        return jax.ShapeDtypeStruct(dims, dtype)

    inner = jnp.einsum("td,dgc->gtc", tokens, inner_weight, preferred_element_type=F32)
    inner = inner.astype(BF16)
    partial, mixed = pl.pallas_call(
        functools.partial(mix_kernel, prompts),
        out_shape=(
            shape((DT_RANK + 2 * STATE, rows)),
            shape((rows, channels), BF16),
        ),
        in_specs=[SMEM] + [VMEM] * 3,
        out_specs=(VMEM, VMEM),
        scratch_shapes=[pltpu.VMEM((rows + 8, channels), F32)],
        compiler_params=params(16),
        name="mix",
    )(prompt_lengths, inner, conv_weight, scan_weight.T)

    def swap(x, axis, size, bit):
        return lax.ppermute(x, axis, [(i, i ^ bit) for i in range(size)])

    near = swap(partial, "tp", tp_size, 1)
    spare = (16 - 2 * prompts * (CONV - 1)) * (tiles // 2)
    early_rows = prompts * WINDOW + 8 * tiles + -(-max(pr_size - spare, 0) // 16) * 16
    attended, square, early = pl.pallas_call(
        functools.partial(attend_kernel, prompts),
        out_shape=(
            shape((rows, features)),
            shape((8, rows)),
            shape((early_rows, LANES), BF16),
        ),
        in_specs=[SMEM] + [VMEM] * 8,
        out_specs=(VMEM, VMEM, VMEM),
        scratch_shapes=[
            pltpu.VMEM((8, LANES), jnp.int32),
        ],
        compiler_params=params(16),
        cost_estimate=pl.CostEstimate(
            flops=2 * rows * width * (features + channels), bytes_accessed=4 << 20, transcendentals=0
        ),
        name="attend",
    )(
        prompt_lengths,
        tokens,
        query_weight,
        key_weight.T,
        value_weight.T,
        inner,
        request_prompt[None],
        request_owner[None],
        request_slot[None],
    )
    pair = partial + near
    bit = 2
    while bit < tp_size // 2:
        pair = pair + swap(pair, "tp", tp_size, bit)
        bit *= 2
    far = swap(pair.astype(BF16), "tp", tp_size, bit)

    payload, states_even, states_odd = scan_call(
        prompts,
        prompt_lengths,
        pair,
        far,
        mixed,
        step_weight,
        step_bias[None],
        mamba_rate,
        early,
    )
    gated, sums = pl.pallas_call(
        gate_kernel,
        out_shape=(shape((rows, channels)), shape((2, rows))),
        in_specs=[VMEM] * 8,
        out_specs=(VMEM, VMEM),
        scratch_shapes=[
            pltpu.VMEM((rows, BLOCK * STATE), BF16),
            pltpu.VMEM((rows, channels), F32),
        ],
        compiler_params=params(16),
        cost_estimate=pl.CostEstimate(flops=1 << 24, bytes_accessed=4 << 20, transcendentals=0),
        name="gate",
    )(pair, far, states_even, states_odd, mixed, inner, mamba_skip[None], square)

    me = lax.axis_index("pr").astype(jnp.int32)
    held = payload[None]
    pr_bits = [1 << i for i in reversed(range((pr_size - 1).bit_length()))]
    tp_bits = [1 << i for i in range((tp_size - 1).bit_length())]
    main, last = pr_bits[:-1], pr_bits[-1]
    near, far = list(tp_bits[:-1]), tp_bits[-1]
    for bit in main[:-1]:
        new = swap(held, "pr", pr_size, bit)
        other = swap(sums, "tp", tp_size, near.pop(0)) if near else jnp.zeros_like(sums)
        held, sums = pl.pallas_call(
            join_kernel,
            out_shape=(
                shape((2 * held.shape[0],) + held.shape[1:], BF16),
                shape(sums.shape),
            ),
            in_specs=[VMEM] * 4,
            out_specs=(VMEM, VMEM),
            compiler_params=params(16),
            name="join",
        )(held, new, sums, other)
    for bit in near:
        sums = sums + swap(sums, "tp", tp_size, bit)
    crossed = swap(held, "pr", pr_size, last)
    fresh = swap(held, "pr", pr_size, main[-1])
    other = swap(sums, "tp", tp_size, far)
    fresh, sums = pl.pallas_call(
        hold_kernel,
        out_shape=(shape(fresh.shape, BF16), shape(sums.shape)),
        in_specs=[VMEM] * 3,
        out_specs=(VMEM, VMEM),
        compiler_params=params(16),
        name="hold",
    )(fresh, sums, other)
    crossed_last = swap(fresh, "pr", pr_size, last)
    wide = -(-slots // 16) * 16
    collected = pl.pallas_call(
        functools.partial(collect_kernel, prompts, slots),
        out_shape=(
            shape((slots * STATE, channels), BF16),
            shape((slots * STATE, 2 * LANES), BF16),
            shape((2 * (CONV - 1) * wide, tiles // 2 * LANES), BF16),
        ),
        in_specs=[SMEM, VMEM, VMEM],
        out_specs=(VMEM, VMEM, VMEM),
        compiler_params=params(32),
        cost_estimate=pl.CostEstimate(flops=1 << 28, bytes_accessed=2 << 20, transcendentals=0),
        name="collect",
    )(me[None], held, fresh)
    attention_out, mamba_out = pl.pallas_call(
        norm_kernel,
        out_shape=(shape((rows, features), BF16), shape((rows, channels), BF16)),
        in_specs=[VMEM] * 5 + [HBM] * 3,
        out_specs=(VMEM, VMEM),
        compiler_params=params(16),
        cost_estimate=pl.CostEstimate(flops=1 << 24, bytes_accessed=2 << 20, transcendentals=0),
        name="norm",
    )(
        attended,
        gated,
        sums,
        attention_gain[None],
        mamba_gain[None],
        inner_weight,
        crossed,
        collected[2],
    )
    keyval, state, conv = pl.pallas_call(
        functools.partial(deliver_kernel, prompts, 2),
        out_shape=(
            shape((slots, 2, WINDOW, HEAD_DIM), BF16),
            shape((slots, STATE, channels), BF16),
            shape((CONV - 1, slots, channels), BF16),
        ),
        in_specs=[SMEM] + [VMEM] * 5,
        out_specs=(HBM, HBM, VMEM),
        scratch_shapes=[
            pltpu.VMEM((slots, 2, WINDOW, HEAD_DIM), BF16),
            pltpu.VMEM((slots, STATE, channels), BF16),
            pltpu.SemaphoreType.DMA((2 * PARTS,)),
        ],
        compiler_params=params(32),
        name="deliver",
    )(me[None], *collected, crossed, crossed_last)
    return (attention_out, mamba_out, keyval, state, conv.transpose(1, 0, 2))


def solution(mesh):
    return jax.shard_map(
        functools.partial(on_device, mesh.shape["pr"], mesh.shape["tp"]),
        mesh=mesh,
        in_specs=(
            P("pr", None),
            P("pr", None),
            P(None, "tp"),
            P(None, "tp"),
            P(None, "tp"),
            P("tp"),
            P(None, None, "tp"),
            P(None, "tp"),
            P("tp", None),
            P(None, "tp"),
            P("tp"),
            P(None, "tp"),
            P("tp"),
            P("tp"),
            P("pr"),
            P("pr"),
            P("pr"),
        ),
        out_specs=(
            P("pr", "tp"),
            P("pr", "tp"),
            P("pr", None, None, "tp"),
            P("pr", None, "tp"),
            P("pr", None, "tp"),
        ),
        check_vma=False,
    )
```

```python
import functools
import math

import jax
import jax.numpy as jnp
from jax import lax
from jax.experimental import pallas as pl
from jax.experimental.pallas import tpu as pltpu
from jax.sharding import PartitionSpec as P

HEADS = 16
KV_HEADS = 4
HEAD_DIM = 64
INNER = 2048
STATE = 16
DT_RANK = 64
CONV = 4
WINDOW = 32
EPSILON = 1e-06
LANES = 128
BLOCK = 16
RESET = 1e30

F32 = jnp.float32
BF16 = jnp.bfloat16
VMEM = pl.BlockSpec(memory_space=pltpu.VMEM)
HBM = pl.BlockSpec(memory_space=pltpu.HBM)


def params(mib):
    return pltpu.CompilerParams(vmem_limit_bytes=mib << 20)


def dot_nt(a, b):
    return lax.dot_general(a, b, (((1,), (1,)), ((), ())), preferred_element_type=F32)


def bounds(len_ref, prompts):
    starts, ends = [], []
    at = 0
    for p in range(prompts):
        starts.append(at)
        at = at + len_ref[0:1, p : p + 1]
        ends.append(at)
    return starts, ends


def first_row_of(position, starts, prompts):
    first = jnp.zeros_like(position)
    for p in range(1, prompts):
        first = jnp.where(position >= starts[p], starts[p], first)
    return first


def last_rows(shape, depth, starts, ends):
    row = lax.broadcasted_iota(jnp.int32, shape, 0)
    position = lax.broadcasted_iota(jnp.int32, shape, 1)
    hit = jnp.zeros(shape, F32)
    for p in range(len(starts)):
        here = (row >= p * depth) & (row < (p + 1) * depth) & (position >= starts[p])
        hit = jnp.where(here & (position - row == ends[p] - (p + 1) * depth), 1.0, hit)
    return hit.astype(BF16)


def row_sums(squares):
    total = squares[:, :LANES]
    for at in range(LANES, squares.shape[1], LANES):
        total = total + squares[:, at : at + LANES]
    return jnp.sum(total.T, axis=0, keepdims=True)


def sigmoid(x):
    return 0.5 * jnp.tanh(0.5 * x) + 0.5


def mix_kernel(
    prompts,
    len_ref,
    inner_ref,
    conv_ref,
    scan_ref,
    partial_ref,
    mixed_ref,
    raw_ref,
):
    _, rows, channels = inner_ref.shape
    starts, _ = bounds(len_ref, prompts)
    raw = inner_ref[0].astype(F32)
    raw_ref[pl.ds(0, 8), :] = jnp.zeros((8, channels), F32)
    raw_ref[pl.ds(8, rows), :] = raw
    position = lax.broadcasted_iota(jnp.int32, (rows, 1), 0)
    offset = position - first_row_of(position, starts, prompts)
    total = raw * conv_ref[CONV - 1 : CONV, :]
    for lag in range(1, CONV):
        shifted = raw_ref[pl.ds(8 - lag, rows), :]
        shifted = jnp.where(offset >= lag, shifted, 0.0)
        total = total + shifted * conv_ref[CONV - 1 - lag : CONV - lag, :]
    mixed = (total * sigmoid(total)).astype(BF16)
    mixed_ref[...] = mixed
    partial_ref[...] = dot_nt(scan_ref[...], mixed)


def attend_kernel(
    prompts,
    len_ref,
    tokens_ref,
    query_ref,
    key_ref,
    value_ref,
    inner_ref,
    prompt_ref,
    owner_ref,
    slot_ref,
    attended_ref,
    square_ref,
    packed_ref,
    request_ref,
):
    rows, width = tokens_ref.shape
    channels = inner_ref.shape[2]
    features = query_ref.shape[1]
    group = features // HEAD_DIM
    starts, ends = bounds(len_ref, prompts)
    tokens = tokens_ref[...]
    queries = jnp.dot(tokens, query_ref[...], preferred_element_type=F32).astype(BF16)
    keys = dot_nt(tokens, jnp.concatenate([key_ref[...]] * group, axis=0)).astype(BF16)
    values = dot_nt(tokens, jnp.concatenate([value_ref[...]] * group, axis=0)).astype(BF16)
    at_row = lax.broadcasted_iota(jnp.int32, (rows, rows), 0)
    at_column = lax.broadcasted_iota(jnp.int32, (rows, rows), 1)
    row_first = first_row_of(at_row, starts, prompts)
    allowed = (at_column <= at_row) & (at_row - at_column < WINDOW) & (at_column >= row_first)
    head_of = lax.broadcasted_iota(jnp.int32, (rows, features), 1) // HEAD_DIM
    zero = jnp.zeros((), BF16)
    attended = jnp.zeros((rows, features), F32)
    for head in range(group):
        mine = head_of == head
        scores = dot_nt(queries, jnp.where(mine, keys, zero)) * HEAD_DIM ** (-0.5)
        scores = jnp.where(allowed, scores, -1e30)
        top = jnp.max(scores, axis=1, keepdims=True)
        expons = jnp.exp(scores - top)
        weights = expons * (1.0 / jnp.sum(expons, axis=1, keepdims=True))
        attended = attended + jnp.dot(
            weights.astype(BF16), jnp.where(mine, values, zero), preferred_element_type=F32
        )
    attended_ref[...] = attended
    square_ref[...] = jnp.broadcast_to(row_sums(attended * attended), square_ref.shape)
    lane = lax.broadcasted_iota(jnp.int32, (rows, LANES), 1)
    both = jnp.where(lane < HEAD_DIM, keys[:, :LANES], values[:, :LANES])
    pick = last_rows((prompts * WINDOW, rows), WINDOW, starts, ends)
    packed_ref[: prompts * WINDOW, :] = jnp.dot(pick, both, preferred_element_type=F32).astype(
        BF16
    )
    requests = owner_ref.shape[1]
    request_ref[...] = jnp.full(request_ref.shape, -1, jnp.int32)
    request_ref[0:1, 0:requests] = owner_ref[...]
    request_ref[1:2, 0:requests] = slot_ref[...]
    request_ref[2:3, 0:requests] = prompt_ref[...]
    depth = prompts * (CONV - 1)
    groups = channels // LANES // 2
    spare = 16 - 2 * depth
    owners = packed_ref.shape[0] - prompts * WINDOW - 16 * groups + spare * groups
    owner = lax.broadcasted_iota(jnp.int32, (owners, LANES), 0) == request_ref[0:1, :]
    slot = lax.broadcasted_iota(jnp.int32, (LANES, LANES), 0) == request_ref[1:2, :]
    number = request_ref[2:3, :] + 1
    filled = dot_nt(
        jnp.where(owner, 1.0, 0.0).astype(BF16),
        jnp.where(slot, number, 0).astype(F32).astype(BF16),
    )
    pick = last_rows((8, rows), CONV - 1, starts, ends)
    tail = jnp.dot(pick, inner_ref[0], preferred_element_type=F32)
    base = prompts * WINDOW
    for group in range(groups):
        at = 2 * group * LANES
        packed_ref[base + 16 * group : base + 16 * (group + 1), :] = jnp.concatenate(
            [
                tail[:depth, at : at + LANES],
                tail[:depth, at + LANES : at + 2 * LANES],
                filled[spare * group : spare * (group + 1), :],
            ],
            axis=0,
        ).astype(BF16)
    if owners > spare * groups:
        packed_ref[base + 16 * groups :, :] = filled[spare * groups :, :].astype(BF16)


def scan_kernel(
    prompts,
    len_ref,
    own_ref,
    other_ref,
    mixed_ref,
    step_weight_ref,
    step_bias_ref,
    rate_ref,
    early_ref,
    payload_ref,
    states_even_ref,
    states_odd_ref,
    decay_ref,
    input_ref,
    in_map_ref,
    scalars_ref,
    sem,
):
    scalars_copy = pltpu.make_async_copy(len_ref, scalars_ref, sem)
    scalars_copy.start()
    rows, channels = mixed_ref.shape
    pairs = rows // BLOCK // 2
    starts, _ = bounds(len_ref, prompts)
    projected = own_ref[...] + other_ref[...].astype(F32)
    low = projected[:DT_RANK, :].T.astype(BF16)
    pre = jnp.dot(low, step_weight_ref[...], preferred_element_type=F32) + step_bias_ref[...]
    step = jnp.maximum(pre, 0.0) + jnp.log1p(jnp.exp(-jnp.abs(pre)))
    position = lax.broadcasted_iota(jnp.int32, (rows, 1), 0)
    is_first = position == 0
    for p in range(1, prompts):
        is_first = is_first | (position == starts[p])
    decay_ref[...] = jnp.where(is_first, RESET, step)
    input_ref[...] = step * mixed_ref[...].astype(F32)
    for block in range(rows // BLOCK):
        columns = slice(block * BLOCK, (block + 1) * BLOCK)
        in_map_ref[block, :, 0:BLOCK] = projected[DT_RANK : DT_RANK + STATE, columns]
    rate = rate_ref[...] * (-math.log2(math.e))

    def advance(block, state, states_ref, index):
        at = pl.multiple_of(block * BLOCK, BLOCK)
        for token in range(BLOCK):
            decay = jnp.exp2(decay_ref[pl.ds(at + token, 1), :] * rate)
            entering = in_map_ref[block, :, token : token + 1] * input_ref[pl.ds(at + token, 1), :]
            state = state * decay + entering
            states_ref[index, token * STATE : (token + 1) * STATE, :] = state.astype(BF16)
        return state

    def two_blocks(pair, state):
        state = advance(2 * pair, state, states_even_ref, pair)
        return advance(2 * pair + 1, state, states_odd_ref, pair)

    lax.fori_loop(0, pairs, two_blocks, jnp.zeros((STATE, channels), F32))
    scalars_copy.wait()
    last = -1
    for p in range(prompts):
        last = last + scalars_ref[0, p]
        block = last // BLOCK
        at = pl.multiple_of((last - block * BLOCK) * STATE, STATE)
        final = jnp.where(
            block % 2 == 0,
            states_even_ref[block // 2, pl.ds(at, STATE), :],
            states_odd_ref[block // 2, pl.ds(at, STATE), :],
        )
        for tile in range(channels // LANES):
            at = (p * (channels // LANES) + tile) * STATE
            payload_ref[at : at + STATE, :] = final[:, tile * LANES : (tile + 1) * LANES]
    base = prompts * channels // LANES * STATE
    payload_ref[base:, :] = early_ref[...]


def scan_call(prompts, lengths, own, other, mixed, *rest):
    rows, channels = mixed.shape
    tiles = channels // LANES
    payload_rows = prompts * tiles * STATE + rest[-1].shape[0]
    states = jax.ShapeDtypeStruct((rows // BLOCK // 2, BLOCK * STATE, channels), BF16)
    return pl.pallas_call(
        functools.partial(scan_kernel, prompts),
        out_shape=(jax.ShapeDtypeStruct((payload_rows, LANES), BF16), states, states),
        in_specs=[VMEM] * 8,
        out_specs=(VMEM,) * 3,
        scratch_shapes=[
            pltpu.VMEM((rows, channels), F32),
            pltpu.VMEM((rows, channels), F32),
            pltpu.VMEM((rows // BLOCK, STATE, LANES), F32),
            pltpu.SMEM((1, prompts), jnp.int32),
            pltpu.SemaphoreType.DMA,
        ],
        compiler_params=params(16),
        name="scan",
    )(lengths, own, other, mixed, *rest)


def gate_kernel(
    own_ref,
    other_ref,
    states_even_ref,
    states_odd_ref,
    mixed_ref,
    inner_ref,
    skip_ref,
    square_ref,
    gated_ref,
    sums_ref,
    out_map_ref,
    scanned_ref,
):
    rows, channels = mixed_ref.shape
    span = BLOCK * STATE
    maps = slice(DT_RANK + STATE, DT_RANK + 2 * STATE)
    out_map = own_ref[maps, :] + other_ref[maps, :].astype(F32)
    row = lax.broadcasted_iota(jnp.int32, (STATE, span), 0)
    column = lax.broadcasted_iota(jnp.int32, (STATE, span), 1)
    tiled = jnp.dot(
        out_map.T.astype(BF16),
        jnp.where(column % STATE == row, 1.0, 0.0).astype(BF16),
        preferred_element_type=F32,
    )
    row = lax.broadcasted_iota(jnp.int32, (rows, span), 0)
    column = lax.broadcasted_iota(jnp.int32, (rows, span), 1)
    out_map_ref[...] = jnp.where(column // STATE == row % BLOCK, tiled, 0.0).astype(BF16)
    for block in range(rows // BLOCK):
        states_ref = states_odd_ref if block % 2 else states_even_ref
        at = slice(block * BLOCK, (block + 1) * BLOCK)
        scanned_ref[at, :] = jnp.dot(
            out_map_ref[at, :], states_ref[block // 2], preferred_element_type=F32
        )
    gate = inner_ref[1].astype(F32)
    gated = (scanned_ref[...] + skip_ref[...] * mixed_ref[...].astype(F32)) * (
        gate * sigmoid(gate)
    )
    gated_ref[...] = gated
    sums_ref[0:1, :] = square_ref[0:1, :]
    sums_ref[1:2, :] = row_sums(gated * gated)


def join_kernel(held_ref, new_ref, own_ref, other_ref, joined_ref, sums_ref):
    count = held_ref.shape[0]
    joined_ref[:count] = held_ref[...]
    joined_ref[count:] = new_ref[...]
    sums_ref[...] = own_ref[...] + other_ref[...]


def hold_kernel(new_ref, own_ref, other_ref, fresh_ref, sums_ref):
    fresh_ref[...] = new_ref[...]
    sums_ref[...] = own_ref[...] + other_ref[...]


def norm_kernel(
    attended_ref,
    gated_ref,
    sums_ref,
    attention_gain_ref,
    mamba_gain_ref,
    crossed_hbm,
    inner_hbm,
    attention_ref,
    mamba_ref,
):
    sums = sums_ref[...]
    sums = jnp.concatenate([sums, jnp.zeros((6, sums.shape[1]), F32)], axis=0).T
    attention_scale = lax.rsqrt(sums[:, 0:1] / (HEADS * HEAD_DIM) + EPSILON)
    attention_ref[...] = (attended_ref[...] * attention_scale * attention_gain_ref[...]).astype(
        BF16
    )
    mamba_scale = lax.rsqrt(sums[:, 1:2] / INNER + EPSILON)
    mamba_ref[...] = (gated_ref[...] * mamba_scale * mamba_gain_ref[...]).astype(BF16)


def one_hot(hit):
    return jnp.where(hit, 1.0, 0.0).astype(BF16)


def deliver_kernel(
    prompts,
    pieces,
    *refs,
):
    keyval_ref, state_ref, conv_ref = refs[pieces:]
    me = lax.axis_index("pr")
    slots, _, channels = state_ref.shape
    tiles = channels // LANES
    blocks = [(ref, index) for ref in refs[:pieces] for index in range(ref.shape[0])]
    sources = len(blocks)
    window_at = prompts * tiles * STATE
    tail_at = window_at + prompts * WINDOW
    depth = CONV - 1
    spare = 16 - 2 * prompts * depth
    table_rows = refs[0].shape[1] - tail_at

    def rows_of(source, at, size):
        ref, index = blocks[source]
        return ref[index, at : at + size, :]

    row = lax.broadcasted_iota(jnp.int32, (table_rows, LANES), 0)
    grouped = row < 8 * tiles
    owner = jnp.where(
        grouped, row // 16 * spare + row % 16 - (16 - spare), row - 8 * tiles + spare * (tiles // 2)
    )
    owner = jnp.where(grouped & (row % 16 < 16 - spare), -1, owner)
    pick = jnp.zeros((1, LANES), F32)
    for source in range(sources):
        filled = rows_of(source, tail_at, table_rows).astype(F32)
        filled = jnp.sum(jnp.where(owner == me, filled, 0.0), axis=0, keepdims=True)
        pick = pick + jnp.where(filled > 0.5, filled + float(source * prompts - 1), 0.0)
    pick = pick.astype(jnp.int32)

    span = sources * prompts * STATE
    wanted = one_hot(lax.broadcasted_iota(jnp.int32, (span, LANES), 0) // STATE == pick)
    states, windows, tails = [], [], []
    for source in range(sources):
        for p in range(prompts):
            at = p * tiles * STATE
            states.append(
                jnp.concatenate(
                    [rows_of(source, at + tile * STATE, STATE) for tile in range(tiles)], axis=1
                )
            )
            at = window_at + p * WINDOW
            windows.append(
                jnp.concatenate(
                    [
                        rows_of(source, at, WINDOW // 2),
                        rows_of(source, at + WINDOW // 2, WINDOW // 2),
                    ],
                    axis=1,
                )
            )
        tails.append(
            jnp.concatenate(
                [rows_of(source, tail_at + 8 * tile, 16) for tile in range(0, tiles, 2)], axis=1
            )
        )
    states = jnp.concatenate(states, axis=0)
    windows = jnp.concatenate(windows, axis=0)
    row = lax.broadcasted_iota(jnp.int32, (slots * STATE, LANES), 0)
    lane = lax.broadcasted_iota(jnp.int32, (slots * STATE, LANES), 1)
    take = dot_nt(one_hot(row // STATE == lane), wanted)
    row = lax.broadcasted_iota(jnp.int32, (slots * STATE, span), 0)
    lane = lax.broadcasted_iota(jnp.int32, (slots * STATE, span), 1)
    take = jnp.where(row % STATE == lane % STATE, take, 0.0).astype(BF16)
    moved = jnp.dot(take, states, preferred_element_type=F32)
    state_ref[...] = moved.astype(BF16).reshape(slots, STATE, channels)
    moved = jnp.dot(take, windows, preferred_element_type=F32)
    moved = moved.astype(BF16).reshape(slots, WINDOW // 2, 2 * LANES)
    for upper in range(2):
        for kind in range(2):
            at = upper * LANES + kind * HEAD_DIM
            keyval_ref[:, kind, upper * WINDOW // 2 : (upper + 1) * WINDOW // 2, :] = moved[
                :, :, at : at + HEAD_DIM
            ]

    wide = -(-slots // 16) * 16
    row = lax.broadcasted_iota(jnp.int32, (wide, LANES), 0)
    lane = lax.broadcasted_iota(jnp.int32, (wide, LANES), 1)
    unit = one_hot(row == lane)
    span = sources * 16
    row = lax.broadcasted_iota(jnp.int32, (span, LANES), 0)
    base = (pick // prompts) * 16 + (pick % prompts) * depth
    hits = [
        one_hot(row == base + prompts * depth * odd + tap) for odd in (0, 1) for tap in range(depth)
    ]
    hits = dot_nt(unit, jnp.concatenate(hits, axis=0)).astype(BF16)
    hits = jnp.concatenate([hits[:, i * span : (i + 1) * span] for i in range(2 * depth)], axis=0)
    moved = jnp.dot(hits, jnp.concatenate(tails, axis=0), preferred_element_type=F32)
    for odd in range(2):
        for tap in range(depth):
            at = (odd * depth + tap) * wide
            for pair in range(tiles // 2):
                tile = 2 * pair + odd
                conv_ref[tap, :, tile * LANES : (tile + 1) * LANES] = moved[
                    at : at + slots, pair * LANES : (pair + 1) * LANES
                ].astype(BF16)


def on_device(
    pr_size,
    tp_size,
    tokens,
    prompt_lengths,
    query_weight,
    key_weight,
    value_weight,
    attention_gain,
    inner_weight,
    conv_weight,
    scan_weight,
    step_weight,
    step_bias,
    mamba_rate,
    mamba_skip,
    mamba_gain,
    request_prompt,
    request_owner,
    request_slot,
):
    rows, width = tokens.shape
    prompts = prompt_lengths.shape[1]
    channels = inner_weight.shape[2]
    features = query_weight.shape[1]
    slots = request_owner.shape[0]
    tiles = channels // LANES

    def shape(dims, dtype=F32):
        return jax.ShapeDtypeStruct(dims, dtype)

    inner = jnp.einsum("td,dgc->gtc", tokens, inner_weight, preferred_element_type=F32)
    inner = inner.astype(BF16)
    partial, mixed = pl.pallas_call(
        functools.partial(mix_kernel, prompts),
        out_shape=(
            shape((DT_RANK + 2 * STATE, rows)),
            shape((rows, channels), BF16),
        ),
        in_specs=[VMEM] * 4,
        out_specs=(VMEM, VMEM),
        scratch_shapes=[pltpu.VMEM((rows + 8, channels), F32)],
        compiler_params=params(16),
        name="mix",
    )(prompt_lengths, inner, conv_weight, scan_weight.T)

    def swap(x, axis, size, bit):
        return lax.ppermute(x, axis, [(i, i ^ bit) for i in range(size)])

    near = swap(partial, "tp", tp_size, 1)
    spare = (16 - 2 * prompts * (CONV - 1)) * (tiles // 2)
    early_rows = prompts * WINDOW + 8 * tiles + -(-max(pr_size - spare, 0) // 16) * 16
    attended, square, early = pl.pallas_call(
        functools.partial(attend_kernel, prompts),
        out_shape=(
            shape((rows, features)),
            shape((8, rows)),
            shape((early_rows, LANES), BF16),
        ),
        in_specs=[VMEM] * 9,
        out_specs=(VMEM, VMEM, VMEM),
        scratch_shapes=[
            pltpu.VMEM((8, LANES), jnp.int32),
        ],
        compiler_params=params(16),
        cost_estimate=pl.CostEstimate(
            flops=2 * rows * width * (features + channels), bytes_accessed=4 << 20, transcendentals=0
        ),
        name="attend",
    )(
        prompt_lengths,
        tokens,
        query_weight,
        key_weight.T,
        value_weight.T,
        inner,
        request_prompt[None],
        request_owner[None],
        request_slot[None],
    )
    pair = partial + near
    bit = 2
    while bit < tp_size // 2:
        pair = pair + swap(pair, "tp", tp_size, bit)
        bit *= 2
    far = swap(pair.astype(BF16), "tp", tp_size, bit)

    payload, states_even, states_odd = scan_call(
        prompts,
        prompt_lengths,
        pair,
        far,
        mixed,
        step_weight,
        step_bias[None],
        mamba_rate,
        early,
    )
    gated, sums = pl.pallas_call(
        gate_kernel,
        out_shape=(shape((rows, channels)), shape((2, rows))),
        in_specs=[VMEM] * 8,
        out_specs=(VMEM, VMEM),
        scratch_shapes=[
            pltpu.VMEM((rows, BLOCK * STATE), BF16),
            pltpu.VMEM((rows, channels), F32),
        ],
        compiler_params=params(16),
        cost_estimate=pl.CostEstimate(flops=1 << 24, bytes_accessed=4 << 20, transcendentals=0),
        name="gate",
    )(pair, far, states_even, states_odd, mixed, inner, mamba_skip[None], square)

    held = payload[None]
    pr_bits = [1 << i for i in reversed(range((pr_size - 1).bit_length()))]
    tp_bits = [1 << i for i in range((tp_size - 1).bit_length())]
    main, last = pr_bits[:-1], pr_bits[-1]
    near, far = list(tp_bits[:-1]), tp_bits[-1]
    for bit in main[:-1]:
        new = swap(held, "pr", pr_size, bit)
        other = swap(sums, "tp", tp_size, near.pop(0)) if near else jnp.zeros_like(sums)
        held, sums = pl.pallas_call(
            join_kernel,
            out_shape=(
                shape((2 * held.shape[0],) + held.shape[1:], BF16),
                shape(sums.shape),
            ),
            in_specs=[VMEM] * 4,
            out_specs=(VMEM, VMEM),
            compiler_params=params(16),
            name="join",
        )(held, new, sums, other)
    for bit in near:
        sums = sums + swap(sums, "tp", tp_size, bit)
    crossed = swap(held, "pr", pr_size, last)
    fresh = swap(held, "pr", pr_size, main[-1])
    other = swap(sums, "tp", tp_size, far)
    fresh, sums = pl.pallas_call(
        hold_kernel,
        out_shape=(shape(fresh.shape, BF16), shape(sums.shape)),
        in_specs=[VMEM] * 3,
        out_specs=(VMEM, VMEM),
        compiler_params=params(16),
        name="hold",
    )(fresh, sums, other)
    pieces = [held, fresh, crossed, swap(fresh, "pr", pr_size, last)]
    attention_out, mamba_out = pl.pallas_call(
        norm_kernel,
        out_shape=(shape((rows, features), BF16), shape((rows, channels), BF16)),
        in_specs=[VMEM] * 5 + [HBM] * 2,
        out_specs=(VMEM, VMEM),
        compiler_params=params(16),
        cost_estimate=pl.CostEstimate(flops=1 << 24, bytes_accessed=2 << 20, transcendentals=0),
        name="norm",
    )(attended, gated, sums, attention_gain[None], mamba_gain[None], crossed, inner_weight)
    keyval, state, conv = pl.pallas_call(
        functools.partial(deliver_kernel, prompts, len(pieces)),
        out_shape=(
            shape((slots, 2, WINDOW, HEAD_DIM), BF16),
            shape((slots, STATE, channels), BF16),
            shape((CONV - 1, slots, channels), BF16),
        ),
        in_specs=[VMEM] * len(pieces),
        out_specs=(VMEM,) * 3,
        compiler_params=params(32),
        name="deliver",
    )(*pieces)
    return (attention_out, mamba_out, keyval, state, conv.transpose(1, 0, 2))


def solution(mesh):
    return jax.shard_map(
        functools.partial(on_device, mesh.shape["pr"], mesh.shape["tp"]),
        mesh=mesh,
        in_specs=(
            P("pr", None),
            P("pr", None),
            P(None, "tp"),
            P(None, "tp"),
            P(None, "tp"),
            P("tp"),
            P(None, None, "tp"),
            P(None, "tp"),
            P("tp", None),
            P(None, "tp"),
            P("tp"),
            P(None, "tp"),
            P("tp"),
            P("tp"),
            P("pr"),
            P("pr"),
            P("pr"),
        ),
        out_specs=(
            P("pr", "tp"),
            P("pr", "tp"),
            P("pr", None, None, "tp"),
            P("pr", None, "tp"),
            P("pr", None, "tp"),
        ),
        check_vma=False,
    )
```

```python
import functools
import math

import jax
import jax.numpy as jnp
from jax import lax
from jax.experimental import pallas as pl
from jax.experimental.pallas import tpu as pltpu
from jax.sharding import PartitionSpec as P

HEADS = 16
KV_HEADS = 4
HEAD_DIM = 64
INNER = 2048
STATE = 16
DT_RANK = 64
CONV = 4
WINDOW = 32
EPSILON = 1e-06
LANES = 128
BLOCK = 16
RESET = 1e30

F32 = jnp.float32
BF16 = jnp.bfloat16
VMEM = pl.BlockSpec(memory_space=pltpu.VMEM)
HBM = pl.BlockSpec(memory_space=pltpu.HBM)


def params(mib):
    return pltpu.CompilerParams(vmem_limit_bytes=mib << 20)


def dot_nt(a, b):
    return lax.dot_general(a, b, (((1,), (1,)), ((), ())), preferred_element_type=F32)


def bounds(len_ref, prompts):
    starts, ends = [], []
    at = 0
    for p in range(prompts):
        starts.append(at)
        at = at + len_ref[0:1, p : p + 1]
        ends.append(at)
    return starts, ends


def first_row_of(position, starts, prompts):
    first = jnp.zeros_like(position)
    for p in range(1, prompts):
        first = jnp.where(position >= starts[p], starts[p], first)
    return first


def last_rows(shape, depth, starts, ends):
    row = lax.broadcasted_iota(jnp.int32, shape, 0)
    position = lax.broadcasted_iota(jnp.int32, shape, 1)
    hit = jnp.zeros(shape, F32)
    for p in range(len(starts)):
        here = (row >= p * depth) & (row < (p + 1) * depth) & (position >= starts[p])
        hit = jnp.where(here & (position - row == ends[p] - (p + 1) * depth), 1.0, hit)
    return hit.astype(BF16)


def row_sums(squares):
    total = squares[:, :LANES]
    for at in range(LANES, squares.shape[1], LANES):
        total = total + squares[:, at : at + LANES]
    return jnp.sum(total.T, axis=0, keepdims=True)


def sigmoid(x):
    return 0.5 * jnp.tanh(0.5 * x) + 0.5


def mix_kernel(
    prompts,
    len_ref,
    inner_ref,
    conv_ref,
    scan_ref,
    partial_ref,
    mixed_ref,
    raw_ref,
):
    _, rows, channels = inner_ref.shape
    starts, _ = bounds(len_ref, prompts)
    raw = inner_ref[0].astype(F32)
    raw_ref[pl.ds(0, 8), :] = jnp.zeros((8, channels), F32)
    raw_ref[pl.ds(8, rows), :] = raw
    position = lax.broadcasted_iota(jnp.int32, (rows, 1), 0)
    offset = position - first_row_of(position, starts, prompts)
    total = raw * conv_ref[CONV - 1 : CONV, :]
    for lag in range(1, CONV):
        shifted = raw_ref[pl.ds(8 - lag, rows), :]
        shifted = jnp.where(offset >= lag, shifted, 0.0)
        total = total + shifted * conv_ref[CONV - 1 - lag : CONV - lag, :]
    mixed = (total * sigmoid(total)).astype(BF16)
    mixed_ref[...] = mixed
    partial_ref[...] = dot_nt(scan_ref[...], mixed)


def attend_kernel(
    prompts,
    len_ref,
    tokens_ref,
    query_ref,
    key_ref,
    value_ref,
    inner_ref,
    prompt_ref,
    owner_ref,
    slot_ref,
    attended_ref,
    square_ref,
    packed_ref,
    request_ref,
):
    rows, width = tokens_ref.shape
    channels = inner_ref.shape[2]
    features = query_ref.shape[1]
    group = features // HEAD_DIM
    starts, ends = bounds(len_ref, prompts)
    tokens = tokens_ref[...]
    queries = jnp.dot(tokens, query_ref[...], preferred_element_type=F32).astype(BF16)
    keys = dot_nt(tokens, jnp.concatenate([key_ref[...]] * group, axis=0)).astype(BF16)
    values = dot_nt(tokens, jnp.concatenate([value_ref[...]] * group, axis=0)).astype(BF16)
    at_row = lax.broadcasted_iota(jnp.int32, (rows, rows), 0)
    at_column = lax.broadcasted_iota(jnp.int32, (rows, rows), 1)
    row_first = first_row_of(at_row, starts, prompts)
    allowed = (at_column <= at_row) & (at_row - at_column < WINDOW) & (at_column >= row_first)
    head_of = lax.broadcasted_iota(jnp.int32, (rows, features), 1) // HEAD_DIM
    zero = jnp.zeros((), BF16)
    attended = jnp.zeros((rows, features), F32)
    for head in range(group):
        mine = head_of == head
        scores = dot_nt(queries, jnp.where(mine, keys, zero)) * HEAD_DIM ** (-0.5)
        scores = jnp.where(allowed, scores, -1e30)
        top = jnp.max(scores, axis=1, keepdims=True)
        expons = jnp.exp(scores - top)
        weights = expons * (1.0 / jnp.sum(expons, axis=1, keepdims=True))
        attended = attended + jnp.dot(
            weights.astype(BF16), jnp.where(mine, values, zero), preferred_element_type=F32
        )
    attended_ref[...] = attended
    square_ref[...] = jnp.broadcast_to(row_sums(attended * attended), square_ref.shape)
    lane = lax.broadcasted_iota(jnp.int32, (rows, LANES), 1)
    both = jnp.where(lane < HEAD_DIM, keys[:, :LANES], values[:, :LANES])
    pick = last_rows((prompts * WINDOW, rows), WINDOW, starts, ends)
    packed_ref[: prompts * WINDOW, :] = jnp.dot(pick, both, preferred_element_type=F32).astype(
        BF16
    )
    requests = owner_ref.shape[1]
    request_ref[...] = jnp.full(request_ref.shape, -1, jnp.int32)
    request_ref[0:1, 0:requests] = owner_ref[...]
    request_ref[1:2, 0:requests] = slot_ref[...]
    request_ref[2:3, 0:requests] = prompt_ref[...]
    depth = prompts * (CONV - 1)
    groups = channels // LANES // 2
    spare = 16 - 2 * depth
    owners = packed_ref.shape[0] - prompts * WINDOW - 16 * groups + spare * groups
    owner = lax.broadcasted_iota(jnp.int32, (owners, LANES), 0) == request_ref[0:1, :]
    slot = lax.broadcasted_iota(jnp.int32, (LANES, LANES), 0) == request_ref[1:2, :]
    number = request_ref[2:3, :] + 1
    filled = dot_nt(
        jnp.where(owner, 1.0, 0.0).astype(BF16),
        jnp.where(slot, number, 0).astype(F32).astype(BF16),
    )
    pick = last_rows((8, rows), CONV - 1, starts, ends)
    tail = jnp.dot(pick, inner_ref[0], preferred_element_type=F32)
    base = prompts * WINDOW
    for group in range(groups):
        at = 2 * group * LANES
        packed_ref[base + 16 * group : base + 16 * (group + 1), :] = jnp.concatenate(
            [
                tail[:depth, at : at + LANES],
                tail[:depth, at + LANES : at + 2 * LANES],
                filled[spare * group : spare * (group + 1), :],
            ],
            axis=0,
        ).astype(BF16)
    if owners > spare * groups:
        packed_ref[base + 16 * groups :, :] = filled[spare * groups :, :].astype(BF16)


def scan_kernel(
    prompts,
    len_ref,
    own_ref,
    other_ref,
    mixed_ref,
    step_weight_ref,
    step_bias_ref,
    rate_ref,
    early_ref,
    payload_ref,
    leaving_ref,
    states_even_ref,
    states_odd_ref,
    decay_ref,
    input_ref,
    in_map_ref,
    out_map_ref,
    scalars_ref,
    sem,
):
    scalars_copy = pltpu.make_async_copy(len_ref, scalars_ref, sem)
    scalars_copy.start()
    rows, channels = mixed_ref.shape
    pairs = rows // BLOCK // 2
    starts, _ = bounds(len_ref, prompts)
    projected = own_ref[...] + other_ref[...]
    low = projected[:DT_RANK, :].T.astype(BF16)
    pre = jnp.dot(low, step_weight_ref[...], preferred_element_type=F32) + step_bias_ref[...]
    step = jnp.maximum(pre, 0.0) + jnp.log1p(jnp.exp(-jnp.abs(pre)))
    position = lax.broadcasted_iota(jnp.int32, (rows, 1), 0)
    is_first = position == 0
    for p in range(1, prompts):
        is_first = is_first | (position == starts[p])
    decay_ref[...] = jnp.where(is_first, RESET, step)
    input_ref[...] = step * mixed_ref[...].astype(F32)
    for block in range(rows // BLOCK):
        columns = slice(block * BLOCK, (block + 1) * BLOCK)
        in_map_ref[block, :, 0:BLOCK] = projected[DT_RANK : DT_RANK + STATE, columns]
        out_map_ref[block, :, 0:BLOCK] = projected[DT_RANK + STATE :, columns]
    rate = rate_ref[...] * (-math.log2(math.e))

    def advance(block, state, states_ref, index):
        at = pl.multiple_of(block * BLOCK, BLOCK)
        for token in range(BLOCK):
            decay = jnp.exp2(decay_ref[pl.ds(at + token, 1), :] * rate)
            entering = in_map_ref[block, :, token : token + 1] * input_ref[pl.ds(at + token, 1), :]
            state = state * decay + entering
            states_ref[index, token * STATE : (token + 1) * STATE, :] = state.astype(BF16)
            leaving = out_map_ref[block, :, token : token + 1] * state
            leaving = leaving[:8, :] + leaving[8:, :]
            row = pl.multiple_of(block * BLOCK * 8, BLOCK * 8) + 8 * token
            for tile in range(channels // LANES):
                leaving_ref[tile, pl.ds(row, 8), :] = leaving[:, tile * LANES : (tile + 1) * LANES]
        return state

    def two_blocks(pair, state):
        state = advance(2 * pair, state, states_even_ref, pair)
        return advance(2 * pair + 1, state, states_odd_ref, pair)

    lax.fori_loop(0, pairs, two_blocks, jnp.zeros((STATE, channels), F32))
    scalars_copy.wait()
    last = -1
    for p in range(prompts):
        last = last + scalars_ref[0, p]
        block = last // BLOCK
        at = pl.multiple_of((last - block * BLOCK) * STATE, STATE)
        final = jnp.where(
            block % 2 == 0,
            states_even_ref[block // 2, pl.ds(at, STATE), :],
            states_odd_ref[block // 2, pl.ds(at, STATE), :],
        )
        for tile in range(channels // LANES):
            at = (p * (channels // LANES) + tile) * STATE
            payload_ref[at : at + STATE, :] = final[:, tile * LANES : (tile + 1) * LANES]
    base = prompts * channels // LANES * STATE
    payload_ref[base:, :] = early_ref[...]


def scan_call(prompts, lengths, own, other, mixed, *rest):
    rows, channels = mixed.shape
    tiles = channels // LANES
    payload_rows = prompts * tiles * STATE + rest[-1].shape[0]
    return pl.pallas_call(
        functools.partial(scan_kernel, prompts),
        out_shape=(
            jax.ShapeDtypeStruct((payload_rows, LANES), BF16),
            jax.ShapeDtypeStruct((tiles, rows * 8, LANES), F32),
        ),
        in_specs=[VMEM] * 8,
        out_specs=(VMEM, VMEM),
        scratch_shapes=[
            pltpu.VMEM((rows // BLOCK // 2, BLOCK * STATE, channels), BF16),
            pltpu.VMEM((rows // BLOCK // 2, BLOCK * STATE, channels), BF16),
            pltpu.VMEM((rows, channels), F32),
            pltpu.VMEM((rows, channels), F32),
            pltpu.VMEM((rows // BLOCK, STATE, LANES), F32),
            pltpu.VMEM((rows // BLOCK, STATE, LANES), F32),
            pltpu.SMEM((1, prompts), jnp.int32),
            pltpu.SemaphoreType.DMA,
        ],
        compiler_params=params(16),
        name="scan",
    )(lengths, own, other, mixed, *rest)


def gate_kernel(
    leaving_ref,
    mixed_ref,
    inner_ref,
    skip_ref,
    square_ref,
    gated_ref,
    sums_ref,
):
    rows, channels = mixed_ref.shape
    scanned = []
    for tile in range(channels // LANES):
        total = leaving_ref[tile, pl.ds(0, rows, stride=8), :]
        for index in range(1, 8):
            total = total + leaving_ref[tile, pl.ds(index, rows, stride=8), :]
        scanned.append(total)
    scanned = jnp.concatenate(scanned, axis=1)
    gate = inner_ref[1].astype(F32)
    gated = (scanned + skip_ref[...] * mixed_ref[...].astype(F32)) * (
        gate * sigmoid(gate)
    )
    gated_ref[...] = gated
    sums_ref[0:1, :] = square_ref[0:1, :]
    sums_ref[1:2, :] = row_sums(gated * gated)


def join_kernel(held_ref, new_ref, own_ref, other_ref, joined_ref, sums_ref):
    count = held_ref.shape[0]
    joined_ref[:count] = held_ref[...]
    joined_ref[count:] = new_ref[...]
    sums_ref[...] = own_ref[...] + other_ref[...]


def hold_kernel(new_ref, own_ref, other_ref, fresh_ref, sums_ref):
    fresh_ref[...] = new_ref[...]
    sums_ref[...] = own_ref[...] + other_ref[...]


def norm_kernel(
    attended_ref,
    gated_ref,
    sums_ref,
    attention_gain_ref,
    mamba_gain_ref,
    crossed_hbm,
    inner_hbm,
    attention_ref,
    mamba_ref,
):
    sums = sums_ref[...]
    sums = jnp.concatenate([sums, jnp.zeros((6, sums.shape[1]), F32)], axis=0).T
    attention_scale = lax.rsqrt(sums[:, 0:1] / (HEADS * HEAD_DIM) + EPSILON)
    attention_ref[...] = (attended_ref[...] * attention_scale * attention_gain_ref[...]).astype(
        BF16
    )
    mamba_scale = lax.rsqrt(sums[:, 1:2] / INNER + EPSILON)
    mamba_ref[...] = (gated_ref[...] * mamba_scale * mamba_gain_ref[...]).astype(BF16)


def one_hot(hit):
    return jnp.where(hit, 1.0, 0.0).astype(BF16)


def deliver_kernel(
    prompts,
    pieces,
    *refs,
):
    keyval_ref, state_ref, conv_ref = refs[pieces:]
    me = lax.axis_index("pr")
    slots, _, channels = state_ref.shape
    tiles = channels // LANES
    blocks = [(ref, index) for ref in refs[:pieces] for index in range(ref.shape[0])]
    sources = len(blocks)
    window_at = prompts * tiles * STATE
    tail_at = window_at + prompts * WINDOW
    depth = CONV - 1
    spare = 16 - 2 * prompts * depth
    table_rows = refs[0].shape[1] - tail_at

    def rows_of(source, at, size):
        ref, index = blocks[source]
        return ref[index, at : at + size, :]

    row = lax.broadcasted_iota(jnp.int32, (table_rows, LANES), 0)
    grouped = row < 8 * tiles
    owner = jnp.where(
        grouped, row // 16 * spare + row % 16 - (16 - spare), row - 8 * tiles + spare * (tiles // 2)
    )
    owner = jnp.where(grouped & (row % 16 < 16 - spare), -1, owner)
    pick = jnp.zeros((1, LANES), F32)
    for source in range(sources):
        filled = rows_of(source, tail_at, table_rows).astype(F32)
        filled = jnp.sum(jnp.where(owner == me, filled, 0.0), axis=0, keepdims=True)
        pick = pick + jnp.where(filled > 0.5, filled + float(source * prompts - 1), 0.0)
    pick = pick.astype(jnp.int32)

    span = sources * prompts * STATE
    wanted = one_hot(lax.broadcasted_iota(jnp.int32, (span, LANES), 0) // STATE == pick)
    states, windows, tails = [], [], []
    for source in range(sources):
        for p in range(prompts):
            at = p * tiles * STATE
            states.append(
                jnp.concatenate(
                    [rows_of(source, at + tile * STATE, STATE) for tile in range(tiles)], axis=1
                )
            )
            at = window_at + p * WINDOW
            windows.append(
                jnp.concatenate(
                    [
                        rows_of(source, at, WINDOW // 2),
                        rows_of(source, at + WINDOW // 2, WINDOW // 2),
                    ],
                    axis=1,
                )
            )
        tails.append(
            jnp.concatenate(
                [rows_of(source, tail_at + 8 * tile, 16) for tile in range(0, tiles, 2)], axis=1
            )
        )
    states = jnp.concatenate(states, axis=0)
    windows = jnp.concatenate(windows, axis=0)
    row = lax.broadcasted_iota(jnp.int32, (slots * STATE, LANES), 0)
    lane = lax.broadcasted_iota(jnp.int32, (slots * STATE, LANES), 1)
    take = dot_nt(one_hot(row // STATE == lane), wanted)
    row = lax.broadcasted_iota(jnp.int32, (slots * STATE, span), 0)
    lane = lax.broadcasted_iota(jnp.int32, (slots * STATE, span), 1)
    take = jnp.where(row % STATE == lane % STATE, take, 0.0).astype(BF16)
    moved = jnp.dot(take, states, preferred_element_type=F32)
    state_ref[...] = moved.astype(BF16).reshape(slots, STATE, channels)
    moved = jnp.dot(take, windows, preferred_element_type=F32)
    moved = moved.astype(BF16).reshape(slots, WINDOW // 2, 2 * LANES)
    for upper in range(2):
        for kind in range(2):
            at = upper * LANES + kind * HEAD_DIM
            keyval_ref[:, kind, upper * WINDOW // 2 : (upper + 1) * WINDOW // 2, :] = moved[
                :, :, at : at + HEAD_DIM
            ]

    wide = -(-slots // 16) * 16
    row = lax.broadcasted_iota(jnp.int32, (wide, LANES), 0)
    lane = lax.broadcasted_iota(jnp.int32, (wide, LANES), 1)
    unit = one_hot(row == lane)
    span = sources * 16
    row = lax.broadcasted_iota(jnp.int32, (span, LANES), 0)
    base = (pick // prompts) * 16 + (pick % prompts) * depth
    hits = [
        one_hot(row == base + prompts * depth * odd + tap) for odd in (0, 1) for tap in range(depth)
    ]
    hits = dot_nt(unit, jnp.concatenate(hits, axis=0)).astype(BF16)
    hits = jnp.concatenate([hits[:, i * span : (i + 1) * span] for i in range(2 * depth)], axis=0)
    moved = jnp.dot(hits, jnp.concatenate(tails, axis=0), preferred_element_type=F32)
    for odd in range(2):
        for tap in range(depth):
            at = (odd * depth + tap) * wide
            for pair in range(tiles // 2):
                tile = 2 * pair + odd
                conv_ref[tap, :, tile * LANES : (tile + 1) * LANES] = moved[
                    at : at + slots, pair * LANES : (pair + 1) * LANES
                ].astype(BF16)


def on_device(
    pr_size,
    tp_size,
    tokens,
    prompt_lengths,
    query_weight,
    key_weight,
    value_weight,
    attention_gain,
    inner_weight,
    conv_weight,
    scan_weight,
    step_weight,
    step_bias,
    mamba_rate,
    mamba_skip,
    mamba_gain,
    request_prompt,
    request_owner,
    request_slot,
):
    rows, width = tokens.shape
    prompts = prompt_lengths.shape[1]
    channels = inner_weight.shape[2]
    features = query_weight.shape[1]
    slots = request_owner.shape[0]
    tiles = channels // LANES

    def shape(dims, dtype=F32):
        return jax.ShapeDtypeStruct(dims, dtype)

    inner = jnp.einsum("td,dgc->gtc", tokens, inner_weight, preferred_element_type=F32)
    inner = inner.astype(BF16)
    partial, mixed = pl.pallas_call(
        functools.partial(mix_kernel, prompts),
        out_shape=(
            shape((DT_RANK + 2 * STATE, rows)),
            shape((rows, channels), BF16),
        ),
        in_specs=[VMEM] * 4,
        out_specs=(VMEM, VMEM),
        scratch_shapes=[pltpu.VMEM((rows + 8, channels), F32)],
        compiler_params=params(16),
        name="mix",
    )(prompt_lengths, inner, conv_weight, scan_weight.T)

    def swap(x, axis, size, bit):
        return lax.ppermute(x, axis, [(i, i ^ bit) for i in range(size)])

    near = swap(partial, "tp", tp_size, 1)
    spare = (16 - 2 * prompts * (CONV - 1)) * (tiles // 2)
    early_rows = prompts * WINDOW + 8 * tiles + -(-max(pr_size - spare, 0) // 16) * 16
    attended, square, early = pl.pallas_call(
        functools.partial(attend_kernel, prompts),
        out_shape=(
            shape((rows, features)),
            shape((8, rows)),
            shape((early_rows, LANES), BF16),
        ),
        in_specs=[VMEM] * 9,
        out_specs=(VMEM, VMEM, VMEM),
        scratch_shapes=[
            pltpu.VMEM((8, LANES), jnp.int32),
        ],
        compiler_params=params(16),
        cost_estimate=pl.CostEstimate(
            flops=2 * rows * width * (features + channels), bytes_accessed=4 << 20, transcendentals=0
        ),
        name="attend",
    )(
        prompt_lengths,
        tokens,
        query_weight,
        key_weight.T,
        value_weight.T,
        inner,
        request_prompt[None],
        request_owner[None],
        request_slot[None],
    )
    pair = partial + near
    bit = 2
    while bit < tp_size // 2:
        pair = pair + swap(pair, "tp", tp_size, bit)
        bit *= 2
    far = swap(pair, "tp", tp_size, bit)

    payload, leaving = scan_call(
        prompts,
        prompt_lengths,
        pair,
        far,
        mixed,
        step_weight,
        step_bias[None],
        mamba_rate,
        early,
    )
    gated, sums = pl.pallas_call(
        gate_kernel,
        out_shape=(shape((rows, channels)), shape((2, rows))),
        in_specs=[VMEM] * 5,
        out_specs=(VMEM, VMEM),
        compiler_params=params(16),
        cost_estimate=pl.CostEstimate(flops=1 << 24, bytes_accessed=4 << 20, transcendentals=0),
        name="gate",
    )(leaving, mixed, inner, mamba_skip[None], square)

    held = payload[None]
    pr_bits = [1 << i for i in reversed(range((pr_size - 1).bit_length()))]
    tp_bits = [1 << i for i in range((tp_size - 1).bit_length())]
    main, last = pr_bits[:-1], pr_bits[-1]
    near, far = list(tp_bits[:-1]), tp_bits[-1]
    for bit in main[:-1]:
        new = swap(held, "pr", pr_size, bit)
        other = swap(sums, "tp", tp_size, near.pop(0)) if near else jnp.zeros_like(sums)
        held, sums = pl.pallas_call(
            join_kernel,
            out_shape=(
                shape((2 * held.shape[0],) + held.shape[1:], BF16),
                shape(sums.shape),
            ),
            in_specs=[VMEM] * 4,
            out_specs=(VMEM, VMEM),
            compiler_params=params(16),
            name="join",
        )(held, new, sums, other)
    for bit in near:
        sums = sums + swap(sums, "tp", tp_size, bit)
    crossed = swap(held, "pr", pr_size, last)
    fresh = swap(held, "pr", pr_size, main[-1])
    other = swap(sums, "tp", tp_size, far)
    fresh, sums = pl.pallas_call(
        hold_kernel,
        out_shape=(shape(fresh.shape, BF16), shape(sums.shape)),
        in_specs=[VMEM] * 3,
        out_specs=(VMEM, VMEM),
        compiler_params=params(16),
        name="hold",
    )(fresh, sums, other)
    pieces = [held, fresh, crossed, swap(fresh, "pr", pr_size, last)]
    attention_out, mamba_out = pl.pallas_call(
        norm_kernel,
        out_shape=(shape((rows, features), BF16), shape((rows, channels), BF16)),
        in_specs=[VMEM] * 5 + [HBM] * 2,
        out_specs=(VMEM, VMEM),
        compiler_params=params(16),
        cost_estimate=pl.CostEstimate(flops=1 << 24, bytes_accessed=2 << 20, transcendentals=0),
        name="norm",
    )(attended, gated, sums, attention_gain[None], mamba_gain[None], crossed, inner_weight)
    keyval, state, conv = pl.pallas_call(
        functools.partial(deliver_kernel, prompts, len(pieces)),
        out_shape=(
            shape((slots, 2, WINDOW, HEAD_DIM), BF16),
            shape((slots, STATE, channels), BF16),
            shape((CONV - 1, slots, channels), BF16),
        ),
        in_specs=[VMEM] * len(pieces),
        out_specs=(VMEM,) * 3,
        compiler_params=params(32),
        name="deliver",
    )(*pieces)
    return (attention_out, mamba_out, keyval, state, conv.transpose(1, 0, 2))


def solution(mesh):
    return jax.shard_map(
        functools.partial(on_device, mesh.shape["pr"], mesh.shape["tp"]),
        mesh=mesh,
        in_specs=(
            P("pr", None),
            P("pr", None),
            P(None, "tp"),
            P(None, "tp"),
            P(None, "tp"),
            P("tp"),
            P(None, None, "tp"),
            P(None, "tp"),
            P("tp", None),
            P(None, "tp"),
            P("tp"),
            P(None, "tp"),
            P("tp"),
            P("tp"),
            P("pr"),
            P("pr"),
            P("pr"),
        ),
        out_specs=(
            P("pr", "tp"),
            P("pr", "tp"),
            P("pr", None, None, "tp"),
            P("pr", None, "tp"),
            P("pr", None, "tp"),
        ),
        check_vma=False,
    )
```

```python
import functools
import math

import jax
import jax.numpy as jnp
from jax import lax
from jax.experimental import pallas as pl
from jax.experimental.pallas import tpu as pltpu
from jax.sharding import PartitionSpec as P

HEADS = 16
KV_HEADS = 4
HEAD_DIM = 64
INNER = 2048
STATE = 16
DT_RANK = 64
CONV = 4
WINDOW = 32
EPSILON = 1e-06
LANES = 128
BLOCK = 16
LONGEST = 160
RESET = 1e30

F32 = jnp.float32
BF16 = jnp.bfloat16
VMEM = pl.BlockSpec(memory_space=pltpu.VMEM)
HBM = pl.BlockSpec(memory_space=pltpu.HBM)


def params(mib):
    return pltpu.CompilerParams(vmem_limit_bytes=mib << 20)


def dot_nt(a, b):
    return lax.dot_general(a, b, (((1,), (1,)), ((), ())), preferred_element_type=F32)


def bounds(len_ref, prompts):
    starts, ends = [], []
    at = 0
    for p in range(prompts):
        starts.append(at)
        at = at + len_ref[0:1, p : p + 1]
        ends.append(at)
    return starts, ends


def first_row_of(position, starts, prompts):
    first = jnp.zeros_like(position)
    for p in range(1, prompts):
        first = jnp.where(position >= starts[p], starts[p], first)
    return first


def last_rows(shape, depth, starts, ends):
    row = lax.broadcasted_iota(jnp.int32, shape, 0)
    position = lax.broadcasted_iota(jnp.int32, shape, 1)
    hit = jnp.zeros(shape, F32)
    for p in range(len(starts)):
        here = (row >= p * depth) & (row < (p + 1) * depth) & (position >= starts[p])
        hit = jnp.where(here & (position - row == ends[p] - (p + 1) * depth), 1.0, hit)
    return hit.astype(BF16)


def row_sums(squares):
    total = squares[:, :LANES]
    for at in range(LANES, squares.shape[1], LANES):
        total = total + squares[:, at : at + LANES]
    return jnp.sum(total.T, axis=0, keepdims=True)


def sigmoid(x):
    return 0.5 * jnp.tanh(0.5 * x) + 0.5


def mix_kernel(
    prompts,
    len_ref,
    inner_ref,
    conv_ref,
    scan_ref,
    partial_ref,
    mixed_ref,
    raw_ref,
):
    _, rows, channels = inner_ref.shape
    starts, _ = bounds(len_ref, prompts)
    raw = inner_ref[0].astype(F32)
    raw_ref[pl.ds(0, 8), :] = jnp.zeros((8, channels), F32)
    raw_ref[pl.ds(8, rows), :] = raw
    position = lax.broadcasted_iota(jnp.int32, (rows, 1), 0)
    offset = position - first_row_of(position, starts, prompts)
    total = raw * conv_ref[CONV - 1 : CONV, :]
    for lag in range(1, CONV):
        shifted = raw_ref[pl.ds(8 - lag, rows), :]
        shifted = jnp.where(offset >= lag, shifted, 0.0)
        total = total + shifted * conv_ref[CONV - 1 - lag : CONV - lag, :]
    mixed = (total * sigmoid(total)).astype(BF16)
    mixed_ref[...] = mixed
    partial_ref[...] = dot_nt(scan_ref[...], mixed)


def attend_kernel(
    prompts,
    len_ref,
    tokens_ref,
    query_ref,
    key_ref,
    value_ref,
    inner_ref,
    prompt_ref,
    owner_ref,
    slot_ref,
    attended_ref,
    square_ref,
    packed_ref,
    request_ref,
):
    rows, width = tokens_ref.shape
    channels = inner_ref.shape[2]
    features = query_ref.shape[1]
    group = features // HEAD_DIM
    starts, ends = bounds(len_ref, prompts)
    tokens = tokens_ref[...]
    queries = jnp.dot(tokens, query_ref[...], preferred_element_type=F32).astype(BF16)
    keys = dot_nt(tokens, jnp.concatenate([key_ref[...]] * group, axis=0)).astype(BF16)
    values = dot_nt(tokens, jnp.concatenate([value_ref[...]] * group, axis=0)).astype(BF16)
    at_row = lax.broadcasted_iota(jnp.int32, (rows, rows), 0)
    at_column = lax.broadcasted_iota(jnp.int32, (rows, rows), 1)
    row_first = first_row_of(at_row, starts, prompts)
    allowed = (at_column <= at_row) & (at_row - at_column < WINDOW) & (at_column >= row_first)
    head_of = lax.broadcasted_iota(jnp.int32, (rows, features), 1) // HEAD_DIM
    zero = jnp.zeros((), BF16)
    attended = jnp.zeros((rows, features), F32)
    for head in range(group):
        mine = head_of == head
        scores = dot_nt(queries, jnp.where(mine, keys, zero)) * HEAD_DIM ** (-0.5)
        scores = jnp.where(allowed, scores, -1e30)
        top = jnp.max(scores, axis=1, keepdims=True)
        expons = jnp.exp(scores - top)
        weights = expons * (1.0 / jnp.sum(expons, axis=1, keepdims=True))
        attended = attended + jnp.dot(
            weights.astype(BF16), jnp.where(mine, values, zero), preferred_element_type=F32
        )
    attended_ref[...] = attended
    square_ref[...] = jnp.broadcast_to(row_sums(attended * attended), square_ref.shape)
    lane = lax.broadcasted_iota(jnp.int32, (rows, LANES), 1)
    both = jnp.where(lane < HEAD_DIM, keys[:, :LANES], values[:, :LANES])
    pick = last_rows((prompts * WINDOW, rows), WINDOW, starts, ends)
    packed_ref[: prompts * WINDOW, :] = jnp.dot(pick, both, preferred_element_type=F32).astype(
        BF16
    )
    requests = owner_ref.shape[1]
    request_ref[...] = jnp.full(request_ref.shape, -1, jnp.int32)
    request_ref[0:1, 0:requests] = owner_ref[...]
    request_ref[1:2, 0:requests] = slot_ref[...]
    request_ref[2:3, 0:requests] = prompt_ref[...]
    depth = prompts * (CONV - 1)
    groups = channels // LANES // 2
    spare = 16 - 2 * depth
    owners = packed_ref.shape[0] - prompts * WINDOW - 16 * groups + spare * groups
    owner = lax.broadcasted_iota(jnp.int32, (owners, LANES), 0) == request_ref[0:1, :]
    slot = lax.broadcasted_iota(jnp.int32, (LANES, LANES), 0) == request_ref[1:2, :]
    number = request_ref[2:3, :] + 1
    filled = dot_nt(
        jnp.where(owner, 1.0, 0.0).astype(BF16),
        jnp.where(slot, number, 0).astype(F32).astype(BF16),
    )
    pick = last_rows((8, rows), CONV - 1, starts, ends)
    tail = jnp.dot(pick, inner_ref[0], preferred_element_type=F32)
    base = prompts * WINDOW
    for group in range(groups):
        at = 2 * group * LANES
        packed_ref[base + 16 * group : base + 16 * (group + 1), :] = jnp.concatenate(
            [
                tail[:depth, at : at + LANES],
                tail[:depth, at + LANES : at + 2 * LANES],
                filled[spare * group : spare * (group + 1), :],
            ],
            axis=0,
        ).astype(BF16)
    if owners > spare * groups:
        packed_ref[base + 16 * groups :, :] = filled[spare * groups :, :].astype(BF16)


def scan_kernel(
    prompts,
    len_ref,
    own_ref,
    other_ref,
    mixed_ref,
    step_weight_ref,
    step_bias_ref,
    rate_ref,
    early_ref,
    payload_ref,
    leaving_ref,
    states_even_ref,
    states_odd_ref,
    decay_ref,
    input_ref,
    in_map_ref,
    out_map_ref,
    scalars_ref,
    sem,
):
    scalars_copy = pltpu.make_async_copy(len_ref, scalars_ref, sem)
    scalars_copy.start()
    rows, channels = mixed_ref.shape
    pairs = rows // BLOCK // 2
    starts, _ = bounds(len_ref, prompts)
    projected = own_ref[...] + other_ref[...]
    low = projected[:DT_RANK, :].T.astype(BF16)
    pre = jnp.dot(low, step_weight_ref[...], preferred_element_type=F32) + step_bias_ref[...]
    step = jnp.maximum(pre, 0.0) + jnp.log1p(jnp.exp(-jnp.abs(pre)))
    position = lax.broadcasted_iota(jnp.int32, (rows, 1), 0)
    is_first = position == 0
    for p in range(1, prompts):
        is_first = is_first | (position == starts[p])
    decay_ref[...] = jnp.where(is_first, RESET, step)
    input_ref[...] = step * mixed_ref[...].astype(F32)
    for block in range(rows // BLOCK):
        columns = slice(block * BLOCK, (block + 1) * BLOCK)
        in_map_ref[block, :, 0:BLOCK] = projected[DT_RANK : DT_RANK + STATE, columns]
        out_map_ref[block, :, 0:BLOCK] = projected[DT_RANK + STATE :, columns]
    rate = rate_ref[...] * (-math.log2(math.e))

    def advance(block, state, states_ref, index, keep):
        at = pl.multiple_of(block * BLOCK, BLOCK)
        for token in range(BLOCK):
            decay = jnp.exp2(decay_ref[pl.ds(at + token, 1), :] * rate)
            entering = in_map_ref[block, :, token : token + 1] * input_ref[pl.ds(at + token, 1), :]
            state = state * decay + entering
            if keep:
                states_ref[index, token * STATE : (token + 1) * STATE, :] = state.astype(BF16)
            leaving = out_map_ref[block, :, token : token + 1] * state
            leaving = leaving[:8, :] + leaving[8:, :]
            row = pl.multiple_of(block * BLOCK * 8, BLOCK * 8) + 8 * token
            for tile in range(channels // LANES):
                leaving_ref[tile, pl.ds(row, 8), :] = leaving[:, tile * LANES : (tile + 1) * LANES]
        return state

    def two_blocks(keep, pair, state):
        state = advance(2 * pair, state, states_even_ref, pair, keep)
        return advance(2 * pair + 1, state, states_odd_ref, pair, keep)

    first, last = 0, pairs
    if prompts == 2:
        first = max(rows - LONGEST - 1, 0) // (2 * BLOCK)
        last = min((LONGEST - 1) // (2 * BLOCK) + 1, pairs)
    state = jnp.zeros((STATE, channels), F32)
    for keep, start, stop in ((False, 0, first), (True, first, last), (False, last, pairs)):
        if start < stop:
            state = lax.fori_loop(start, stop, functools.partial(two_blocks, keep), state)
    scalars_copy.wait()
    last = -1
    for p in range(prompts):
        last = last + scalars_ref[0, p]
        block = last // BLOCK
        at = pl.multiple_of((last - block * BLOCK) * STATE, STATE)
        if p == prompts - 1:
            final = state.astype(BF16)
        else:
            final = jnp.where(
                block % 2 == 0,
                states_even_ref[block // 2, pl.ds(at, STATE), :],
                states_odd_ref[block // 2, pl.ds(at, STATE), :],
            )
        for tile in range(channels // LANES):
            at = (p * (channels // LANES) + tile) * STATE
            payload_ref[at : at + STATE, :] = final[:, tile * LANES : (tile + 1) * LANES]
    base = prompts * channels // LANES * STATE
    payload_ref[base:, :] = early_ref[...]


def scan_call(prompts, lengths, own, other, mixed, *rest):
    rows, channels = mixed.shape
    tiles = channels // LANES
    payload_rows = prompts * tiles * STATE + rest[-1].shape[0]
    return pl.pallas_call(
        functools.partial(scan_kernel, prompts),
        out_shape=(
            jax.ShapeDtypeStruct((payload_rows, LANES), BF16),
            jax.ShapeDtypeStruct((tiles, rows * 8, LANES), F32),
        ),
        in_specs=[VMEM] * 8,
        out_specs=(VMEM, VMEM),
        scratch_shapes=[
            pltpu.VMEM((rows // BLOCK // 2, BLOCK * STATE, channels), BF16),
            pltpu.VMEM((rows // BLOCK // 2, BLOCK * STATE, channels), BF16),
            pltpu.VMEM((rows, channels), F32),
            pltpu.VMEM((rows, channels), F32),
            pltpu.VMEM((rows // BLOCK, STATE, LANES), F32),
            pltpu.VMEM((rows // BLOCK, STATE, LANES), F32),
            pltpu.SMEM((1, prompts), jnp.int32),
            pltpu.SemaphoreType.DMA,
        ],
        compiler_params=params(16),
        name="scan",
    )(lengths, own, other, mixed, *rest)


def gate_kernel(
    leaving_ref,
    mixed_ref,
    inner_ref,
    skip_ref,
    square_ref,
    gated_ref,
    sums_ref,
):
    rows, channels = mixed_ref.shape
    scanned = []
    for tile in range(channels // LANES):
        total = leaving_ref[tile, pl.ds(0, rows, stride=8), :]
        for index in range(1, 8):
            total = total + leaving_ref[tile, pl.ds(index, rows, stride=8), :]
        scanned.append(total)
    scanned = jnp.concatenate(scanned, axis=1)
    gate = inner_ref[1].astype(F32)
    gated = (scanned + skip_ref[...] * mixed_ref[...].astype(F32)) * (
        gate * sigmoid(gate)
    )
    gated_ref[...] = gated
    sums_ref[0:1, :] = square_ref[0:1, :]
    sums_ref[1:2, :] = row_sums(gated * gated)


def join_kernel(held_ref, new_ref, own_ref, other_ref, joined_ref, sums_ref):
    count = held_ref.shape[0]
    joined_ref[:count] = held_ref[...]
    joined_ref[count:] = new_ref[...]
    sums_ref[...] = own_ref[...] + other_ref[...]


def hold_kernel(new_ref, own_ref, other_ref, fresh_ref, sums_ref):
    fresh_ref[...] = new_ref[...]
    sums_ref[...] = own_ref[...] + other_ref[...]


def norm_kernel(
    attended_ref,
    gated_ref,
    sums_ref,
    attention_gain_ref,
    mamba_gain_ref,
    crossed_hbm,
    inner_hbm,
    attention_ref,
    mamba_ref,
):
    sums = sums_ref[...]
    sums = jnp.concatenate([sums, jnp.zeros((6, sums.shape[1]), F32)], axis=0).T
    attention_scale = lax.rsqrt(sums[:, 0:1] / (HEADS * HEAD_DIM) + EPSILON)
    attention_ref[...] = (attended_ref[...] * attention_scale * attention_gain_ref[...]).astype(
        BF16
    )
    mamba_scale = lax.rsqrt(sums[:, 1:2] / INNER + EPSILON)
    mamba_ref[...] = (gated_ref[...] * mamba_scale * mamba_gain_ref[...]).astype(BF16)


def one_hot(hit):
    return jnp.where(hit, 1.0, 0.0).astype(BF16)


def deliver_kernel(
    prompts,
    pieces,
    *refs,
):
    keyval_ref, state_ref, conv_ref = refs[pieces:]
    me = lax.axis_index("pr")
    slots, _, channels = state_ref.shape
    tiles = channels // LANES
    blocks = [(ref, index) for ref in refs[:pieces] for index in range(ref.shape[0])]
    sources = len(blocks)
    window_at = prompts * tiles * STATE
    tail_at = window_at + prompts * WINDOW
    depth = CONV - 1
    spare = 16 - 2 * prompts * depth
    table_rows = refs[0].shape[1] - tail_at

    def rows_of(source, at, size):
        ref, index = blocks[source]
        return ref[index, at : at + size, :]

    row = lax.broadcasted_iota(jnp.int32, (table_rows, LANES), 0)
    grouped = row < 8 * tiles
    owner = jnp.where(
        grouped, row // 16 * spare + row % 16 - (16 - spare), row - 8 * tiles + spare * (tiles // 2)
    )
    owner = jnp.where(grouped & (row % 16 < 16 - spare), -1, owner)
    pick = jnp.zeros((1, LANES), F32)
    for source in range(sources):
        filled = rows_of(source, tail_at, table_rows).astype(F32)
        filled = jnp.sum(jnp.where(owner == me, filled, 0.0), axis=0, keepdims=True)
        pick = pick + jnp.where(filled > 0.5, filled + float(source * prompts - 1), 0.0)
    pick = pick.astype(jnp.int32)

    span = sources * prompts * STATE
    wanted = one_hot(lax.broadcasted_iota(jnp.int32, (span, LANES), 0) // STATE == pick)
    states, windows, tails = [], [], []
    for source in range(sources):
        for p in range(prompts):
            at = p * tiles * STATE
            states.append(
                jnp.concatenate(
                    [rows_of(source, at + tile * STATE, STATE) for tile in range(tiles)], axis=1
                )
            )
            at = window_at + p * WINDOW
            windows.append(
                jnp.concatenate(
                    [
                        rows_of(source, at, WINDOW // 2),
                        rows_of(source, at + WINDOW // 2, WINDOW // 2),
                    ],
                    axis=1,
                )
            )
        tails.append(
            jnp.concatenate(
                [rows_of(source, tail_at + 8 * tile, 16) for tile in range(0, tiles, 2)], axis=1
            )
        )
    states = jnp.concatenate(states, axis=0)
    windows = jnp.concatenate(windows, axis=0)
    row = lax.broadcasted_iota(jnp.int32, (slots * STATE, LANES), 0)
    lane = lax.broadcasted_iota(jnp.int32, (slots * STATE, LANES), 1)
    take = dot_nt(one_hot(row // STATE == lane), wanted)
    row = lax.broadcasted_iota(jnp.int32, (slots * STATE, span), 0)
    lane = lax.broadcasted_iota(jnp.int32, (slots * STATE, span), 1)
    take = jnp.where(row % STATE == lane % STATE, take, 0.0).astype(BF16)
    moved = jnp.dot(take, states, preferred_element_type=F32)
    state_ref[...] = moved.astype(BF16).reshape(slots, STATE, channels)
    moved = jnp.dot(take, windows, preferred_element_type=F32)
    moved = moved.astype(BF16).reshape(slots, WINDOW // 2, 2 * LANES)
    for upper in range(2):
        for kind in range(2):
            at = upper * LANES + kind * HEAD_DIM
            keyval_ref[:, kind, upper * WINDOW // 2 : (upper + 1) * WINDOW // 2, :] = moved[
                :, :, at : at + HEAD_DIM
            ]

    wide = -(-slots // 16) * 16
    row = lax.broadcasted_iota(jnp.int32, (wide, LANES), 0)
    lane = lax.broadcasted_iota(jnp.int32, (wide, LANES), 1)
    unit = one_hot(row == lane)
    span = sources * 16
    row = lax.broadcasted_iota(jnp.int32, (span, LANES), 0)
    base = (pick // prompts) * 16 + (pick % prompts) * depth
    hits = [
        one_hot(row == base + prompts * depth * odd + tap) for odd in (0, 1) for tap in range(depth)
    ]
    hits = dot_nt(unit, jnp.concatenate(hits, axis=0)).astype(BF16)
    hits = jnp.concatenate([hits[:, i * span : (i + 1) * span] for i in range(2 * depth)], axis=0)
    moved = jnp.dot(hits, jnp.concatenate(tails, axis=0), preferred_element_type=F32)
    for odd in range(2):
        for tap in range(depth):
            at = (odd * depth + tap) * wide
            for pair in range(tiles // 2):
                tile = 2 * pair + odd
                conv_ref[tap, :, tile * LANES : (tile + 1) * LANES] = moved[
                    at : at + slots, pair * LANES : (pair + 1) * LANES
                ].astype(BF16)


def on_device(
    pr_size,
    tp_size,
    tokens,
    prompt_lengths,
    query_weight,
    key_weight,
    value_weight,
    attention_gain,
    inner_weight,
    conv_weight,
    scan_weight,
    step_weight,
    step_bias,
    mamba_rate,
    mamba_skip,
    mamba_gain,
    request_prompt,
    request_owner,
    request_slot,
):
    rows, width = tokens.shape
    prompts = prompt_lengths.shape[1]
    channels = inner_weight.shape[2]
    features = query_weight.shape[1]
    slots = request_owner.shape[0]
    tiles = channels // LANES

    def shape(dims, dtype=F32):
        return jax.ShapeDtypeStruct(dims, dtype)

    inner = jnp.einsum("td,dgc->gtc", tokens, inner_weight, preferred_element_type=F32)
    inner = inner.astype(BF16)
    partial, mixed = pl.pallas_call(
        functools.partial(mix_kernel, prompts),
        out_shape=(
            shape((DT_RANK + 2 * STATE, rows)),
            shape((rows, channels), BF16),
        ),
        in_specs=[VMEM] * 4,
        out_specs=(VMEM, VMEM),
        scratch_shapes=[pltpu.VMEM((rows + 8, channels), F32)],
        compiler_params=params(16),
        name="mix",
    )(prompt_lengths, inner, conv_weight, scan_weight.T)

    def swap(x, axis, size, bit):
        return lax.ppermute(x, axis, [(i, i ^ bit) for i in range(size)])

    near = swap(partial, "tp", tp_size, 1)
    spare = (16 - 2 * prompts * (CONV - 1)) * (tiles // 2)
    early_rows = prompts * WINDOW + 8 * tiles + -(-max(pr_size - spare, 0) // 16) * 16
    attended, square, early = pl.pallas_call(
        functools.partial(attend_kernel, prompts),
        out_shape=(
            shape((rows, features)),
            shape((8, rows)),
            shape((early_rows, LANES), BF16),
        ),
        in_specs=[VMEM] * 9,
        out_specs=(VMEM, VMEM, VMEM),
        scratch_shapes=[
            pltpu.VMEM((8, LANES), jnp.int32),
        ],
        compiler_params=params(16),
        cost_estimate=pl.CostEstimate(
            flops=2 * rows * width * (features + channels), bytes_accessed=4 << 20, transcendentals=0
        ),
        name="attend",
    )(
        prompt_lengths,
        tokens,
        query_weight,
        key_weight.T,
        value_weight.T,
        inner,
        request_prompt[None],
        request_owner[None],
        request_slot[None],
    )
    pair = partial + near
    bit = 2
    while bit < tp_size // 2:
        pair = pair + swap(pair, "tp", tp_size, bit)
        bit *= 2
    far = swap(pair, "tp", tp_size, bit)

    payload, leaving = scan_call(
        prompts,
        prompt_lengths,
        pair,
        far,
        mixed,
        step_weight,
        step_bias[None],
        mamba_rate,
        early,
    )
    gated, sums = pl.pallas_call(
        gate_kernel,
        out_shape=(shape((rows, channels)), shape((2, rows))),
        in_specs=[VMEM] * 5,
        out_specs=(VMEM, VMEM),
        compiler_params=params(16),
        cost_estimate=pl.CostEstimate(flops=1 << 24, bytes_accessed=4 << 20, transcendentals=0),
        name="gate",
    )(leaving, mixed, inner, mamba_skip[None], square)

    held = payload[None]
    pr_bits = [1 << i for i in reversed(range((pr_size - 1).bit_length()))]
    tp_bits = [1 << i for i in range((tp_size - 1).bit_length())]
    main, last = pr_bits[:-1], pr_bits[-1]
    near, far = list(tp_bits[:-1]), tp_bits[-1]
    for bit in main[:-1]:
        new = swap(held, "pr", pr_size, bit)
        other = swap(sums, "tp", tp_size, near.pop(0)) if near else jnp.zeros_like(sums)
        held, sums = pl.pallas_call(
            join_kernel,
            out_shape=(
                shape((2 * held.shape[0],) + held.shape[1:], BF16),
                shape(sums.shape),
            ),
            in_specs=[VMEM] * 4,
            out_specs=(VMEM, VMEM),
            compiler_params=params(16),
            name="join",
        )(held, new, sums, other)
    for bit in near:
        sums = sums + swap(sums, "tp", tp_size, bit)
    crossed = swap(held, "pr", pr_size, last)
    fresh = swap(held, "pr", pr_size, main[-1])
    other = swap(sums, "tp", tp_size, far)
    fresh, sums = pl.pallas_call(
        hold_kernel,
        out_shape=(shape(fresh.shape, BF16), shape(sums.shape)),
        in_specs=[VMEM] * 3,
        out_specs=(VMEM, VMEM),
        compiler_params=params(16),
        name="hold",
    )(fresh, sums, other)
    pieces = [held, fresh, crossed, swap(fresh, "pr", pr_size, last)]
    attention_out, mamba_out = pl.pallas_call(
        norm_kernel,
        out_shape=(shape((rows, features), BF16), shape((rows, channels), BF16)),
        in_specs=[VMEM] * 5 + [HBM] * 2,
        out_specs=(VMEM, VMEM),
        compiler_params=params(16),
        cost_estimate=pl.CostEstimate(flops=1 << 24, bytes_accessed=2 << 20, transcendentals=0),
        name="norm",
    )(attended, gated, sums, attention_gain[None], mamba_gain[None], crossed, inner_weight)
    keyval, state, conv = pl.pallas_call(
        functools.partial(deliver_kernel, prompts, len(pieces)),
        out_shape=(
            shape((slots, 2, WINDOW, HEAD_DIM), BF16),
            shape((slots, STATE, channels), BF16),
            shape((CONV - 1, slots, channels), BF16),
        ),
        in_specs=[VMEM] * len(pieces),
        out_specs=(VMEM,) * 3,
        compiler_params=params(32),
        name="deliver",
    )(*pieces)
    return (attention_out, mamba_out, keyval, state, conv.transpose(1, 0, 2))


def solution(mesh):
    return jax.shard_map(
        functools.partial(on_device, mesh.shape["pr"], mesh.shape["tp"]),
        mesh=mesh,
        in_specs=(
            P("pr", None),
            P("pr", None),
            P(None, "tp"),
            P(None, "tp"),
            P(None, "tp"),
            P("tp"),
            P(None, None, "tp"),
            P(None, "tp"),
            P("tp", None),
            P(None, "tp"),
            P("tp"),
            P(None, "tp"),
            P("tp"),
            P("tp"),
            P("pr"),
            P("pr"),
            P("pr"),
        ),
        out_specs=(
            P("pr", "tp"),
            P("pr", "tp"),
            P("pr", None, None, "tp"),
            P("pr", None, "tp"),
            P("pr", None, "tp"),
        ),
        check_vma=False,
    )
```
